32 devices in a mesh: dp: 4 (over x, core), ctx: 8 (over z, y).
Axes of the slice: x: 2, y: 2, z: 4, core: 2. Of those that a mesh axis runs over, the one named last changes fastest.
Arguments:
- residual: bfloat16 [512, 4, 1024], P('ctx', 'dp'), may hold values from -10 to 10
- projections: bfloat16 [512, 4, 3072], P('ctx', 'dp'), may hold values from -8 to 8
- out_weight: bfloat16 [1024, 1024], replicated, may hold values from -0.1875 to 0.1875
- gain_one: float32 [1024], replicated, may hold values from 0.1 to 1.9
- up_weight: bfloat16 [1024, 2048], replicated, may hold values from -0.1875 to 0.1875
- conv_kernel: float32 [31, 1024], replicated, may hold values from -1 to 1
- gain_two: float32 [1024], replicated, may hold values from 0.1 to 1.9
- down_weight: bfloat16 [1024, 1024], replicated, may hold values from -0.1875 to 0.1875
- lengths: int32 [4], P('dp'), may hold values from 128 to 512, as said below
- out_grad: bfloat16 [512, 4, 1024], P('ctx', 'dp'), may hold values from -0.13183594 to 0.13183594
Outputs:
- block_out: bfloat16 [512, 4, 1024], P('ctx', 'dp')
- up_grad: float32 [2048, 1024], P(('dp', 'ctx'))
- down_grad: float32 [1024, 1024], P(('dp', 'ctx'))
- kernel_grad: float32 [1024, 31], P(('dp', 'ctx'))
- gain_one_grad: float32 [1024], P(('dp', 'ctx'))
- gain_two_grad: float32 [1024], P(('dp', 'ctx'))
The draws below stay inside these ranges and needn't reach their ends.
Inputs may be any that keep to these rules, and one draw needn't show every extreme that they name: `lengths`: utterance 0 has all 512 frames valid.
All inputs are finite; a program needn't handle non-finite values.
Results may differ from the reference program's by a relative error of at most 0.02.
Values may be sent and summed in bfloat16 or wider, within the bound.
No kernel may reach another device: no remote copies, remote signals or barrier semaphores. Data moves between devices by JAX's collectives and lax.ppermute only.
A program may use at most 128 MiB of HBM per device.

```python
import math
import jax
import jax.numpy as jnp
from jax import lax

D = 1024
HEADS = 16
HD = 64
KERNEL = 31
HALF = 15
NUTT = 4
LEN = 512


def draw_projections(key, part):
    shape = (LEN, NUTT, HEADS, 3, HD)
    base_key = jax.random.fold_in(key, 11)
    spread = jnp.array([1.6, 1.6, 1.0], jnp.float32)[None, None, None, :, None]
    values = jax.random.truncated_normal(base_key, -4.0, 4.0, shape, jnp.float32) * spread
    return values.reshape(LEN, NUTT, 3 * D).astype(jnp.bfloat16)


def draw_residual(key, part):
    shape = (LEN, NUTT, D)
    row_scale = jnp.exp(jax.random.uniform(jax.random.fold_in(key, 32), (LEN, NUTT, 1), jnp.float32, math.log(0.1), 0.0))
    col_scale = jnp.exp(jax.random.uniform(jax.random.fold_in(key, 33), (1, 1, D), jnp.float32, math.log(0.3), math.log(3.0)))
    values = jax.random.truncated_normal(jax.random.fold_in(key, 31), -3.0, 3.0, shape, jnp.float32) * row_scale * col_scale
    return values.astype(jnp.bfloat16)


def draw_lengths(key, part):
    counts = jax.random.randint(jax.random.fold_in(key, 21), (NUTT,), LEN // 4, LEN + 1, dtype=jnp.int32)
    return counts.at[0].set(LEN)


def spiked(values, own_key, source, target, parts, factor):
    owner, partner = [(jnp.arange(values.shape[axis_at]) // (values.shape[axis_at] // parts)).reshape([-1 if axis == axis_at else 1 for axis in range(values.ndim)]) for axis_at in (source, target)]
    chosen = jax.random.permutation(own_key, parts)[partner]
    strong = (owner == chosen) | (owner == (partner + parts // 2) % parts)
    return jnp.where(strong, factor * values, values)


def block_levels(rng, dims, split, smallest, largest):
    level, own = 1.0, jax.random.fold_in(rng, 6)
    for dim, parts in split:
        heights = jnp.exp(jax.random.uniform(jax.random.fold_in(own, dim), (parts,), jnp.float32, smallest / len(split), largest / len(split)))
        level = level * jnp.repeat(heights, dims[dim] // parts).reshape([-1 if axis == dim else 1 for axis in range(len(dims))])
    return level


def bell_draw(own_key, dims, deviation, reach, shards=(), held_as=jnp.bfloat16):
    values = jax.random.normal(own_key, dims, jnp.float32) * deviation
    if len(shards) > 0:
        values = block_levels(own_key, dims, shards, -0.22, 0.18) * values
    return jnp.clip(values, min=-reach, max=reach).astype(held_as)


def gaussian_with(key, shape, scale, reach, pieces, heavy, kind=jnp.bfloat16):
    values = scale * jax.random.normal(key, shape, jnp.float32)
    if pieces:
        values = values * block_levels(key, shape, pieces, -0.22, 0.18)
    return jnp.clip(spiked(values, jax.random.fold_in(key, 3), *heavy), -reach, reach).astype(kind)


def setup_inputs(seed: int = 0) -> dict:
    streams_of = jax.random.split(jax.random.key(seed), 11)
    return {
        "residual": draw_residual(jax.random.fold_in(streams_of[10], 71), 0),
        "projections": draw_projections(jax.random.fold_in(streams_of[10], 71), 0),
        "out_weight": bell_draw(streams_of[2], (D, D), D ** -0.5, 0.1875),
        "gain_one": jnp.clip(1.0 + 0.18 * jax.random.normal(streams_of[3], (D,), jnp.float32), 0.1, 1.9),
        "up_weight": bell_draw(streams_of[4], (D, 2 * D), D ** -0.5, 0.1875),
        "conv_kernel": bell_draw(streams_of[5], (KERNEL, D), KERNEL ** -0.5, 1.0, (), jnp.float32),
        "gain_two": jnp.clip(1.0 + 0.18 * jax.random.normal(streams_of[6], (D,), jnp.float32), 0.1, 1.9),
        "down_weight": bell_draw(streams_of[7], (D, D), D ** -0.5, 0.1875),
        "lengths": draw_lengths(jax.random.fold_in(streams_of[10], 71), 0),
        "out_grad": gaussian_with(streams_of[9], (LEN, NUTT, D), (1.0 / (LEN * NUTT) ** 0.5), 0.13183594, ((0, 8), (1, 4)), (0, 2, 8, 2.0)),
    }


EPSILON = 1e-05

def normalize(values):
    center = values - lax.optimization_barrier(jnp.mean(values, axis=-1, keepdims=True))
    inverse = lax.rsqrt(lax.optimization_barrier(jnp.mean(center * center, axis=-1, keepdims=True)) + EPSILON)
    return (center * inverse, inverse)

def attend_item(item):
    packed, key_marks = item
    query_rows = packed[:, :HD]
    key_rows = packed[:, HD:2 * HD]
    value_rows = packed[:, 2 * HD:]
    scores = jnp.dot(query_rows, key_rows.T, preferred_element_type=jnp.float32) * HD ** (-0.5)
    scores = jnp.where(key_marks[None, :] > 0, scores, -jnp.inf)
    highest = lax.optimization_barrier(jnp.max(scores, axis=-1, keepdims=True))
    raised = jnp.exp(scores - highest)
    weights_bf = (raised / lax.optimization_barrier(jnp.sum(raised, axis=-1, keepdims=True))).astype(jnp.bfloat16)
    return jnp.dot(weights_bf, value_rows, preferred_element_type=jnp.float32).astype(jnp.bfloat16)

def reference(residual, projections, out_weight, gain_one, up_weight, conv_kernel, gain_two, down_weight, lengths, out_grad):
    row_total = LEN * NUTT
    positions = jnp.arange(LEN, dtype=jnp.int32)
    valid = (positions[:, None] < lengths[None, :]).astype(jnp.bfloat16)
    items = projections.reshape(LEN, NUTT * HEADS, 3 * HD).transpose(1, 0, 2)
    item_marks = jnp.broadcast_to(valid.T[:, None, :], (NUTT, HEADS, LEN)).reshape(NUTT * HEADS, LEN)
    attended = lax.map(attend_item, (items, item_marks))
    context = attended.transpose(1, 0, 2).reshape(row_total, D)
    hidden = residual.reshape(row_total, D).astype(jnp.float32) + jnp.dot(context, out_weight, preferred_element_type=jnp.float32)
    normed_one, inverse_one = normalize(hidden)
    scaled_one = (normed_one * gain_one).astype(jnp.bfloat16)
    lifted = jnp.dot(scaled_one, up_weight, preferred_element_type=jnp.float32)
    linear_part = lifted[:, :D]
    gate_part = jax.nn.sigmoid(lifted[:, D:])
    row_mask = valid.reshape(row_total, 1).astype(jnp.float32)
    glu_out = (linear_part * gate_part * row_mask).astype(jnp.bfloat16)
    glu_wide = jnp.pad(glu_out.reshape(LEN, NUTT, D).astype(jnp.float32), ((HALF, HALF), (0, 0), (0, 0)))
    conv_out = jnp.zeros((LEN, NUTT, D), jnp.float32)
    for offset in range(KERNEL):
        conv_out = conv_out + conv_kernel[offset] * glu_wide[offset:offset + LEN]
    normed_two, inverse_two = normalize(conv_out.reshape(row_total, D))
    pre_act = normed_two * gain_two
    gate_two = jax.nn.sigmoid(pre_act)
    activated = (pre_act * gate_two).astype(jnp.bfloat16)
    block_out = (hidden + jnp.dot(activated, down_weight, preferred_element_type=jnp.float32)).astype(jnp.bfloat16)
    block_out = block_out.reshape(LEN, NUTT, D)
    cotangent = (out_grad * valid[:, :, None]).reshape(row_total, D)
    down_grad = jnp.dot(cotangent.T, activated, preferred_element_type=jnp.float32)
    act_grad = jnp.dot(cotangent, down_weight.T, preferred_element_type=jnp.float32)
    pre_grad = act_grad * gate_two * (1.0 + pre_act * (1.0 - gate_two))
    gain_two_grad = lax.optimization_barrier(jnp.sum(pre_grad * normed_two, axis=0))
    scaled_grad = pre_grad * gain_two
    conv_grad = inverse_two * (scaled_grad - lax.optimization_barrier(jnp.mean(scaled_grad, axis=-1, keepdims=True)) - normed_two * lax.optimization_barrier(jnp.mean(scaled_grad * normed_two, axis=-1, keepdims=True)))
    conv_grad = conv_grad.astype(jnp.bfloat16)
    conv_full = conv_grad.reshape(LEN, NUTT, D).astype(jnp.float32)
    conv_wide = jnp.pad(conv_full, ((HALF, HALF), (0, 0), (0, 0)))
    kernel_cols = []
    glu_grad = jnp.zeros((LEN, NUTT, D), jnp.float32)
    for offset in range(KERNEL):
        kernel_cols.append(lax.optimization_barrier(jnp.sum(conv_full * glu_wide[offset:offset + LEN], axis=(0, 1))))
        start = 2 * HALF - offset
        glu_grad = glu_grad + conv_kernel[offset] * conv_wide[start:start + LEN]
    kernel_grad = jnp.stack(kernel_cols, axis=1)
    glu_grad = glu_grad.reshape(row_total, D) * row_mask
    linear_grad = glu_grad * gate_part
    gate_grad = glu_grad * linear_part * gate_part * (1.0 - gate_part)
    lifted_grad = jnp.concatenate([linear_grad, gate_grad], axis=1).astype(jnp.bfloat16)
    up_grad = jnp.dot(lifted_grad.T, scaled_one, preferred_element_type=jnp.float32)
    input_grad = jnp.dot(lifted_grad, up_weight.T, preferred_element_type=jnp.float32)
    gain_one_grad = lax.optimization_barrier(jnp.sum(input_grad * normed_one, axis=0))
    return (block_out, up_grad, down_grad, kernel_grad, gain_one_grad, gain_two_grad)
```

```python
import jax
import jax.numpy as jnp
from jax import lax
from jax.sharding import Mesh, PartitionSpec as P

HEADS = 16


EPSILON = 1e-05

MARGIN = 32

CTX = ("chi", "clo")
FIRST = ("dlo", "chi")
SECOND = ("dhi", "clo")


def normalize(values):
    center = values - jnp.mean(values, axis=-1, keepdims=True)
    inverse = lax.rsqrt(jnp.mean(center * center, axis=-1, keepdims=True) + EPSILON)
    return (center * inverse, inverse)


def attend(packed, key_lengths):
    length, count, triple = packed.shape
    head_size = triple // 3
    query_rows = packed[:, :, :head_size]
    key_rows = packed[:, :, head_size : 2 * head_size]
    value_rows = packed[:, :, 2 * head_size :]
    allowed = jnp.arange(length, dtype=jnp.int32)[None, :] < key_lengths[:, None]
    scores = (
        jnp.einsum("qmd,kmd->mqk", query_rows, key_rows, preferred_element_type=jnp.float32)
        * head_size ** (-0.5)
    )
    scores = jnp.where(allowed[:, None, :], scores, -jnp.inf)
    highest = jnp.max(scores, axis=-1, keepdims=True)
    raised = jnp.exp(scores - highest)
    weights_bf = (raised / jnp.sum(raised, axis=-1, keepdims=True)).astype(jnp.bfloat16)
    return jnp.einsum(
        "mqk,kmd->qmd", weights_bf, value_rows, preferred_element_type=jnp.float32
    ).astype(jnp.bfloat16)


def by_owner(cols, sizes):
    dhi, dlo, chi, clo = sizes
    rows, width = cols.shape
    part = width // (dhi * dlo * chi * clo)
    split = cols.reshape(rows, dhi, dlo, chi, clo, part)
    return jnp.transpose(split, (2, 3, 0, 1, 4, 5)).reshape(dlo * chi, rows, dhi * clo * part)


def gathered(rows, chi):
    copies = jnp.broadcast_to(rows[None], (chi,) + rows.shape)
    line = lax.all_to_all(copies, "chi", split_axis=0, concat_axis=0, tiled=True)
    line = line.reshape(chi * rows.shape[0], rows.shape[1])
    other = lax.ppermute(line, "dlo", [(0, 1), (1, 0)])
    first = lax.axis_index("dlo") == 0
    return jnp.concatenate([jnp.where(first, line, other), jnp.where(first, other, line)], axis=0)


def on_device(
    residual,
    projections,
    out_weight,
    gain_one,
    up_weight,
    conv_kernel,
    gain_two,
    down_weight,
    lengths,
    out_grad,
):
    frames, utter_count, width = residual.shape
    head_size = width // HEADS
    kernel_len = conv_kernel.shape[0]
    half = (kernel_len - 1) // 2
    dhi, dlo, chi, clo = sizes = tuple(lax.axis_size(a) for a in ("dhi", "dlo", "chi", "clo"))
    ctx = chi * clo
    length = frames * ctx
    items = utter_count * HEADS // ctx
    me = lax.axis_index(CTX)
    bf = jnp.bfloat16
    f32 = jnp.float32

    packed = projections.reshape(frames, ctx, items, 3 * head_size)
    packed = lax.all_to_all(packed, CTX, split_axis=1, concat_axis=0, tiled=True)
    packed = packed.reshape(length, items, 3 * head_size)

    both = jnp.concatenate([residual, out_grad], axis=-1)
    up = [(i, i + 1) for i in range(ctx - 1)]
    down = [(j, i) for i, j in up]
    before = lax.ppermute(both[frames - MARGIN :], CTX, up)
    after = lax.ppermute(both[:MARGIN], CTX, down)
    both = jnp.concatenate([before, both, after], axis=0)
    wide = frames + 2 * MARGIN
    place = me * frames - MARGIN + jnp.arange(wide, dtype=jnp.int32)
    valid = (place[:, None] >= 0) & (place[:, None] < lengths[None, :])
    row_mask = valid.astype(f32)[:, :, None]
    cot = jnp.where(valid[:, :, None], both[:, :, width:], 0)
    edge = MARGIN // 2
    near = wide - 2 * edge
    cot_near = cot[edge : edge + near]
    cot_own = cot[MARGIN : MARGIN + frames].reshape(frames * utter_count, width)
    act_grad = lax.dot_general(
        cot_near, down_weight, (((2,), (1,)), ((), ())), preferred_element_type=f32
    )

    key_lengths = lengths[(me * items + jnp.arange(items, dtype=jnp.int32)) // HEADS]
    context = attend(packed, key_lengths).reshape(length, items * head_size)
    padded = jnp.pad(context, ((MARGIN, MARGIN), (0, 0)))
    windows = jnp.stack([padded[i * frames : i * frames + wide] for i in range(ctx)])
    context = lax.all_to_all(windows, CTX, split_axis=0, concat_axis=0, tiled=True)
    context = jnp.transpose(context, (1, 0, 2)).reshape(wide, utter_count, width)

    cot_cols = lax.all_to_all(
        by_owner(cot_own, sizes), FIRST, split_axis=0, concat_axis=0, tiled=True
    )

    hidden = both[:, :, :width].astype(f32) + jnp.einsum(
        "fuc,cd->fud", context, out_weight, preferred_element_type=f32
    )
    normed_one, _ = normalize(hidden)
    scaled_one = (normed_one * gain_one).astype(bf)
    own = slice(MARGIN, MARGIN + frames)
    own_near = slice(MARGIN - edge, MARGIN - edge + frames)
    rows = frames * utter_count
    scaled_own = scaled_one[own].reshape(rows, width)
    scaled_all = gathered(scaled_own, chi)

    lifted = jnp.einsum("fuc,cd->fud", scaled_one, up_weight, preferred_element_type=f32)
    linear_part = lifted[:, :, :width]
    gate_part = jax.nn.sigmoid(lifted[:, :, width:])
    glu = (linear_part * gate_part * row_mask).astype(bf).astype(f32)
    conv_out = jnp.zeros((near, utter_count, width), f32)
    for j in range(kernel_len):
        start = edge + j - half
        conv_out = conv_out + conv_kernel[j] * glu[start : start + near]
    normed_two, inverse_two = normalize(conv_out)
    pre_act = normed_two * gain_two
    gate_two = jax.nn.sigmoid(pre_act)
    activated = (pre_act * gate_two)[own_near].astype(bf).reshape(rows, width)
    activated_all = gathered(activated, chi)
    block_out = (
        hidden[own].reshape(rows, width)
        + jnp.dot(activated, down_weight, preferred_element_type=f32)
    ).astype(bf)
    block_out = block_out.reshape(frames, utter_count, width)

    pre_grad = act_grad * gate_two * (1.0 + pre_act * (1.0 - gate_two))
    gain_two_grad = jnp.sum((pre_grad * normed_two)[own_near], axis=(0, 1))
    scaled_grad = pre_grad * gain_two
    conv_grad = inverse_two * (
        scaled_grad
        - jnp.mean(scaled_grad, axis=-1, keepdims=True)
        - normed_two * jnp.mean(scaled_grad * normed_two, axis=-1, keepdims=True)
    )
    conv_grad = conv_grad.astype(bf).astype(f32)
    conv_own = conv_grad[own_near]
    small = []
    glu_grad = jnp.zeros((frames, utter_count, width), f32)
    for j in range(kernel_len):
        start = MARGIN + j - half
        small.append(jnp.sum(conv_own * glu[start : start + frames], axis=(0, 1)))
        start = MARGIN - edge + half - j
        glu_grad = glu_grad + conv_kernel[j] * conv_grad[start : start + frames]
    glu_grad = glu_grad * row_mask[own]
    gate_own = gate_part[own]
    linear_grad = glu_grad * gate_own
    gate_grad = glu_grad * linear_part[own] * gate_own * (1.0 - gate_own)
    lifted_grad = jnp.concatenate([linear_grad, gate_grad], axis=-1).astype(bf)
    lifted_grad = lifted_grad.reshape(rows, 2 * width)
    input_grad = lax.dot_general(
        lifted_grad, up_weight, (((1,), (1,)), ((), ())), preferred_element_type=f32
    )
    gain_one_grad = jnp.sum(input_grad * normed_one[own].reshape(rows, width), axis=0)

    small = small + [gain_one_grad, gain_two_grad]
    count = kernel_len + 2
    small = by_owner(jnp.stack(small).astype(bf), sizes)
    small = small.reshape(dlo * chi, -1)
    cols = by_owner(lifted_grad, sizes)
    col_count = cols.shape[2]
    spare = -small.shape[1] % col_count
    small = jnp.pad(small, ((0, 0), (0, spare))).reshape(dlo * chi, -1, col_count)
    message = jnp.concatenate([cols, small], axis=1)
    message = lax.all_to_all(message, FIRST, split_axis=0, concat_axis=0, tiled=True)
    cols = message[:, :rows].reshape(-1, col_count)
    small = jnp.sum(message[:, rows:].astype(f32), axis=0).reshape(-1)
    seconds = dhi * clo
    small_width = width // (ctx * dhi * dlo)
    small = small[: count * seconds * small_width].reshape(count, seconds, small_width)
    small = jnp.transpose(small, (1, 0, 2)).reshape(seconds, count * small_width)

    up_part = lax.dot_general(
        cols, scaled_all, (((0,), (0,)), ((), ())), preferred_element_type=f32
    ).reshape(seconds, -1, width)
    down_part = lax.dot_general(
        cot_cols.reshape(cols.shape[0], -1),
        activated_all,
        (((0,), (0,)), ((), ())),
        preferred_element_type=f32,
    ).reshape(seconds, -1, width)
    spare = -small.shape[1] % width
    small = jnp.pad(small, ((0, 0), (0, spare))).reshape(seconds, -1, width)
    up_rows, down_rows = up_part.shape[1], down_part.shape[1]
    parts = jnp.concatenate([up_part.astype(bf), down_part.astype(bf), small.astype(bf)], axis=1)
    parts = lax.all_to_all(parts, SECOND, split_axis=0, concat_axis=0, tiled=True)
    total = jnp.sum(parts.astype(f32), axis=0)
    up_grad = total[:up_rows]
    down_grad = total[up_rows : up_rows + down_rows]
    small = total[up_rows + down_rows :].reshape(-1)[: count * small_width]
    small = small.reshape(count, small_width)
    kernel_grad = jnp.transpose(small[:kernel_len])
    return (block_out, up_grad, down_grad, kernel_grad, small[kernel_len], small[kernel_len + 1])


def solution(mesh):
    dp, ctx = mesh.shape["dp"], mesh.shape["ctx"]
    fine = Mesh(mesh.devices.reshape(dp // 2, 2, ctx // 2, 2), ("dhi", "dlo", "chi", "clo"))
    dp_axes, ctx_axes = ("dhi", "dlo"), ("chi", "clo")
    every = ("dhi", "dlo", "chi", "clo")
    in_specs = (
        P(ctx_axes, dp_axes, None),
        P(ctx_axes, dp_axes, None),
        P(),
        P(),
        P(),
        P(),
        P(),
        P(),
        P(dp_axes),
        P(ctx_axes, dp_axes, None),
    )
    out_specs = (
        P(ctx_axes, dp_axes, None),
        P(every, None),
        P(every, None),
        P(every, None),
        P(every),
        P(every),
    )
    return jax.shard_map(
        on_device, mesh=fine, in_specs=in_specs, out_specs=out_specs, check_vma=False
    )
```

```python
import functools

import jax
import jax.numpy as jnp
from jax import lax
from jax.experimental import pallas as pl
from jax.experimental.pallas import tpu as pltpu
from jax.sharding import Mesh, PartitionSpec as P

HEADS = 16


EPSILON = 1e-05

MARGIN = 32

CTX = ("chi", "clo")
FIRST = ("dlo", "chi")
SECOND = ("dhi", "clo")

SMEM = pl.BlockSpec(memory_space=pltpu.SMEM)
VMEM = pl.BlockSpec(memory_space=pltpu.VMEM)


def normalize(values):
    center = values - jnp.mean(values, axis=-1, keepdims=True)
    inverse = lax.rsqrt(jnp.mean(center * center, axis=-1, keepdims=True) + EPSILON)
    return (center * inverse, inverse)


def attend(packed, key_lengths):
    length, count, triple = packed.shape
    head_size = triple // 3
    query_rows = packed[:, :, :head_size]
    key_rows = packed[:, :, head_size : 2 * head_size]
    value_rows = packed[:, :, 2 * head_size :]
    allowed = jnp.arange(length, dtype=jnp.int32)[None, :] < key_lengths[:, None]
    scores = (
        jnp.einsum("qmd,kmd->mqk", query_rows, key_rows, preferred_element_type=jnp.float32)
        * head_size ** (-0.5)
    )
    scores = jnp.where(allowed[:, None, :], scores, -jnp.inf)
    highest = jnp.max(scores, axis=-1, keepdims=True)
    raised = jnp.exp(scores - highest)
    weights_bf = (raised / jnp.sum(raised, axis=-1, keepdims=True)).astype(jnp.bfloat16)
    return jnp.einsum(
        "mqk,kmd->qmd", weights_bf, value_rows, preferred_element_type=jnp.float32
    ).astype(jnp.bfloat16)


def by_owner(cols, sizes):
    dhi, dlo, chi, clo = sizes
    rows, width = cols.shape
    part = width // (dhi * dlo * chi * clo)
    split = cols.reshape(rows, dhi, dlo, chi, clo, part)
    return jnp.transpose(split, (2, 3, 0, 1, 4, 5)).reshape(dlo * chi, rows, dhi * clo * part)


def gathered(rows, chi):
    copies = jnp.broadcast_to(rows[None], (chi,) + rows.shape)
    line = lax.all_to_all(copies, "chi", split_axis=0, concat_axis=0, tiled=True)
    line = line.reshape(chi * rows.shape[0], rows.shape[1])
    other = lax.ppermute(line, "dlo", [(0, 1), (1, 0)])
    first = lax.axis_index("dlo") == 0
    return jnp.concatenate([jnp.where(first, line, other), jnp.where(first, other, line)], axis=0)


def params():
    return pltpu.CompilerParams(vmem_limit_bytes=40 * 1024 * 1024)


def struct(shape, dtype):
    return jax.ShapeDtypeStruct(shape, dtype)


def split_kernel(proj_ref, out_ref, sems):
    count, _, span = out_ref.shape
    copies = [
        pltpu.make_async_copy(proj_ref.at[:, pl.ds(i * span, span)], out_ref.at[i], sems.at[i])
        for i in range(count)
    ]
    for copy in copies:
        copy.start()
    for copy in copies:
        copy.wait()


def split_heads(proj, count):
    rows, cols = proj.shape
    return pl.pallas_call(
        split_kernel,
        out_shape=struct((count, rows, cols // count), proj.dtype),
        in_specs=[pl.BlockSpec(memory_space=pl.ANY)],
        out_specs=pl.BlockSpec(memory_space=pl.ANY),
        scratch_shapes=[pltpu.SemaphoreType.DMA((count,))],
        compiler_params=params(),
        name="split_heads",
    )(proj)


def edge_kernel(res_ref, grad_ref, low_ref, high_ref, sems):
    rows, width = res_ref.shape
    copies = []
    for i, (source, lanes) in enumerate(((res_ref, 0), (grad_ref, width))):
        copies.append(
            pltpu.make_async_copy(
                source.at[pl.ds(0, MARGIN)], low_ref.at[:, pl.ds(lanes, width)], sems.at[2 * i]
            )
        )
        copies.append(
            pltpu.make_async_copy(
                source.at[pl.ds(rows - MARGIN, MARGIN)],
                high_ref.at[:, pl.ds(lanes, width)],
                sems.at[2 * i + 1],
            )
        )
    for copy in copies:
        copy.start()
    for copy in copies:
        copy.wait()


def edges(res, grad):
    shape = struct((MARGIN, 2 * res.shape[1]), res.dtype)
    spec = pl.BlockSpec(memory_space=pl.ANY)
    return pl.pallas_call(
        edge_kernel,
        out_shape=(shape, shape),
        in_specs=[spec, spec],
        out_specs=(spec, spec),
        scratch_shapes=[pltpu.SemaphoreType.DMA((4,))],
        compiler_params=params(),
        name="edges",
    )(res, grad)


def attend_kernel(head_size, frames, scalar_ref, qkv_ref, out_ref):
    length = qkv_ref.shape[0]
    count = qkv_ref.shape[1] // (3 * head_size)
    ctx, wide, _ = out_ref.shape
    allowed = lax.broadcasted_iota(jnp.int32, (length, length), 1) < scalar_ref[0]
    outs = []
    for m in range(count):
        base = 3 * head_size * m
        query = qkv_ref[:, base : base + head_size]
        key = qkv_ref[:, base + head_size : base + 2 * head_size]
        value = qkv_ref[:, base + 2 * head_size : base + 3 * head_size]
        scores = (
            lax.dot_general(
                query, key, (((1,), (1,)), ((), ())), preferred_element_type=jnp.float32
            )
            * head_size ** (-0.5)
        )
        scores = jnp.where(allowed, scores, -jnp.inf)
        raised = jnp.exp(scores - jnp.max(scores, axis=-1, keepdims=True))
        weights = raised * (1.0 / jnp.sum(raised, axis=-1, keepdims=True))
        outs.append(
            jnp.dot(weights.astype(jnp.bfloat16), value, preferred_element_type=jnp.float32)
        )
    context = jnp.concatenate(outs, axis=1).astype(jnp.bfloat16)
    for i in range(ctx):
        low = max(i * frames - MARGIN, 0)
        high = min(i * frames - MARGIN + wide, length)
        at = low - (i * frames - MARGIN)
        out_ref[i, at : at + high - low, :] = context[low:high]
        if at > 0:
            out_ref[i, :at, :] = jnp.zeros((at, context.shape[1]), context.dtype)
        if at + high - low < wide:
            rest = wide - (at + high - low)
            out_ref[i, wide - rest :, :] = jnp.zeros((rest, context.shape[1]), context.dtype)


def attend_windows(scalars, qkv, head_size, frames, ctx):
    wide = frames + 2 * MARGIN
    return pl.pallas_call(
        functools.partial(attend_kernel, head_size, frames),
        out_shape=struct((ctx, wide, qkv.shape[1] // 3), jnp.bfloat16),
        in_specs=[SMEM, VMEM],
        out_specs=VMEM,
        compiler_params=params(),
        name="attend",
    )(scalars, qkv)


def cot_kernel(scalar_ref, grad_ref, low_ref, high_ref, weight_ref, act_ref, cols_ref):
    frames, width = grad_ref.shape
    edge = MARGIN // 2
    whole = jnp.concatenate(
        [low_ref[edge:, width:], grad_ref[...], high_ref[: MARGIN - edge, width:]], axis=0
    )
    near = whole.shape[0]
    place = scalar_ref[1] - edge + lax.broadcasted_iota(jnp.int32, (near, width), 0)
    valid = (place >= 0) & (place < scalar_ref[0])
    whole = jnp.where(valid, whole.astype(jnp.float32), 0.0).astype(jnp.bfloat16)
    act_ref[...] = lax.dot_general(
        whole, weight_ref[...], (((1,), (1,)), ((), ())), preferred_element_type=jnp.float32
    )
    own = whole[edge : edge + frames]
    count, _, span = cols_ref.shape
    half = width // 2
    piece = span // 2
    for i in range(count):
        cols_ref[i, :, :] = jnp.concatenate(
            [own[:, i * piece : (i + 1) * piece], own[:, half + i * piece : half + (i + 1) * piece]],
            axis=1,
        )


def cot_part(scalars, grad, low, high, weight, count):
    frames, width = grad.shape
    return pl.pallas_call(
        cot_kernel,
        out_shape=(
            struct((frames + MARGIN, width), jnp.float32),
            struct((count, frames, width // count), jnp.bfloat16),
        ),
        in_specs=[SMEM, VMEM, VMEM, VMEM, VMEM],
        out_specs=(VMEM, VMEM),
        compiler_params=params(),
        name="cotangent",
    )(scalars, grad, low, high, weight)


def hidden_kernel(
    context_ref, res_ref, low_ref, high_ref, weight_ref, gain_ref,
    hidden_ref, normed_ref, scaled_ref, own_ref,
):
    frames, width = res_ref.shape
    ctx, wide, _ = context_ref.shape
    context = jnp.concatenate([context_ref[i] for i in range(ctx)], axis=1)
    product = jnp.dot(context, weight_ref[...], preferred_element_type=jnp.float32)
    step = 32
    for at in range(0, wide, step):
        if at < MARGIN:
            res = low_ref[at : at + step, :width]
        elif at < MARGIN + frames:
            res = res_ref[at - MARGIN : at - MARGIN + step, :]
        else:
            res = high_ref[at - MARGIN - frames : at - MARGIN - frames + step, :width]
        hidden = res.astype(jnp.float32) + product[at : at + step]
        normed, _ = normalize(hidden)
        scaled = (normed * gain_ref[...]).astype(jnp.bfloat16)
        scaled_ref[at : at + step, :] = scaled
        if MARGIN <= at < MARGIN + frames:
            rows = slice(at - MARGIN, at - MARGIN + step)
            hidden_ref[rows, :] = hidden
            normed_ref[rows, :] = normed
            own_ref[rows, :] = scaled


def hidden_part(context, res, low, high, weight, gain):
    frames, width = res.shape
    wide = frames + 2 * MARGIN
    return pl.pallas_call(
        hidden_kernel,
        out_shape=(
            struct((frames, width), jnp.float32),
            struct((frames, width), jnp.float32),
            struct((wide, width), jnp.bfloat16),
            struct((frames, width), jnp.bfloat16),
        ),
        in_specs=[VMEM] * 6,
        out_specs=(VMEM,) * 4,
        compiler_params=params(),
        name="hidden",
    )(context, res, low, high, weight, gain)


def conv_kernel_body(
    scalar_ref, scaled_ref, weight_ref, taps_ref, gain_ref,
    act_ref, linear_ref, gate_ref, glu_ref, normed_ref, inverse_ref, conv_ref,
):
    frames, width = act_ref.shape
    wide = scaled_ref.shape[0]
    taps = taps_ref.shape[0]
    half = (taps - 1) // 2
    edge = MARGIN // 2
    near = wide - 2 * edge
    linear = jnp.dot(scaled_ref[...], weight_ref[:, :width], preferred_element_type=jnp.float32)
    lifted = jnp.dot(scaled_ref[...], weight_ref[:, width:], preferred_element_type=jnp.float32)
    step = 32
    for at in range(0, wide, step):
        place = scalar_ref[1] - MARGIN + at + lax.broadcasted_iota(jnp.int32, (step, width), 0)
        valid = (place >= 0) & (place < scalar_ref[0])
        gate = jax.nn.sigmoid(lifted[at : at + step])
        value = linear[at : at + step]
        glu = jnp.where(valid, value * gate, 0.0)
        glu_ref[at : at + step, :] = glu.astype(jnp.bfloat16).astype(jnp.float32)
        if MARGIN <= at < MARGIN + frames:
            rows = slice(at - MARGIN, at - MARGIN + step)
            linear_ref[rows, :] = value
            gate_ref[rows, :] = gate

    def lanes(i, carry):
        cols = pl.ds(pl.multiple_of(i * 128, 128), 128)
        block = glu_ref[:, cols]
        total = jnp.zeros((near, 128), jnp.float32)
        for shift in range(8):
            moved = block if shift == 0 else pltpu.roll(block, wide - shift, 0)
            for j in range(taps):
                start = edge + j - half
                if start % 8 == shift:
                    total = total + taps_ref[j : j + 1, cols] * moved[start - shift : start - shift + near]
        conv_ref[:, cols] = total
        return carry

    lax.fori_loop(0, width // 128, lanes, 0)
    step = 16
    for at in range(0, near, step):
        normed, inverse = normalize(conv_ref[at : at + step, :])
        normed_ref[at : at + step, :] = normed
        inverse_ref[at : at + step, :] = jnp.broadcast_to(inverse, (step, 128))
        if MARGIN - edge <= at < MARGIN - edge + frames:
            pre = normed * gain_ref[...]
            rows = slice(at - (MARGIN - edge), at - (MARGIN - edge) + step)
            act_ref[rows, :] = (pre * jax.nn.sigmoid(pre)).astype(jnp.bfloat16)


def conv_part(scalars, scaled, weight, taps, gain):
    wide, width = scaled.shape
    frames = wide - 2 * MARGIN
    near = wide - MARGIN
    f32 = jnp.float32
    return pl.pallas_call(
        conv_kernel_body,
        out_shape=(
            struct((frames, width), jnp.bfloat16),
            struct((frames, width), f32),
            struct((frames, width), f32),
            struct((wide, width), f32),
            struct((near, width), f32),
            struct((near, 128), f32),
        ),
        in_specs=[SMEM] + [VMEM] * 4,
        out_specs=(VMEM,) * 6,
        scratch_shapes=[pltpu.VMEM((near, width), f32)],
        compiler_params=params(),
        name="conv",
    )(scalars, scaled, weight, taps, gain)


def back_kernel(
    scalar_ref, act_grad_ref, cols_ref, hidden_ref, one_ref, activated_ref, linear_ref, gate_ref,
    glu_ref, normed_ref, inverse_ref, taps_ref, gain_ref, down_ref, up_ref,
    block_ref, message_ref, grad_ref, small_ref, lifted_ref,
):
    frames, width = hidden_ref.shape
    near = normed_ref.shape[0]
    wide = glu_ref.shape[0]
    taps = taps_ref.shape[0]
    half = (taps - 1) // 2
    edge = MARGIN // 2
    first = MARGIN - edge
    gain = gain_ref[...]
    step = 16
    two = jnp.zeros((1, width), jnp.float32)
    for at in range(0, near, step):
        normed = normed_ref[at : at + step, :]
        pre = normed * gain
        gate = jax.nn.sigmoid(pre)
        grad = act_grad_ref[at : at + step, :] * gate * (1.0 + pre * (1.0 - gate))
        if first <= at < first + frames:
            two = two + jnp.sum(grad * normed, axis=0, keepdims=True)
        scaled = grad * gain
        result = inverse_ref[at : at + step, 0:1] * (
            scaled
            - jnp.mean(scaled, axis=-1, keepdims=True)
            - normed * jnp.mean(scaled * normed, axis=-1, keepdims=True)
        )
        grad_ref[at : at + step, :] = result.astype(jnp.bfloat16).astype(jnp.float32)
    small_ref[32:, :] = jnp.zeros((16, width), jnp.float32)
    small_ref[taps + 1 : taps + 2, :] = two

    place = scalar_ref[1] + lax.broadcasted_iota(jnp.int32, (frames, 128), 0)
    valid = place < scalar_ref[0]

    def lanes(i, carry):
        cols = pl.ds(pl.multiple_of(i * 128, 128), 128)
        high = pl.ds(pl.multiple_of(i * 128 + width, 128), 128)
        block = grad_ref[:, cols]
        own = block[first : first + frames]
        total = jnp.zeros((frames, 128), jnp.float32)
        for shift in range(8):
            moved = block if shift == 0 else pltpu.roll(block, near - shift, 0)
            for j in range(taps):
                start = first + half - j
                if start % 8 == shift:
                    total = total + taps_ref[j : j + 1, cols] * moved[start - shift : start - shift + frames]
        block = glu_ref[:, cols]
        for shift in range(8):
            moved = block if shift == 0 else pltpu.roll(block, wide - shift, 0)
            for j in range(taps):
                start = MARGIN + j - half
                if start % 8 == shift:
                    small_ref[j : j + 1, cols] = jnp.sum(
                        own * moved[start - shift : start - shift + frames], axis=0, keepdims=True
                    )
        total = jnp.where(valid, total, 0.0)
        gate = gate_ref[:, cols]
        linear_grad = (total * gate).astype(jnp.bfloat16)
        gate_grad = (total * linear_ref[:, cols] * gate * (1.0 - gate)).astype(jnp.bfloat16)
        lifted_ref[:, cols] = linear_grad
        lifted_ref[:, high] = gate_grad
        message_ref[i, :frames, :128] = linear_grad
        message_ref[i, :frames, 128:256] = gate_grad
        message_ref[i, :frames, 256:384] = cols_ref[i]
        return carry

    lax.fori_loop(0, width // 128, lanes, 0)
    input_grad = lax.dot_general(
        lifted_ref[...], up_ref[...], (((1,), (1,)), ((), ())), preferred_element_type=jnp.float32
    )
    small_ref[taps : taps + 1, :] = jnp.sum(input_grad * one_ref[...], axis=0, keepdims=True)
    for i in range(width // 128):
        for part in range(3):
            rows = small_ref[part * 16 : (part + 1) * 16, :]
            message_ref[i, frames:, part * 128 : (part + 1) * 128] = jnp.concatenate(
                [rows[:, i * 64 : (i + 1) * 64], rows[:, (i + 8) * 64 : (i + 9) * 64]], axis=1
            ).astype(jnp.bfloat16)
    block_ref[...] = (
        hidden_ref[...]
        + jnp.dot(activated_ref[...], down_ref[...], preferred_element_type=jnp.float32)
    ).astype(jnp.bfloat16)


def back_part(*operands):
    frames, width = operands[3].shape
    near = frames + MARGIN
    f32, bf = jnp.float32, jnp.bfloat16
    return pl.pallas_call(
        back_kernel,
        out_shape=(
            struct((frames, width), bf),
            struct((width // 128, frames + 16, 384), bf),
        ),
        in_specs=[SMEM] + [VMEM] * 14,
        out_specs=(VMEM,) * 2,
        scratch_shapes=[
            pltpu.VMEM((near, width), f32),
            pltpu.VMEM((48, width), f32),
            pltpu.VMEM((frames, 2 * width), bf),
        ],
        compiler_params=params(),
        name="backward",
    )(*operands)


def product_kernel(count, scalar_ref, message_ref, *refs):
    pieces = refs[: 4 * count]
    parts_ref, cols_ref, one_ref, two_ref = refs[4 * count :]
    frames, width = pieces[0].shape
    core, line = scalar_ref[2], scalar_ref[3]
    small = jnp.zeros((16, 384), jnp.float32)
    for side in range(2):
        for k in range(count):
            at = (side * count + k) * frames
            source = (core ^ side) * count + (line ^ k)
            cols_ref[at : at + frames, :] = message_ref[source, :frames, :]
            small = small + message_ref[source, frames:, :].astype(jnp.float32)
            one_ref[at : at + frames, :] = pieces[side * count + k][...]
            two_ref[at : at + frames, :] = pieces[2 * count + side * count + k][...]
    turned = (((0,), (0,)), ((), ()))
    up = lax.dot_general(
        cols_ref[:, :256], one_ref[...], turned, preferred_element_type=jnp.float32
    ).astype(jnp.bfloat16)
    down = lax.dot_general(
        cols_ref[:, 256:], two_ref[...], turned, preferred_element_type=jnp.float32
    ).astype(jnp.bfloat16)
    small = small.astype(jnp.bfloat16)
    for s in range(4):
        parts_ref[s, :64, :] = up[s * 64 : (s + 1) * 64]
        parts_ref[s, 64:96, :] = down[s * 32 : (s + 1) * 32]
        parts_ref[s, 96:, :384] = small
        parts_ref[s, 96:, 384:] = jnp.zeros((16, width - 384), jnp.bfloat16)


def product_part(scalars, message, pieces):
    count = len(pieces) // 4
    frames, width = pieces[0].shape
    bf = jnp.bfloat16
    rows = 2 * count * frames
    return pl.pallas_call(
        functools.partial(product_kernel, count),
        out_shape=struct((4, 112, width), bf),
        in_specs=[SMEM] + [VMEM] * (1 + len(pieces)),
        out_specs=VMEM,
        scratch_shapes=[
            pltpu.VMEM((rows, 384), bf),
            pltpu.VMEM((rows, width), bf),
            pltpu.VMEM((rows, width), bf),
        ],
        compiler_params=params(),
        name="products",
    )(scalars, message, *pieces)


def sum_kernel(taps, scalar_ref, parts_ref, up_ref, down_ref, kernel_ref, one_ref, two_ref):
    total = parts_ref[0].astype(jnp.float32)
    for s in range(1, parts_ref.shape[0]):
        total = total + parts_ref[s].astype(jnp.float32)
    up_ref[...] = total[:64]
    down_ref[...] = total[64:96]
    small = jnp.concatenate([total[96:112, :128], total[96:112, 128:256]], axis=0)
    back = (128 - 32 * scalar_ref[4]) % 128
    small = pltpu.roll(small, back, 1)
    last = pltpu.roll(total[96:104, 256:384], back, 1)
    kernel_ref[...] = jnp.transpose(small)[:32, :taps]
    one_ref[...] = small[taps : taps + 1, :32]
    two_ref[...] = last[:1, :32]


def sum_part(scalars, parts, taps):
    width = parts.shape[2]
    f32 = jnp.float32
    return pl.pallas_call(
        functools.partial(sum_kernel, taps),
        out_shape=(
            struct((64, width), f32),
            struct((32, width), f32),
            struct((32, taps), f32),
            struct((1, 32), f32),
            struct((1, 32), f32),
        ),
        in_specs=[SMEM, VMEM],
        out_specs=(VMEM,) * 5,
        compiler_params=params(),
        name="sums",
    )(scalars, parts)


def line_pieces(rows, chi):
    pieces = [rows]
    for k in range(1, chi):
        pieces.append(lax.ppermute(rows, "chi", [(i, i ^ k) for i in range(chi)]))
    return pieces


def swapped(pieces):
    return [lax.ppermute(piece, "dlo", [(0, 1), (1, 0)]) for piece in pieces]


def small_device(
    residual, projections, out_weight, gain_one, up_weight, conv_kernel, gain_two, down_weight,
    lengths, out_grad,
):
    frames, _, width = residual.shape
    taps = conv_kernel.shape[0]
    chi, clo = lax.axis_size("chi"), lax.axis_size("clo")
    ctx = chi * clo
    head_size = width // HEADS
    me = lax.axis_index(CTX)
    second = lax.axis_index("dhi") * clo + lax.axis_index("clo")
    scalars = jnp.stack(
        [lengths[0], me * frames, lax.axis_index("dlo"), lax.axis_index("chi"), second]
    ).astype(jnp.int32)
    res = residual.reshape(frames, width)
    grad = out_grad.reshape(frames, width)
    gain_one = gain_one.reshape(1, width)
    gain_two = gain_two.reshape(1, width)

    qkv = split_heads(projections.reshape(frames, 3 * width), ctx)
    qkv = lax.all_to_all(qkv, CTX, split_axis=0, concat_axis=0, tiled=True)
    low, high = edges(res, grad)
    up = [(i, i + 1) for i in range(ctx - 1)]
    down = [(j, i) for i, j in up]
    before = lax.ppermute(high, CTX, up)
    after = lax.ppermute(low, CTX, down)
    windows = attend_windows(scalars, qkv.reshape(ctx * frames, -1), head_size, frames, ctx)
    windows = lax.all_to_all(windows, CTX, split_axis=0, concat_axis=0, tiled=True)
    act_grad, cot_cols = cot_part(scalars, grad, before, after, down_weight, 2 * chi)

    hidden, normed_one, scaled, scaled_own = hidden_part(
        windows, res, before, after, out_weight, gain_one
    )
    ones = line_pieces(scaled_own, chi)
    activated, linear, gate, glu, normed_two, inverse_two = conv_part(
        scalars, scaled, up_weight, conv_kernel, gain_two
    )
    twos = line_pieces(activated, chi)
    block_out, message = back_part(
        scalars, act_grad, cot_cols, hidden, normed_one, activated, linear, gate,
        glu, normed_two, inverse_two, conv_kernel, gain_two, down_weight, up_weight,
    )
    ones = ones + swapped(ones)
    twos = twos + swapped(twos)
    message = lax.all_to_all(message, FIRST, split_axis=0, concat_axis=0, tiled=True)
    parts = product_part(scalars, message, ones + twos)
    parts = lax.all_to_all(parts, SECOND, split_axis=0, concat_axis=0, tiled=True)
    up_grad, down_grad, kernel_grad, one, two = sum_part(scalars, parts, taps)
    return (
        block_out.reshape(frames, 1, width), up_grad, down_grad, kernel_grad,
        one.reshape(-1), two.reshape(-1),
    )


def fits(residual, conv_kernel, sizes):
    dhi, dlo, chi, clo = sizes
    frames, utter_count, width = residual.shape
    return (
        utter_count == 1
        and frames == 64
        and width == 1024
        and conv_kernel.shape[0] == 31
        and (dhi, dlo, chi, clo) == (2, 2, 4, 2)
    )


def on_device(
    residual,
    projections,
    out_weight,
    gain_one,
    up_weight,
    conv_kernel,
    gain_two,
    down_weight,
    lengths,
    out_grad,
):
    frames, utter_count, width = residual.shape
    head_size = width // HEADS
    kernel_len = conv_kernel.shape[0]
    half = (kernel_len - 1) // 2
    dhi, dlo, chi, clo = sizes = tuple(lax.axis_size(a) for a in ("dhi", "dlo", "chi", "clo"))
    if fits(residual, conv_kernel, sizes):
        return small_device(
            residual,
            projections,
            out_weight,
            gain_one,
            up_weight,
            conv_kernel,
            gain_two,
            down_weight,
            lengths,
            out_grad,
        )
    ctx = chi * clo
    length = frames * ctx
    items = utter_count * HEADS // ctx
    me = lax.axis_index(CTX)
    bf = jnp.bfloat16
    f32 = jnp.float32

    packed = projections.reshape(frames, ctx, items, 3 * head_size)
    packed = lax.all_to_all(packed, CTX, split_axis=1, concat_axis=0, tiled=True)
    packed = packed.reshape(length, items, 3 * head_size)

    both = jnp.concatenate([residual, out_grad], axis=-1)
    up = [(i, i + 1) for i in range(ctx - 1)]
    down = [(j, i) for i, j in up]
    before = lax.ppermute(both[frames - MARGIN :], CTX, up)
    after = lax.ppermute(both[:MARGIN], CTX, down)
    both = jnp.concatenate([before, both, after], axis=0)
    wide = frames + 2 * MARGIN
    place = me * frames - MARGIN + jnp.arange(wide, dtype=jnp.int32)
    valid = (place[:, None] >= 0) & (place[:, None] < lengths[None, :])
    row_mask = valid.astype(f32)[:, :, None]
    cot = jnp.where(valid[:, :, None], both[:, :, width:], 0)
    edge = MARGIN // 2
    near = wide - 2 * edge
    cot_near = cot[edge : edge + near]
    cot_own = cot[MARGIN : MARGIN + frames].reshape(frames * utter_count, width)
    act_grad = lax.dot_general(
        cot_near, down_weight, (((2,), (1,)), ((), ())), preferred_element_type=f32
    )

    key_lengths = lengths[(me * items + jnp.arange(items, dtype=jnp.int32)) // HEADS]
    context = attend(packed, key_lengths).reshape(length, items * head_size)
    padded = jnp.pad(context, ((MARGIN, MARGIN), (0, 0)))
    windows = jnp.stack([padded[i * frames : i * frames + wide] for i in range(ctx)])
    context = lax.all_to_all(windows, CTX, split_axis=0, concat_axis=0, tiled=True)
    context = jnp.transpose(context, (1, 0, 2)).reshape(wide, utter_count, width)

    cot_cols = lax.all_to_all(
        by_owner(cot_own, sizes), FIRST, split_axis=0, concat_axis=0, tiled=True
    )

    hidden = both[:, :, :width].astype(f32) + jnp.einsum(
        "fuc,cd->fud", context, out_weight, preferred_element_type=f32
    )
    normed_one, _ = normalize(hidden)
    scaled_one = (normed_one * gain_one).astype(bf)
    own = slice(MARGIN, MARGIN + frames)
    own_near = slice(MARGIN - edge, MARGIN - edge + frames)
    rows = frames * utter_count
    scaled_own = scaled_one[own].reshape(rows, width)
    scaled_all = gathered(scaled_own, chi)

    lifted = jnp.einsum("fuc,cd->fud", scaled_one, up_weight, preferred_element_type=f32)
    linear_part = lifted[:, :, :width]
    gate_part = jax.nn.sigmoid(lifted[:, :, width:])
    glu = (linear_part * gate_part * row_mask).astype(bf).astype(f32)
    conv_out = jnp.zeros((near, utter_count, width), f32)
    for j in range(kernel_len):
        start = edge + j - half
        conv_out = conv_out + conv_kernel[j] * glu[start : start + near]
    normed_two, inverse_two = normalize(conv_out)
    pre_act = normed_two * gain_two
    gate_two = jax.nn.sigmoid(pre_act)
    activated = (pre_act * gate_two)[own_near].astype(bf).reshape(rows, width)
    activated_all = gathered(activated, chi)
    block_out = (
        hidden[own].reshape(rows, width)
        + jnp.dot(activated, down_weight, preferred_element_type=f32)
    ).astype(bf)
    block_out = block_out.reshape(frames, utter_count, width)

    pre_grad = act_grad * gate_two * (1.0 + pre_act * (1.0 - gate_two))
    gain_two_grad = jnp.sum((pre_grad * normed_two)[own_near], axis=(0, 1))
    scaled_grad = pre_grad * gain_two
    conv_grad = inverse_two * (
        scaled_grad
        - jnp.mean(scaled_grad, axis=-1, keepdims=True)
        - normed_two * jnp.mean(scaled_grad * normed_two, axis=-1, keepdims=True)
    )
    conv_grad = conv_grad.astype(bf).astype(f32)
    conv_own = conv_grad[own_near]
    small = []
    glu_grad = jnp.zeros((frames, utter_count, width), f32)
    for j in range(kernel_len):
        start = MARGIN + j - half
        small.append(jnp.sum(conv_own * glu[start : start + frames], axis=(0, 1)))
        start = MARGIN - edge + half - j
        glu_grad = glu_grad + conv_kernel[j] * conv_grad[start : start + frames]
    glu_grad = glu_grad * row_mask[own]
    gate_own = gate_part[own]
    linear_grad = glu_grad * gate_own
    gate_grad = glu_grad * linear_part[own] * gate_own * (1.0 - gate_own)
    lifted_grad = jnp.concatenate([linear_grad, gate_grad], axis=-1).astype(bf)
    lifted_grad = lifted_grad.reshape(rows, 2 * width)
    input_grad = lax.dot_general(
        lifted_grad, up_weight, (((1,), (1,)), ((), ())), preferred_element_type=f32
    )
    gain_one_grad = jnp.sum(input_grad * normed_one[own].reshape(rows, width), axis=0)

    small = small + [gain_one_grad, gain_two_grad]
    count = kernel_len + 2
    small = by_owner(jnp.stack(small).astype(bf), sizes)
    small = small.reshape(dlo * chi, -1)
    cols = by_owner(lifted_grad, sizes)
    col_count = cols.shape[2]
    spare = -small.shape[1] % col_count
    small = jnp.pad(small, ((0, 0), (0, spare))).reshape(dlo * chi, -1, col_count)
    message = jnp.concatenate([cols, small], axis=1)
    message = lax.all_to_all(message, FIRST, split_axis=0, concat_axis=0, tiled=True)
    cols = message[:, :rows].reshape(-1, col_count)
    small = jnp.sum(message[:, rows:].astype(f32), axis=0).reshape(-1)
    seconds = dhi * clo
    small_width = width // (ctx * dhi * dlo)
    small = small[: count * seconds * small_width].reshape(count, seconds, small_width)
    small = jnp.transpose(small, (1, 0, 2)).reshape(seconds, count * small_width)

    up_part = lax.dot_general(
        cols, scaled_all, (((0,), (0,)), ((), ())), preferred_element_type=f32
    ).reshape(seconds, -1, width)
    down_part = lax.dot_general(
        cot_cols.reshape(cols.shape[0], -1),
        activated_all,
        (((0,), (0,)), ((), ())),
        preferred_element_type=f32,
    ).reshape(seconds, -1, width)
    spare = -small.shape[1] % width
    small = jnp.pad(small, ((0, 0), (0, spare))).reshape(seconds, -1, width)
    up_rows, down_rows = up_part.shape[1], down_part.shape[1]
    parts = jnp.concatenate([up_part.astype(bf), down_part.astype(bf), small.astype(bf)], axis=1)
    parts = lax.all_to_all(parts, SECOND, split_axis=0, concat_axis=0, tiled=True)
    total = jnp.sum(parts.astype(f32), axis=0)
    up_grad = total[:up_rows]
    down_grad = total[up_rows : up_rows + down_rows]
    small = total[up_rows + down_rows :].reshape(-1)[: count * small_width]
    small = small.reshape(count, small_width)
    kernel_grad = jnp.transpose(small[:kernel_len])
    return (block_out, up_grad, down_grad, kernel_grad, small[kernel_len], small[kernel_len + 1])


def solution(mesh):
    dp, ctx = mesh.shape["dp"], mesh.shape["ctx"]
    fine = Mesh(mesh.devices.reshape(dp // 2, 2, ctx // 2, 2), ("dhi", "dlo", "chi", "clo"))
    dp_axes, ctx_axes = ("dhi", "dlo"), ("chi", "clo")
    every = ("dhi", "dlo", "chi", "clo")
    in_specs = (
        P(ctx_axes, dp_axes, None),
        P(ctx_axes, dp_axes, None),
        P(),
        P(),
        P(),
        P(),
        P(),
        P(),
        P(dp_axes),
        P(ctx_axes, dp_axes, None),
    )
    out_specs = (
        P(ctx_axes, dp_axes, None),
        P(every, None),
        P(every, None),
        P(every, None),
        P(every),
        P(every),
    )
    return jax.shard_map(
        on_device, mesh=fine, in_specs=in_specs, out_specs=out_specs, check_vma=False
    )
```

```python
import functools

import jax
import jax.numpy as jnp
from jax import lax
from jax.experimental import pallas as pl
from jax.experimental.pallas import tpu as pltpu
from jax.sharding import Mesh, PartitionSpec as P

HEADS = 16


EPSILON = 1e-05

MARGIN = 32

CTX = ("chi", "clo")
FIRST = ("dlo", "chi")
SECOND = ("dhi", "clo")

SMEM = pl.BlockSpec(memory_space=pltpu.SMEM)
VMEM = pl.BlockSpec(memory_space=pltpu.VMEM)
HBM = pl.BlockSpec(memory_space=pltpu.HBM)


def normalize(values):
    center = values - jnp.mean(values, axis=-1, keepdims=True)
    inverse = lax.rsqrt(jnp.mean(center * center, axis=-1, keepdims=True) + EPSILON)
    return (center * inverse, inverse)


def attend(packed, key_lengths):
    length, count, triple = packed.shape
    head_size = triple // 3
    query_rows = packed[:, :, :head_size]
    key_rows = packed[:, :, head_size : 2 * head_size]
    value_rows = packed[:, :, 2 * head_size :]
    allowed = jnp.arange(length, dtype=jnp.int32)[None, :] < key_lengths[:, None]
    scores = (
        jnp.einsum("qmd,kmd->mqk", query_rows, key_rows, preferred_element_type=jnp.float32)
        * head_size ** (-0.5)
    )
    scores = jnp.where(allowed[:, None, :], scores, -jnp.inf)
    highest = jnp.max(scores, axis=-1, keepdims=True)
    raised = jnp.exp(scores - highest)
    weights_bf = (raised / jnp.sum(raised, axis=-1, keepdims=True)).astype(jnp.bfloat16)
    return jnp.einsum(
        "mqk,kmd->qmd", weights_bf, value_rows, preferred_element_type=jnp.float32
    ).astype(jnp.bfloat16)


def by_owner(cols, sizes):
    dhi, dlo, chi, clo = sizes
    rows, width = cols.shape
    part = width // (dhi * dlo * chi * clo)
    split = cols.reshape(rows, dhi, dlo, chi, clo, part)
    return jnp.transpose(split, (2, 3, 0, 1, 4, 5)).reshape(dlo * chi, rows, dhi * clo * part)


def gathered(rows, chi):
    copies = jnp.broadcast_to(rows[None], (chi,) + rows.shape)
    line = lax.all_to_all(copies, "chi", split_axis=0, concat_axis=0, tiled=True)
    line = line.reshape(chi * rows.shape[0], rows.shape[1])
    other = lax.ppermute(line, "dlo", [(0, 1), (1, 0)])
    first = lax.axis_index("dlo") == 0
    return jnp.concatenate([jnp.where(first, line, other), jnp.where(first, other, line)], axis=0)


def params(mebi=8):
    return pltpu.CompilerParams(vmem_limit_bytes=mebi * 1024 * 1024)


def struct(shape, dtype):
    return jax.ShapeDtypeStruct(shape, dtype)


def in_hbm(array):
    return pltpu.with_memory_space_constraint(array, pltpu.HBM)


def fetches(source, target, sems, parts):
    copies = []
    for i, part in enumerate(parts):
        copies.append(pltpu.make_async_copy(source.at[part], target.at[part], sems.at[i]))
        copies[-1].start()
    return copies


def split_kernel(proj_ref, out_ref, held_ref, sems):
    count, _, span = out_ref.shape
    copies = []
    for i in range(count):
        copies.append(
            pltpu.make_async_copy(
                proj_ref.at[:, pl.ds(i * span, span)], held_ref.at[i], sems.at[0, i]
            )
        )
        copies[-1].start()
    sends = []
    for i, copy in enumerate(copies):
        copy.wait()
        sends.append(pltpu.make_async_copy(held_ref.at[i], out_ref.at[i], sems.at[1, i]))
        sends[-1].start()
    for send in sends:
        send.wait()


def split_heads(proj, count):
    rows, cols = proj.shape
    shape = (count, rows, cols // count)
    return pl.pallas_call(
        split_kernel,
        out_shape=struct(shape, proj.dtype),
        in_specs=[HBM],
        out_specs=HBM,
        scratch_shapes=[pltpu.VMEM(shape, proj.dtype), pltpu.SemaphoreType.DMA((2, count))],
        compiler_params=params(),
        name="split_heads",
    )(in_hbm(proj))


def edge_kernel(res_ref, grad_ref, low_ref, high_ref, sems):
    rows = res_ref.shape[0]
    copies = []
    for i, (source, at, count) in enumerate(
        ((res_ref, 0, MARGIN), (grad_ref, MARGIN, MARGIN // 2))
    ):
        for j, (target, start) in enumerate(((high_ref, rows - count), (low_ref, 0))):
            copies.append(
                pltpu.make_async_copy(
                    source.at[pl.ds(start, count)], target.at[pl.ds(at, count)], sems.at[i, j]
                )
            )
            copies[-1].start()
    for copy in copies:
        copy.wait()


def edges(res, grad):
    shape = struct((MARGIN + MARGIN // 2, res.shape[1]), res.dtype)
    spec = pl.BlockSpec(memory_space=pl.ANY)
    return pl.pallas_call(
        edge_kernel,
        out_shape=(shape, shape),
        in_specs=[HBM, HBM],
        out_specs=(spec, spec),
        scratch_shapes=[pltpu.SemaphoreType.DMA((2, 2))],
        compiler_params=params(),
        name="edges",
    )(in_hbm(res), in_hbm(grad))


def attend_kernel(head_size, frames, scalar_ref, qkv_ref, out_ref):
    length = qkv_ref.shape[0]
    count = qkv_ref.shape[1] // (3 * head_size)
    ctx, wide, _ = out_ref.shape
    allowed = lax.broadcasted_iota(jnp.int32, (length, length), 1) < scalar_ref[0]
    outs = []
    for m in range(count):
        base = 3 * head_size * m
        query = qkv_ref[:, base : base + head_size]
        key = qkv_ref[:, base + head_size : base + 2 * head_size]
        value = qkv_ref[:, base + 2 * head_size : base + 3 * head_size]
        scores = (
            lax.dot_general(
                query, key, (((1,), (1,)), ((), ())), preferred_element_type=jnp.float32
            )
            * head_size ** (-0.5)
        )
        scores = jnp.where(allowed, scores, -jnp.inf)
        raised = jnp.exp(scores - jnp.max(scores, axis=-1, keepdims=True))
        weights = raised * (1.0 / jnp.sum(raised, axis=-1, keepdims=True))
        outs.append(
            jnp.dot(weights.astype(jnp.bfloat16), value, preferred_element_type=jnp.float32)
        )
    context = jnp.concatenate(outs, axis=1).astype(jnp.bfloat16)
    for i in range(ctx):
        low = max(i * frames - MARGIN, 0)
        high = min(i * frames - MARGIN + wide, length)
        at = low - (i * frames - MARGIN)
        out_ref[i, at : at + high - low, :] = context[low:high]
        if at > 0:
            out_ref[i, :at, :] = jnp.zeros((at, context.shape[1]), context.dtype)
        if at + high - low < wide:
            rest = wide - (at + high - low)
            out_ref[i, wide - rest :, :] = jnp.zeros((rest, context.shape[1]), context.dtype)


def attend_windows(scalars, qkv, head_size, frames, ctx):
    wide = frames + 2 * MARGIN
    return pl.pallas_call(
        functools.partial(attend_kernel, head_size, frames),
        out_shape=struct((ctx, wide, qkv.shape[1] // 3), jnp.bfloat16),
        in_specs=[SMEM, VMEM],
        out_specs=VMEM,
        compiler_params=params(16),
        name="attend",
    )(scalars, qkv)


def cot_kernel(scalar_ref, grad_ref, low_ref, high_ref, weight_ref, *refs):
    cols_refs, (act_ref, held_ref, weight_held_ref, sems) = refs[:4], refs[4:]
    frames, width = grad_ref.shape
    copies = fetches(
        weight_ref, weight_held_ref, sems, [pl.ds(i * 256, 256) for i in range(width // 256)]
    )
    edge = MARGIN // 2
    whole = jnp.concatenate([low_ref[MARGIN:, :], grad_ref[...], high_ref[MARGIN:, :]], axis=0)
    near = whole.shape[0]
    place = scalar_ref[1] - edge + lax.broadcasted_iota(jnp.int32, (near, width), 0)
    valid = (place >= 0) & (place < scalar_ref[0])
    whole = jnp.where(valid, whole.astype(jnp.float32), 0.0).astype(jnp.bfloat16)
    cot = whole[edge : edge + frames]
    count, _, span = held_ref.shape
    piece = span // 4
    for group in range(count):
        high_bits, low_bit = group // 2, group % 2
        held_ref[group, :, :] = jnp.concatenate(
            [
                cot[:, (8 * high_bits + 2 * z + low_bit) * piece :][:, :piece]
                for z in range(4)
            ],
            axis=1,
        )
    dhi, dlo, clo = scalar_ref[5], scalar_ref[2], scalar_ref[6]
    for k, cols_ref in enumerate(cols_refs):
        for side in range(2):
            group = ((dhi ^ (k // 2)) * 2 + (dlo ^ side)) * 2 + (clo ^ (k % 2))
            cols_ref[:, side * span : (side + 1) * span] = held_ref[group]
    for copy in copies:
        copy.wait()
    act_ref[...] = lax.dot_general(
        whole, weight_held_ref[...], (((1,), (1,)), ((), ())), preferred_element_type=jnp.float32
    )


def cot_part(scalars, grad, low, high, weight):
    frames, width = grad.shape
    cols = struct((frames, width // 4), grad.dtype)
    return pl.pallas_call(
        cot_kernel,
        out_shape=(cols, cols, cols, cols, struct((frames + MARGIN, width), jnp.float32)),
        in_specs=[SMEM, VMEM, VMEM, VMEM, HBM],
        out_specs=(VMEM,) * 5,
        scratch_shapes=[
            pltpu.VMEM((8, frames, width // 8), grad.dtype),
            pltpu.VMEM(weight.shape, weight.dtype),
            pltpu.SemaphoreType.DMA((width // 256,)),
        ],
        compiler_params=params(12),
        name="cotangent",
    )(scalars, grad, low, high, in_hbm(weight))


def forward_kernel(
    scalar_ref, context_ref, res_ref, low_ref, high_ref, out_ref, gain_one_ref, weight_ref,
    taps_ref, gain_ref, cols_own_ref, cols_y_ref, cols_x_ref, cols_xy_ref,
    hidden_ref, one_ref, own_ref, act_ref, to_y_ref, to_x_ref, to_xy_ref, linear_ref, gate_ref, glu_ref,
    normed_ref, inverse_ref, scaled_ref, conv_ref, out_held_ref, held_ref, res_held_ref, out_sems, sems, res_sems,
):
    frames, width = res_ref.shape
    ctx, wide, lanes = context_ref.shape
    taps = taps_ref.shape[0]
    half = (taps - 1) // 2
    edge = MARGIN // 2
    near = wide - 2 * edge
    depth = 2 * lanes
    res_copies = fetches(res_ref, res_held_ref, res_sems, [slice(None)])
    out_copies = fetches(
        out_ref, out_held_ref, out_sems, [pl.ds(i * depth, depth) for i in range(ctx // 2)]
    )
    span = 256
    copies = fetches(
        weight_ref, held_ref, sems, [pl.ds(i * span, span) for i in range(width // span)]
    )
    product = jnp.zeros((wide, width), jnp.float32)
    for i, copy in enumerate(out_copies):
        copy.wait()
        product = product + jnp.dot(
            jnp.concatenate([context_ref[2 * i], context_ref[2 * i + 1]], axis=1),
            out_held_ref[i * depth : (i + 1) * depth, :],
            preferred_element_type=jnp.float32,
        )
    res_copies[0].wait()
    step = 32
    for at in range(0, wide, step):
        if at < MARGIN:
            res = low_ref[at : at + step, :]
        elif at < MARGIN + frames:
            res = res_held_ref[at - MARGIN : at - MARGIN + step, :]
        else:
            res = high_ref[at - MARGIN - frames : at - MARGIN - frames + step, :]
        hidden = res.astype(jnp.float32) + product[at : at + step]
        normed, _ = normalize(hidden)
        scaled = (normed * gain_one_ref[...]).astype(jnp.bfloat16)
        scaled_ref[at : at + step, :] = scaled
        if MARGIN <= at < MARGIN + frames:
            rows = slice(at - MARGIN, at - MARGIN + step)
            hidden_ref[rows, :] = hidden
            one_ref[rows, :] = normed
            own_ref[rows, :] = scaled
    for copy in copies:
        copy.wait()
    place = scalar_ref[1] - MARGIN + lax.broadcasted_iota(jnp.int32, (wide, span), 0)
    valid = (place >= 0) & (place < scalar_ref[0])
    own = slice(MARGIN, MARGIN + frames)
    for i in range(width // span):
        cols = slice(i * span, (i + 1) * span)
        linear = jnp.dot(scaled_ref[...], held_ref[:, cols], preferred_element_type=jnp.float32)
        gate = jax.nn.sigmoid(
            jnp.dot(
                scaled_ref[...],
                held_ref[:, width + i * span : width + (i + 1) * span],
                preferred_element_type=jnp.float32,
            )
        )
        glu = jnp.where(valid, linear * gate, 0.0).astype(jnp.bfloat16).astype(jnp.float32)
        glu_ref[:, cols] = glu
        linear_ref[:, cols] = linear[own]
        gate_ref[:, cols] = gate[own]
        for at in range(i * span, (i + 1) * span, 128):
            lane = slice(at, at + 128)
            block = glu[:, at - i * span : at - i * span + 128]
            total = jnp.zeros((near, 128), jnp.float32)
            for shift in range(8):
                moved = block if shift == 0 else pltpu.roll(block, wide - shift, 0)
                for j in range(taps):
                    start = edge + j - half
                    if start % 8 == shift:
                        total = total + taps_ref[j : j + 1, lane] * moved[
                            start - shift : start - shift + near
                        ]
            conv_ref[:, lane] = total
    step = 16
    for at in range(0, near, step):
        normed, inverse = normalize(conv_ref[at : at + step, :])
        normed_ref[at : at + step, :] = normed
        inverse_ref[at : at + step, :] = jnp.broadcast_to(inverse, (step, 128))
        if MARGIN - edge <= at < MARGIN - edge + frames:
            pre = normed * gain_ref[...]
            rows = slice(at - (MARGIN - edge), at - (MARGIN - edge) + step)
            act = (pre * jax.nn.sigmoid(pre)).astype(jnp.bfloat16)
            for ref in (act_ref, to_y_ref, to_x_ref, to_xy_ref):
                ref[rows, :width] = act
    act_ref[:, width:] = cols_own_ref[...]
    to_y_ref[:, width:] = cols_y_ref[...]
    to_x_ref[:, width:] = cols_x_ref[...]
    to_xy_ref[:, width:] = cols_xy_ref[...]


def forward_part(scalars, context, res, low, high, out_weight, gain_one, weight, taps, gain, cols):
    frames, width = res.shape
    ctx, wide, _ = context.shape
    near = wide - MARGIN
    f32, bf = jnp.float32, jnp.bfloat16
    return pl.pallas_call(
        forward_kernel,
        out_shape=(
            struct((frames, width), f32),
            struct((frames, width), f32),
            struct((frames, width), bf),
            struct((frames, width + width // 4), bf),
            struct((frames, width + width // 4), bf),
            struct((frames, width + width // 4), bf),
            struct((frames, width + width // 4), bf),
            struct((frames, width), f32),
            struct((frames, width), f32),
            struct((wide, width), f32),
            struct((near, width), f32),
            struct((near, 128), f32),
        ),
        in_specs=[SMEM, VMEM, HBM, VMEM, VMEM, HBM, VMEM, HBM] + [VMEM] * 6,
        out_specs=(VMEM,) * 12,
        scratch_shapes=[
            pltpu.VMEM((wide, width), bf),
            pltpu.VMEM((near, width), f32),
            pltpu.VMEM(out_weight.shape, bf),
            pltpu.VMEM(weight.shape, bf),
            pltpu.VMEM(res.shape, bf),
            pltpu.SemaphoreType.DMA((ctx // 2,)),
            pltpu.SemaphoreType.DMA((width // 256,)),
            pltpu.SemaphoreType.DMA((1,)),
        ],
        compiler_params=params(24),
        name="forward",
    )(
        scalars, context, in_hbm(res), low, high, in_hbm(out_weight), gain_one, in_hbm(weight), taps, gain,
        *cols,
    )


def back_kernel(
    scalar_ref, act_grad_ref, one_ref, linear_ref, gate_ref,
    glu_ref, normed_ref, inverse_ref, taps_ref, gain_ref, up_ref,
    message_ref, grad_ref, small_ref, lifted_ref, held_ref, sems,
):
    frames, width = one_ref.shape
    near = normed_ref.shape[0]
    wide = glu_ref.shape[0]
    taps = taps_ref.shape[0]
    half = (taps - 1) // 2
    edge = MARGIN // 2
    first = MARGIN - edge
    copies = fetches(up_ref, held_ref, sems, [pl.ds(i * 256, 256) for i in range(width // 256)])
    gain = gain_ref[...]
    step = 16
    two = jnp.zeros((1, width), jnp.float32)
    for at in range(0, near, step):
        normed = normed_ref[at : at + step, :]
        pre = normed * gain
        gate = jax.nn.sigmoid(pre)
        grad = act_grad_ref[at : at + step, :] * gate * (1.0 + pre * (1.0 - gate))
        if first <= at < first + frames:
            two = two + jnp.sum(grad * normed, axis=0, keepdims=True)
        scaled = grad * gain
        result = inverse_ref[at : at + step, 0:1] * (
            scaled
            - jnp.mean(scaled, axis=-1, keepdims=True)
            - normed * jnp.mean(scaled * normed, axis=-1, keepdims=True)
        )
        grad_ref[at : at + step, :] = result.astype(jnp.bfloat16).astype(jnp.float32)
    small_ref[32:, :] = jnp.zeros((16, width), jnp.float32)
    small_ref[taps + 1 : taps + 2, :] = two

    place = scalar_ref[1] + lax.broadcasted_iota(jnp.int32, (frames, 128), 0)
    valid = place < scalar_ref[0]

    def lanes(i, carry):
        cols = pl.ds(pl.multiple_of(i * 128, 128), 128)
        high = pl.ds(pl.multiple_of(i * 128 + width, 128), 128)
        block = grad_ref[:, cols]
        own = block[first : first + frames]
        total = jnp.zeros((frames, 128), jnp.float32)
        for shift in range(8):
            moved = block if shift == 0 else pltpu.roll(block, near - shift, 0)
            for j in range(taps):
                start = first + half - j
                if start % 8 == shift:
                    total = total + taps_ref[j : j + 1, cols] * moved[start - shift : start - shift + frames]
        block = glu_ref[:, cols]
        for shift in range(8):
            moved = block if shift == 0 else pltpu.roll(block, wide - shift, 0)
            for j in range(taps):
                start = MARGIN + j - half
                if start % 8 == shift:
                    small_ref[j : j + 1, cols] = jnp.sum(
                        own * moved[start - shift : start - shift + frames], axis=0, keepdims=True
                    )
        total = jnp.where(valid, total, 0.0)
        gate = gate_ref[:, cols]
        linear_grad = (total * gate).astype(jnp.bfloat16)
        gate_grad = (total * linear_ref[:, cols] * gate * (1.0 - gate)).astype(jnp.bfloat16)
        lifted_ref[:, cols] = linear_grad
        lifted_ref[:, high] = gate_grad
        message_ref[i, :frames, :128] = linear_grad
        message_ref[i, :frames, 128:256] = gate_grad
        return carry

    lax.fori_loop(0, width // 128, lanes, 0)
    for copy in copies:
        copy.wait()
    input_grad = lax.dot_general(
        lifted_ref[...], held_ref[...], (((1,), (1,)), ((), ())), preferred_element_type=jnp.float32
    )
    small_ref[taps : taps + 1, :] = jnp.sum(input_grad * one_ref[...], axis=0, keepdims=True)
    for i in range(width // 128):
        for part in range(2):
            rows = small_ref[part * 24 : (part + 1) * 24, :]
            message_ref[i, frames:, part * 128 : (part + 1) * 128] = jnp.concatenate(
                [rows[:, i * 64 : (i + 1) * 64], rows[:, (i + 8) * 64 : (i + 9) * 64]], axis=1
            ).astype(jnp.bfloat16)


def block_kernel(hidden_ref, activated_ref, down_ref, block_ref, held_ref, sems):
    width = hidden_ref.shape[1]
    copies = fetches(
        down_ref, held_ref, sems, [pl.ds(i * 256, 256) for i in range(width // 256)]
    )
    for copy in copies:
        copy.wait()
    block_ref[...] = (
        hidden_ref[...]
        + jnp.dot(
            activated_ref[:, :width], held_ref[...], preferred_element_type=jnp.float32
        )
    ).astype(jnp.bfloat16)


def block_part(hidden, activated, down):
    return pl.pallas_call(
        block_kernel,
        out_shape=struct(hidden.shape, jnp.bfloat16),
        in_specs=[VMEM, VMEM, HBM],
        out_specs=VMEM,
        scratch_shapes=[
            pltpu.VMEM(down.shape, down.dtype),
            pltpu.SemaphoreType.DMA((down.shape[0] // 256,)),
        ],
        compiler_params=params(12),
        name="block_out",
    )(hidden, activated, in_hbm(down))


def back_part(*operands):
    frames, width = operands[2].shape
    near = frames + MARGIN
    f32, bf = jnp.float32, jnp.bfloat16
    return pl.pallas_call(
        back_kernel,
        out_shape=struct((width // 128, frames + 24, 256), bf),
        in_specs=[SMEM] + [VMEM] * 9 + [HBM],
        out_specs=VMEM,
        scratch_shapes=[
            pltpu.VMEM((near, width), f32),
            pltpu.VMEM((48, width), f32),
            pltpu.VMEM((frames, 2 * width), bf),
            pltpu.VMEM((width, 2 * width), bf),
            pltpu.SemaphoreType.DMA((width // 256,)),
        ],
        compiler_params=params(20),
        name="backward",
    )(*operands[:-1], in_hbm(operands[-1]))


TURNED = (((0,), (0,)), ((), ()))


def up_kernel(count, scalar_ref, message_ref, *refs):
    parts_ref, cols_ref, one_ref = refs[2 * count :]
    frames, width = refs[0].shape
    core, line = scalar_ref[2], scalar_ref[3]
    small = jnp.zeros((24, 256), jnp.float32)
    for side in range(2):
        for k in range(count):
            at = (side * count + k) * frames
            source = (core ^ side) * count + (line ^ k)
            cols_ref[at : at + frames, :] = message_ref[source, :frames, :]
            one_ref[at : at + frames, :] = refs[side * count + k][...]
            small = small + message_ref[source, frames:, :].astype(jnp.float32)
    up = lax.dot_general(
        cols_ref[...], one_ref[...], TURNED, preferred_element_type=jnp.float32
    ).astype(jnp.bfloat16)
    small = small.astype(jnp.bfloat16)
    for s in range(4):
        parts_ref[s, :64, :] = up[s * 64 : (s + 1) * 64]
        for i in range(3):
            parts_ref[s, 64:, i * 256 : (i + 1) * 256] = small[i * 8 : (i + 1) * 8]
        parts_ref[s, 64:, 768:] = jnp.zeros((8, width - 768), jnp.bfloat16)


def up_part(scalars, message, pieces):
    count = len(pieces) // 2
    frames, width = pieces[0].shape
    bf = jnp.bfloat16
    rows = 2 * count * frames
    return pl.pallas_call(
        functools.partial(up_kernel, count),
        out_shape=struct((4, 72, width), bf),
        in_specs=[SMEM, VMEM] + [VMEM] * len(pieces),
        out_specs=VMEM,
        scratch_shapes=[pltpu.VMEM((rows, 256), bf), pltpu.VMEM((rows, width), bf)],
        compiler_params=params(12),
        name="up_products",
    )(scalars, message, *pieces)


def down_kernel(scalar_ref, *refs):
    count = (len(refs) - 3) // 3
    pieces, outs = refs[: 2 * count], refs[2 * count : 3 * count]
    cols_ref, rows_ref, total_ref = refs[3 * count :]
    frames, width = pieces[0].shape[0], rows_ref.shape[1]
    span = cols_ref.shape[1]
    for i, piece in enumerate(pieces):
        rows = slice(i * frames, (i + 1) * frames)
        at = width + (i // count) * span
        rows_ref[rows, :] = piece[:, :width]
        cols_ref[rows, :] = piece[:, at : at + span]
    total_ref[...] = lax.dot_general(
        cols_ref[...], rows_ref[...], TURNED, preferred_element_type=jnp.float32
    )
    line = scalar_ref[3]
    for k, out in enumerate(outs):
        at = pl.multiple_of((line ^ k) * 32, 32)
        out[...] = total_ref[pl.ds(at, 32), :].astype(jnp.bfloat16)


def down_part(scalars, pieces, width):
    count = len(pieces) // 2
    frames = pieces[0].shape[0]
    bf = jnp.bfloat16
    rows = 2 * count * frames
    return pl.pallas_call(
        down_kernel,
        out_shape=(struct((32, width), bf),) * count,
        in_specs=[SMEM] + [VMEM] * (2 * count),
        out_specs=(VMEM,) * count,
        scratch_shapes=[
            pltpu.VMEM((rows, 128), bf),
            pltpu.VMEM((rows, width), bf),
            pltpu.VMEM((128, width), jnp.float32),
        ],
        compiler_params=params(12),
        name="down_products",
    )(scalars, *pieces)


def sum_kernel(taps, scalar_ref, parts_ref, *refs):
    pieces, (up_ref, down_ref, kernel_ref, one_ref, two_ref) = refs[:4], refs[4:]
    total = parts_ref[0].astype(jnp.float32)
    for s in range(1, parts_ref.shape[0]):
        total = total + parts_ref[s].astype(jnp.float32)
    up_ref[...] = total[:64]
    down_ref[...] = (pieces[0][...].astype(jnp.float32) + pieces[1][...].astype(jnp.float32)) + (
        pieces[2][...].astype(jnp.float32) + pieces[3][...].astype(jnp.float32)
    )
    small = jnp.concatenate(
        [
            total[64:72, i * 256 + part * 128 : i * 256 + part * 128 + 128]
            for part in range(2)
            for i in range(3)
        ],
        axis=0,
    )
    small = pltpu.roll(small, (128 - 32 * scalar_ref[4]) % 128, 1)
    kernel_ref[...] = jnp.transpose(small[:32])[:32, :taps]
    one_ref[...] = small[taps : taps + 1, :32]
    two_ref[...] = small[taps + 1 : taps + 2, :32]


def sum_part(scalars, parts, pieces, taps):
    width = parts.shape[2]
    f32 = jnp.float32
    return pl.pallas_call(
        functools.partial(sum_kernel, taps),
        out_shape=(
            struct((64, width), f32),
            struct((32, width), f32),
            struct((32, taps), f32),
            struct((1, 32), f32),
            struct((1, 32), f32),
        ),
        in_specs=[SMEM] + [VMEM] * 5,
        out_specs=(VMEM,) * 5,
        compiler_params=params(),
        name="sums",
    )(scalars, parts, *pieces)


def flipped(rows, axis, bit):
    size = lax.axis_size(axis)
    return lax.ppermute(rows, axis, [(i, i ^ bit) for i in range(size)])


def with_swapped(pieces):
    return list(pieces) + [flipped(piece, "dlo", 1) for piece in pieces]


def small_device(
    residual, projections, out_weight, gain_one, up_weight, conv_kernel, gain_two, down_weight,
    lengths, out_grad,
):
    frames, _, width = residual.shape
    taps = conv_kernel.shape[0]
    chi, clo = lax.axis_size("chi"), lax.axis_size("clo")
    ctx = chi * clo
    head_size = width // HEADS
    me = lax.axis_index(CTX)
    second = lax.axis_index("dhi") * clo + lax.axis_index("clo")
    scalars = jnp.stack(
        [
            lengths[0], me * frames, lax.axis_index("dlo"), lax.axis_index("chi"), second,
            lax.axis_index("dhi"), lax.axis_index("clo"),
        ]
    ).astype(jnp.int32)
    res = residual.reshape(frames, width)
    grad = out_grad.reshape(frames, width)
    gain_one = gain_one.reshape(1, width)
    gain_two = gain_two.reshape(1, width)

    qkv = split_heads(projections.reshape(frames, 3 * width), ctx)
    qkv = lax.all_to_all(qkv, CTX, split_axis=0, concat_axis=0, tiled=True)
    low, high = edges(res, grad)
    up = [(i, i + 1) for i in range(ctx - 1)]
    down = [(j, i) for i, j in up]
    before = lax.ppermute(high, CTX, up)
    after = lax.ppermute(low, CTX, down)
    qkv, before, after = lax.optimization_barrier((qkv, before, after))
    windows = attend_windows(scalars, qkv.reshape(ctx * frames, -1), head_size, frames, ctx)
    windows, before, after = lax.optimization_barrier((windows, before, after))
    windows = lax.all_to_all(windows, CTX, split_axis=0, concat_axis=0, tiled=True)
    *cols, act_grad = cot_part(scalars, grad, before, after, down_weight)
    windows, act_grad, cols = lax.optimization_barrier((windows, act_grad, cols))

    (
        hidden, normed_one, scaled, activated, to_y, to_x, to_xy, linear, gate, glu,
        normed_two, inverse_two,
    ) = forward_part(
        scalars, windows, res, before, after, out_weight, gain_one, up_weight, conv_kernel,
        gain_two, cols,
    )
    pairs = [(i, i ^ 3) for i in range(4)]
    received = (
        flipped(scaled, "chi", 2),
        flipped(scaled, "chi", 1),
        flipped(to_x, "dhi", 1),
        flipped(to_y, "clo", 1),
        lax.ppermute(to_xy, SECOND, pairs),
    )
    message = back_part(
        scalars, act_grad, normed_one, linear, gate,
        glu, normed_two, inverse_two, conv_kernel, gain_two, up_weight,
    )
    message, received = lax.optimization_barrier((message, received))
    one_far, one_near, from_x, from_y, from_xy = received
    message = lax.all_to_all(message, FIRST, split_axis=0, concat_axis=0, tiled=True)
    one_last = flipped(one_far, "chi", 1)
    downs = down_part(scalars, with_swapped([activated, from_y, from_x, from_xy]), width)
    block_out = block_part(hidden, activated, down_weight)
    early = with_swapped([scaled, one_near, one_far])
    one_last, downs, block_out, early = lax.optimization_barrier(
        (one_last, downs, block_out, early)
    )
    last = with_swapped([one_last])
    ones = early[:3] + last[:1] + early[3:] + last[1:]
    parts = up_part(scalars, message, ones)
    parts = lax.all_to_all(parts, SECOND, split_axis=0, concat_axis=0, tiled=True)
    downs = [downs[0]] + [flipped(downs[k], "chi", k) for k in range(1, chi)]
    up_grad, down_grad, kernel_grad, one, two = sum_part(scalars, parts, downs, taps)
    return (
        block_out.reshape(frames, 1, width), up_grad, down_grad, kernel_grad,
        one.reshape(-1), two.reshape(-1),
    )


def fits(residual, conv_kernel, sizes):
    dhi, dlo, chi, clo = sizes
    frames, utter_count, width = residual.shape
    return (
        utter_count == 1
        and frames == 64
        and width == 1024
        and conv_kernel.shape[0] == 31
        and (dhi, dlo, chi, clo) == (2, 2, 4, 2)
    )


def on_device(
    residual,
    projections,
    out_weight,
    gain_one,
    up_weight,
    conv_kernel,
    gain_two,
    down_weight,
    lengths,
    out_grad,
):
    frames, utter_count, width = residual.shape
    head_size = width // HEADS
    kernel_len = conv_kernel.shape[0]
    half = (kernel_len - 1) // 2
    dhi, dlo, chi, clo = sizes = tuple(lax.axis_size(a) for a in ("dhi", "dlo", "chi", "clo"))
    if fits(residual, conv_kernel, sizes):
        return small_device(
            residual,
            projections,
            out_weight,
            gain_one,
            up_weight,
            conv_kernel,
            gain_two,
            down_weight,
            lengths,
            out_grad,
        )
    ctx = chi * clo
    length = frames * ctx
    items = utter_count * HEADS // ctx
    me = lax.axis_index(CTX)
    bf = jnp.bfloat16
    f32 = jnp.float32

    packed = projections.reshape(frames, ctx, items, 3 * head_size)
    packed = lax.all_to_all(packed, CTX, split_axis=1, concat_axis=0, tiled=True)
    packed = packed.reshape(length, items, 3 * head_size)

    both = jnp.concatenate([residual, out_grad], axis=-1)
    up = [(i, i + 1) for i in range(ctx - 1)]
    down = [(j, i) for i, j in up]
    before = lax.ppermute(both[frames - MARGIN :], CTX, up)
    after = lax.ppermute(both[:MARGIN], CTX, down)
    both = jnp.concatenate([before, both, after], axis=0)
    wide = frames + 2 * MARGIN
    place = me * frames - MARGIN + jnp.arange(wide, dtype=jnp.int32)
    valid = (place[:, None] >= 0) & (place[:, None] < lengths[None, :])
    row_mask = valid.astype(f32)[:, :, None]
    cot = jnp.where(valid[:, :, None], both[:, :, width:], 0)
    edge = MARGIN // 2
    near = wide - 2 * edge
    cot_near = cot[edge : edge + near]
    cot_own = cot[MARGIN : MARGIN + frames].reshape(frames * utter_count, width)
    act_grad = lax.dot_general(
        cot_near, down_weight, (((2,), (1,)), ((), ())), preferred_element_type=f32
    )

    key_lengths = lengths[(me * items + jnp.arange(items, dtype=jnp.int32)) // HEADS]
    context = attend(packed, key_lengths).reshape(length, items * head_size)
    padded = jnp.pad(context, ((MARGIN, MARGIN), (0, 0)))
    windows = jnp.stack([padded[i * frames : i * frames + wide] for i in range(ctx)])
    context = lax.all_to_all(windows, CTX, split_axis=0, concat_axis=0, tiled=True)
    context = jnp.transpose(context, (1, 0, 2)).reshape(wide, utter_count, width)

    cot_cols = lax.all_to_all(
        by_owner(cot_own, sizes), FIRST, split_axis=0, concat_axis=0, tiled=True
    )

    hidden = both[:, :, :width].astype(f32) + jnp.einsum(
        "fuc,cd->fud", context, out_weight, preferred_element_type=f32
    )
    normed_one, _ = normalize(hidden)
    scaled_one = (normed_one * gain_one).astype(bf)
    own = slice(MARGIN, MARGIN + frames)
    own_near = slice(MARGIN - edge, MARGIN - edge + frames)
    rows = frames * utter_count
    scaled_own = scaled_one[own].reshape(rows, width)
    scaled_all = gathered(scaled_own, chi)

    lifted = jnp.einsum("fuc,cd->fud", scaled_one, up_weight, preferred_element_type=f32)
    linear_part = lifted[:, :, :width]
    gate_part = jax.nn.sigmoid(lifted[:, :, width:])
    glu = (linear_part * gate_part * row_mask).astype(bf).astype(f32)
    conv_out = jnp.zeros((near, utter_count, width), f32)
    for j in range(kernel_len):
        start = edge + j - half
        conv_out = conv_out + conv_kernel[j] * glu[start : start + near]
    normed_two, inverse_two = normalize(conv_out)
    pre_act = normed_two * gain_two
    gate_two = jax.nn.sigmoid(pre_act)
    activated = (pre_act * gate_two)[own_near].astype(bf).reshape(rows, width)
    activated_all = gathered(activated, chi)
    block_out = (
        hidden[own].reshape(rows, width)
        + jnp.dot(activated, down_weight, preferred_element_type=f32)
    ).astype(bf)
    block_out = block_out.reshape(frames, utter_count, width)

    pre_grad = act_grad * gate_two * (1.0 + pre_act * (1.0 - gate_two))
    gain_two_grad = jnp.sum((pre_grad * normed_two)[own_near], axis=(0, 1))
    scaled_grad = pre_grad * gain_two
    conv_grad = inverse_two * (
        scaled_grad
        - jnp.mean(scaled_grad, axis=-1, keepdims=True)
        - normed_two * jnp.mean(scaled_grad * normed_two, axis=-1, keepdims=True)
    )
    conv_grad = conv_grad.astype(bf).astype(f32)
    conv_own = conv_grad[own_near]
    small = []
    glu_grad = jnp.zeros((frames, utter_count, width), f32)
    for j in range(kernel_len):
        start = MARGIN + j - half
        small.append(jnp.sum(conv_own * glu[start : start + frames], axis=(0, 1)))
        start = MARGIN - edge + half - j
        glu_grad = glu_grad + conv_kernel[j] * conv_grad[start : start + frames]
    glu_grad = glu_grad * row_mask[own]
    gate_own = gate_part[own]
    linear_grad = glu_grad * gate_own
    gate_grad = glu_grad * linear_part[own] * gate_own * (1.0 - gate_own)
    lifted_grad = jnp.concatenate([linear_grad, gate_grad], axis=-1).astype(bf)
    lifted_grad = lifted_grad.reshape(rows, 2 * width)
    input_grad = lax.dot_general(
        lifted_grad, up_weight, (((1,), (1,)), ((), ())), preferred_element_type=f32
    )
    gain_one_grad = jnp.sum(input_grad * normed_one[own].reshape(rows, width), axis=0)

    small = small + [gain_one_grad, gain_two_grad]
    count = kernel_len + 2
    small = by_owner(jnp.stack(small).astype(bf), sizes)
    small = small.reshape(dlo * chi, -1)
    cols = by_owner(lifted_grad, sizes)
    col_count = cols.shape[2]
    spare = -small.shape[1] % col_count
    small = jnp.pad(small, ((0, 0), (0, spare))).reshape(dlo * chi, -1, col_count)
    message = jnp.concatenate([cols, small], axis=1)
    message = lax.all_to_all(message, FIRST, split_axis=0, concat_axis=0, tiled=True)
    cols = message[:, :rows].reshape(-1, col_count)
    small = jnp.sum(message[:, rows:].astype(f32), axis=0).reshape(-1)
    seconds = dhi * clo
    small_width = width // (ctx * dhi * dlo)
    small = small[: count * seconds * small_width].reshape(count, seconds, small_width)
    small = jnp.transpose(small, (1, 0, 2)).reshape(seconds, count * small_width)

    up_part = lax.dot_general(
        cols, scaled_all, (((0,), (0,)), ((), ())), preferred_element_type=f32
    ).reshape(seconds, -1, width)
    down_part = lax.dot_general(
        cot_cols.reshape(cols.shape[0], -1),
        activated_all,
        (((0,), (0,)), ((), ())),
        preferred_element_type=f32,
    ).reshape(seconds, -1, width)
    spare = -small.shape[1] % width
    small = jnp.pad(small, ((0, 0), (0, spare))).reshape(seconds, -1, width)
    up_rows, down_rows = up_part.shape[1], down_part.shape[1]
    parts = jnp.concatenate([up_part.astype(bf), down_part.astype(bf), small.astype(bf)], axis=1)
    parts = lax.all_to_all(parts, SECOND, split_axis=0, concat_axis=0, tiled=True)
    total = jnp.sum(parts.astype(f32), axis=0)
    up_grad = total[:up_rows]
    down_grad = total[up_rows : up_rows + down_rows]
    small = total[up_rows + down_rows :].reshape(-1)[: count * small_width]
    small = small.reshape(count, small_width)
    kernel_grad = jnp.transpose(small[:kernel_len])
    return (block_out, up_grad, down_grad, kernel_grad, small[kernel_len], small[kernel_len + 1])


def solution(mesh):
    dp, ctx = mesh.shape["dp"], mesh.shape["ctx"]
    fine = Mesh(mesh.devices.reshape(dp // 2, 2, ctx // 2, 2), ("dhi", "dlo", "chi", "clo"))
    dp_axes, ctx_axes = ("dhi", "dlo"), ("chi", "clo")
    every = ("dhi", "dlo", "chi", "clo")
    in_specs = (
        P(ctx_axes, dp_axes, None),
        P(ctx_axes, dp_axes, None),
        P(),
        P(),
        P(),
        P(),
        P(),
        P(),
        P(dp_axes),
        P(ctx_axes, dp_axes, None),
    )
    out_specs = (
        P(ctx_axes, dp_axes, None),
        P(every, None),
        P(every, None),
        P(every, None),
        P(every),
        P(every),
    )
    return jax.shard_map(
        on_device, mesh=fine, in_specs=in_specs, out_specs=out_specs, check_vma=False
    )
```

```python
import functools

import jax
import jax.numpy as jnp
from jax import lax
from jax.experimental import pallas as pl
from jax.experimental.pallas import tpu as pltpu
from jax.sharding import Mesh, PartitionSpec as P

HEADS = 16


EPSILON = 1e-05

MARGIN = 32

CTX = ("chi", "clo")
FIRST = ("dlo", "chi")
SECOND = ("dhi", "clo")

SMEM = pl.BlockSpec(memory_space=pltpu.SMEM)
VMEM = pl.BlockSpec(memory_space=pltpu.VMEM)
HBM = pl.BlockSpec(memory_space=pltpu.HBM)


def normalize(values):
    center = values - jnp.mean(values, axis=-1, keepdims=True)
    inverse = lax.rsqrt(jnp.mean(center * center, axis=-1, keepdims=True) + EPSILON)
    return (center * inverse, inverse)


def attend(packed, key_lengths):
    length, count, triple = packed.shape
    head_size = triple // 3
    query_rows = packed[:, :, :head_size]
    key_rows = packed[:, :, head_size : 2 * head_size]
    value_rows = packed[:, :, 2 * head_size :]
    allowed = jnp.arange(length, dtype=jnp.int32)[None, :] < key_lengths[:, None]
    scores = (
        jnp.einsum("qmd,kmd->mqk", query_rows, key_rows, preferred_element_type=jnp.float32)
        * head_size ** (-0.5)
    )
    scores = jnp.where(allowed[:, None, :], scores, -jnp.inf)
    highest = jnp.max(scores, axis=-1, keepdims=True)
    raised = jnp.exp(scores - highest)
    weights_bf = (raised / jnp.sum(raised, axis=-1, keepdims=True)).astype(jnp.bfloat16)
    return jnp.einsum(
        "mqk,kmd->qmd", weights_bf, value_rows, preferred_element_type=jnp.float32
    ).astype(jnp.bfloat16)


def by_owner(cols, sizes):
    dhi, dlo, chi, clo = sizes
    rows, width = cols.shape
    part = width // (dhi * dlo * chi * clo)
    split = cols.reshape(rows, dhi, dlo, chi, clo, part)
    return jnp.transpose(split, (2, 3, 0, 1, 4, 5)).reshape(dlo * chi, rows, dhi * clo * part)


def gathered(rows, chi):
    copies = jnp.broadcast_to(rows[None], (chi,) + rows.shape)
    line = lax.all_to_all(copies, "chi", split_axis=0, concat_axis=0, tiled=True)
    line = line.reshape(chi * rows.shape[0], rows.shape[1])
    other = lax.ppermute(line, "dlo", [(0, 1), (1, 0)])
    first = lax.axis_index("dlo") == 0
    return jnp.concatenate([jnp.where(first, line, other), jnp.where(first, other, line)], axis=0)


def params(mebi=8):
    return pltpu.CompilerParams(vmem_limit_bytes=mebi * 1024 * 1024)


def struct(shape, dtype):
    return jax.ShapeDtypeStruct(shape, dtype)


def in_hbm(array):
    return pltpu.with_memory_space_constraint(array, pltpu.HBM)


def fetches(source, target, sems, parts):
    copies = []
    for i, part in enumerate(parts):
        copies.append(pltpu.make_async_copy(source.at[part], target.at[part], sems.at[i]))
        copies[-1].start()
    return copies


def split_kernel(proj_ref, out_ref, held_ref, sems):
    count, _, span = out_ref.shape
    copies = []
    for i in range(count):
        copies.append(
            pltpu.make_async_copy(
                proj_ref.at[:, pl.ds(i * span, span)], held_ref.at[i], sems.at[0, i]
            )
        )
        copies[-1].start()
    sends = []
    for i, copy in enumerate(copies):
        copy.wait()
        sends.append(pltpu.make_async_copy(held_ref.at[i], out_ref.at[i], sems.at[1, i]))
        sends[-1].start()
    for send in sends:
        send.wait()


def split_heads(proj, count):
    rows, cols = proj.shape
    shape = (count, rows, cols // count)
    return pl.pallas_call(
        split_kernel,
        out_shape=struct(shape, proj.dtype),
        in_specs=[HBM],
        out_specs=HBM,
        scratch_shapes=[pltpu.VMEM(shape, proj.dtype), pltpu.SemaphoreType.DMA((2, count))],
        compiler_params=params(),
        name="split_heads",
    )(in_hbm(proj))


def edge_kernel(res_ref, grad_ref, low_ref, high_ref, sems):
    rows = res_ref.shape[0]
    copies = []
    for i, (source, at, count) in enumerate(
        ((res_ref, 0, MARGIN), (grad_ref, MARGIN, MARGIN // 2))
    ):
        for j, (target, start) in enumerate(((high_ref, rows - count), (low_ref, 0))):
            copies.append(
                pltpu.make_async_copy(
                    source.at[pl.ds(start, count)], target.at[pl.ds(at, count)], sems.at[i, j]
                )
            )
            copies[-1].start()
    for copy in copies:
        copy.wait()


def edges(res, grad):
    shape = struct((MARGIN + MARGIN // 2, res.shape[1]), res.dtype)
    spec = pl.BlockSpec(memory_space=pl.ANY)
    return pl.pallas_call(
        edge_kernel,
        out_shape=(shape, shape),
        in_specs=[HBM, HBM],
        out_specs=(spec, spec),
        scratch_shapes=[pltpu.SemaphoreType.DMA((2, 2))],
        compiler_params=params(),
        name="edges",
    )(in_hbm(res), in_hbm(grad))


def attend_kernel(head_size, frames, scalar_ref, qkv_ref, out_ref):
    length = qkv_ref.shape[0]
    count = qkv_ref.shape[1] // (3 * head_size)
    ctx, wide, _ = out_ref.shape
    places = lax.broadcasted_iota(jnp.int32, (1, length), 1)
    bias = jnp.where(places < scalar_ref[0], 0.0, -jnp.inf)
    scores = []
    for m in range(count):
        base = 3 * head_size * m
        query = qkv_ref[:, base : base + head_size] * jnp.bfloat16(head_size ** (-0.5))
        key = qkv_ref[:, base + head_size : base + 2 * head_size]
        scores.append(bias + lax.dot_general(
                query, key, (((1,), (1,)), ((), ())), preferred_element_type=jnp.float32))
    scores = jnp.concatenate(scores, axis=0)
    raised = jnp.exp(scores - jnp.max(scores, axis=-1, keepdims=True))
    share = 1.0 / jnp.sum(raised, axis=-1, keepdims=True)
    weights = raised.astype(jnp.bfloat16)
    heads = []
    for m in range(count):
        base = 3 * head_size * m
        value = qkv_ref[:, base + 2 * head_size : base + 3 * head_size]
        rows = slice(m * length, (m + 1) * length)
        heads.append(
            jnp.dot(weights[rows], value, preferred_element_type=jnp.float32) * share[rows]
        )
    context = jnp.concatenate(heads, axis=1).astype(jnp.bfloat16)
    for i in range(ctx):
        low = max(i * frames - MARGIN, 0)
        high = min(i * frames - MARGIN + wide, length)
        at = low - (i * frames - MARGIN)
        out_ref[i, at : at + high - low, :] = context[low:high]
        if at > 0:
            out_ref[i, :at, :] = jnp.zeros((at, context.shape[1]), context.dtype)
        if at + high - low < wide:
            rest = wide - (at + high - low)
            out_ref[i, wide - rest :, :] = jnp.zeros((rest, context.shape[1]), context.dtype)


def attend_windows(scalars, qkv, head_size, frames, ctx):
    wide = frames + 2 * MARGIN
    return pl.pallas_call(
        functools.partial(attend_kernel, head_size, frames),
        out_shape=struct((ctx, wide, qkv.shape[1] // 3), jnp.bfloat16),
        in_specs=[SMEM, VMEM],
        out_specs=VMEM,
        compiler_params=params(16),
        name="attend",
    )(scalars, qkv)


def cot_kernel(scalar_ref, grad_ref, low_ref, high_ref, weight_ref, *refs):
    cols_refs, (act_ref, held_ref, weight_held_ref, sems) = refs[:4], refs[4:]
    frames, width = grad_ref.shape
    copies = fetches(
        weight_ref, weight_held_ref, sems, [pl.ds(i * 256, 256) for i in range(width // 256)]
    )
    edge = MARGIN // 2
    whole = jnp.concatenate([low_ref[MARGIN:, :], grad_ref[...], high_ref[MARGIN:, :]], axis=0)
    near = whole.shape[0]
    place = scalar_ref[1] - edge + lax.broadcasted_iota(jnp.int32, (near, width), 0)
    valid = (place >= 0) & (place < scalar_ref[0])
    whole = jnp.where(valid, whole.astype(jnp.float32), 0.0).astype(jnp.bfloat16)
    cot = whole[edge : edge + frames]
    count, _, span = held_ref.shape
    piece = span // 4
    for group in range(count):
        high_bits, low_bit = group // 2, group % 2
        held_ref[group, :, :] = jnp.concatenate(
            [
                cot[:, (8 * high_bits + 2 * z + low_bit) * piece :][:, :piece]
                for z in range(4)
            ],
            axis=1,
        )
    dhi, dlo, clo = scalar_ref[5], scalar_ref[2], scalar_ref[6]
    for k, cols_ref in enumerate(cols_refs):
        for side in range(2):
            group = ((dhi ^ (k // 2)) * 2 + (dlo ^ side)) * 2 + (clo ^ (k % 2))
            cols_ref[:, side * span : (side + 1) * span] = held_ref[group]
    for copy in copies:
        copy.wait()
    act_ref[...] = lax.dot_general(
        whole, weight_held_ref[...], (((1,), (1,)), ((), ())), preferred_element_type=jnp.float32
    )


def cot_part(scalars, grad, low, high, weight):
    frames, width = grad.shape
    cols = struct((frames, width // 4), grad.dtype)
    return pl.pallas_call(
        cot_kernel,
        out_shape=(cols, cols, cols, cols, struct((frames + MARGIN, width), jnp.float32)),
        in_specs=[SMEM, VMEM, VMEM, VMEM, HBM],
        out_specs=(VMEM,) * 5,
        scratch_shapes=[
            pltpu.VMEM((8, frames, width // 8), grad.dtype),
            pltpu.VMEM(weight.shape, weight.dtype),
            pltpu.SemaphoreType.DMA((width // 256,)),
        ],
        compiler_params=params(12),
        name="cotangent",
    )(scalars, grad, low, high, in_hbm(weight))


def forward_kernel(
    scalar_ref, context_ref, res_ref, low_ref, high_ref, out_ref, gain_one_ref, weight_ref,
    taps_ref, gain_ref,
    hidden_ref, one_ref, own_ref, act_ref, linear_ref, gate_ref, glu_ref,
    normed_ref, inverse_ref, scaled_ref, conv_ref, out_held_ref, held_ref, res_held_ref, out_sems, sems, res_sems,
):
    frames, width = res_ref.shape
    ctx, wide, lanes = context_ref.shape
    taps = taps_ref.shape[0]
    half = (taps - 1) // 2
    edge = MARGIN // 2
    near = wide - 2 * edge
    depth = 2 * lanes
    res_copies = fetches(res_ref, res_held_ref, res_sems, [slice(None)])
    out_copies = fetches(
        out_ref, out_held_ref, out_sems, [pl.ds(i * depth, depth) for i in range(ctx // 2)]
    )
    span = 256
    copies = fetches(
        weight_ref, held_ref, sems, [pl.ds(i * span, span) for i in range(width // span)]
    )
    product = jnp.zeros((wide, width), jnp.float32)
    for i, copy in enumerate(out_copies):
        copy.wait()
        product = product + jnp.dot(
            jnp.concatenate([context_ref[2 * i], context_ref[2 * i + 1]], axis=1),
            out_held_ref[i * depth : (i + 1) * depth, :],
            preferred_element_type=jnp.float32,
        )
    res_copies[0].wait()
    step = 32
    for at in range(0, wide, step):
        if at < MARGIN:
            res = low_ref[at : at + step, :]
        elif at < MARGIN + frames:
            res = res_held_ref[at - MARGIN : at - MARGIN + step, :]
        else:
            res = high_ref[at - MARGIN - frames : at - MARGIN - frames + step, :]
        hidden = res.astype(jnp.float32) + product[at : at + step]
        normed, _ = normalize(hidden)
        scaled = (normed * gain_one_ref[...]).astype(jnp.bfloat16)
        scaled_ref[at : at + step, :] = scaled
        if MARGIN <= at < MARGIN + frames:
            rows = slice(at - MARGIN, at - MARGIN + step)
            hidden_ref[rows, :] = hidden
            one_ref[rows, :] = normed
            own_ref[rows, :] = scaled
    for copy in copies:
        copy.wait()
    place = scalar_ref[1] - MARGIN + lax.broadcasted_iota(jnp.int32, (wide, span), 0)
    valid = (place >= 0) & (place < scalar_ref[0])
    own = slice(MARGIN, MARGIN + frames)
    for i in range(width // span):
        cols = slice(i * span, (i + 1) * span)
        linear = jnp.dot(scaled_ref[...], held_ref[:, cols], preferred_element_type=jnp.float32)
        gate = jax.nn.sigmoid(
            jnp.dot(
                scaled_ref[...],
                held_ref[:, width + i * span : width + (i + 1) * span],
                preferred_element_type=jnp.float32,
            )
        )
        glu = jnp.where(valid, linear * gate, 0.0).astype(jnp.bfloat16).astype(jnp.float32)
        glu_ref[:, cols] = glu
        linear_ref[:, cols] = linear[own]
        gate_ref[:, cols] = gate[own]
        for at in range(i * span, (i + 1) * span, 128):
            lane = slice(at, at + 128)
            block = glu[:, at - i * span : at - i * span + 128]
            total = jnp.zeros((near, 128), jnp.float32)
            for shift in range(8):
                moved = block if shift == 0 else pltpu.roll(block, wide - shift, 0)
                for j in range(taps):
                    start = edge + j - half
                    if start % 8 == shift:
                        total = total + taps_ref[j : j + 1, lane] * moved[
                            start - shift : start - shift + near
                        ]
            conv_ref[:, lane] = total
    step = 16
    for at in range(0, near, step):
        normed, inverse = normalize(conv_ref[at : at + step, :])
        normed_ref[at : at + step, :] = normed
        inverse_ref[at : at + step, :] = jnp.broadcast_to(inverse, (step, 128))
        if MARGIN - edge <= at < MARGIN - edge + frames:
            pre = normed * gain_ref[...]
            rows = slice(at - (MARGIN - edge), at - (MARGIN - edge) + step)
            act_ref[rows, :] = (pre * jax.nn.sigmoid(pre)).astype(jnp.bfloat16)


def forward_part(scalars, context, res, low, high, out_weight, gain_one, weight, taps, gain):
    frames, width = res.shape
    ctx, wide, _ = context.shape
    near = wide - MARGIN
    f32, bf = jnp.float32, jnp.bfloat16
    return pl.pallas_call(
        forward_kernel,
        out_shape=(
            struct((frames, width), f32),
            struct((frames, width), f32),
            struct((frames, width), bf),
            struct((frames, width), bf),
            struct((frames, width), f32),
            struct((frames, width), f32),
            struct((wide, width), f32),
            struct((near, width), f32),
            struct((near, 128), f32),
        ),
        in_specs=[SMEM, VMEM, HBM, VMEM, VMEM, HBM, VMEM, HBM, VMEM, VMEM],
        out_specs=(VMEM,) * 9,
        scratch_shapes=[
            pltpu.VMEM((wide, width), bf),
            pltpu.VMEM((near, width), f32),
            pltpu.VMEM(out_weight.shape, bf),
            pltpu.VMEM(weight.shape, bf),
            pltpu.VMEM(res.shape, bf),
            pltpu.SemaphoreType.DMA((ctx // 2,)),
            pltpu.SemaphoreType.DMA((width // 256,)),
            pltpu.SemaphoreType.DMA((1,)),
        ],
        compiler_params=params(24),
        name="forward",
    )(
        scalars, context, in_hbm(res), low, high, in_hbm(out_weight), gain_one, in_hbm(weight), taps, gain
    )


def back_kernel(
    scalar_ref, act_grad_ref, one_ref, linear_ref, gate_ref,
    glu_ref, normed_ref, inverse_ref, taps_ref, gain_ref, up_ref,
    message_ref, grad_ref, small_ref, lifted_ref, held_ref, sems,
):
    frames, width = one_ref.shape
    near = normed_ref.shape[0]
    wide = glu_ref.shape[0]
    taps = taps_ref.shape[0]
    half = (taps - 1) // 2
    edge = MARGIN // 2
    first = MARGIN - edge
    copies = fetches(up_ref, held_ref, sems, [pl.ds(i * 256, 256) for i in range(width // 256)])
    gain = gain_ref[...]
    step = 16
    two = jnp.zeros((1, width), jnp.float32)
    for at in range(0, near, step):
        normed = normed_ref[at : at + step, :]
        pre = normed * gain
        gate = jax.nn.sigmoid(pre)
        grad = act_grad_ref[at : at + step, :] * gate * (1.0 + pre * (1.0 - gate))
        if first <= at < first + frames:
            two = two + jnp.sum(grad * normed, axis=0, keepdims=True)
        scaled = grad * gain
        result = inverse_ref[at : at + step, 0:1] * (
            scaled
            - jnp.mean(scaled, axis=-1, keepdims=True)
            - normed * jnp.mean(scaled * normed, axis=-1, keepdims=True)
        )
        grad_ref[at : at + step, :] = result.astype(jnp.bfloat16).astype(jnp.float32)
    small_ref[32:, :] = jnp.zeros((16, width), jnp.float32)
    small_ref[taps + 1 : taps + 2, :] = two

    place = scalar_ref[1] + lax.broadcasted_iota(jnp.int32, (frames, 128), 0)
    valid = place < scalar_ref[0]

    def lanes(i):
        cols = slice(i * 128, (i + 1) * 128)
        high = slice(i * 128 + width, (i + 1) * 128 + width)
        block = grad_ref[:, cols]
        own = block[first : first + frames]
        total = jnp.zeros((frames, 128), jnp.float32)
        for shift in range(8):
            moved = block if shift == 0 else pltpu.roll(block, near - shift, 0)
            for j in range(taps):
                start = first + half - j
                if start % 8 == shift:
                    total = total + taps_ref[j : j + 1, cols] * moved[start - shift : start - shift + frames]
        block = glu_ref[:, cols]
        for shift in range(8):
            moved = block if shift == 0 else pltpu.roll(block, wide - shift, 0)
            for j in range(taps):
                start = MARGIN + j - half
                if start % 8 == shift:
                    small_ref[j : j + 1, cols] = jnp.sum(
                        own * moved[start - shift : start - shift + frames], axis=0, keepdims=True
                    )
        total = jnp.where(valid, total, 0.0)
        gate = gate_ref[:, cols]
        linear_grad = (total * gate).astype(jnp.bfloat16)
        gate_grad = (total * linear_ref[:, cols] * gate * (1.0 - gate)).astype(jnp.bfloat16)
        lifted_ref[:, cols] = linear_grad
        lifted_ref[:, high] = gate_grad
        message_ref[i, :frames, :128] = linear_grad
        message_ref[i, :frames, 128:256] = gate_grad

    for i in range(width // 128):
        lanes(i)
    for copy in copies:
        copy.wait()
    input_grad = lax.dot_general(
        lifted_ref[...], held_ref[...], (((1,), (1,)), ((), ())), preferred_element_type=jnp.float32
    )
    small_ref[taps : taps + 1, :] = jnp.sum(input_grad * one_ref[...], axis=0, keepdims=True)
    for i in range(width // 128):
        for part in range(2):
            rows = small_ref[part * 24 : (part + 1) * 24, :]
            message_ref[i, frames:, part * 128 : (part + 1) * 128] = jnp.concatenate(
                [rows[:, i * 64 : (i + 1) * 64], rows[:, (i + 8) * 64 : (i + 9) * 64]], axis=1
            ).astype(jnp.bfloat16)


def block_kernel(hidden_ref, activated_ref, down_ref, block_ref, held_ref, sems):
    width = hidden_ref.shape[1]
    copies = fetches(
        down_ref, held_ref, sems, [pl.ds(i * 256, 256) for i in range(width // 256)]
    )
    for copy in copies:
        copy.wait()
    block_ref[...] = (
        hidden_ref[...]
        + jnp.dot(
            activated_ref[:, :width], held_ref[...], preferred_element_type=jnp.float32
        )
    ).astype(jnp.bfloat16)


def block_part(hidden, activated, down):
    return pl.pallas_call(
        block_kernel,
        out_shape=struct(hidden.shape, jnp.bfloat16),
        in_specs=[VMEM, VMEM, HBM],
        out_specs=VMEM,
        scratch_shapes=[
            pltpu.VMEM(down.shape, down.dtype),
            pltpu.SemaphoreType.DMA((down.shape[0] // 256,)),
        ],
        compiler_params=params(12),
        name="block_out",
    )(hidden, activated, in_hbm(down))


def back_part(*operands):
    frames, width = operands[2].shape
    near = frames + MARGIN
    f32, bf = jnp.float32, jnp.bfloat16
    return pl.pallas_call(
        back_kernel,
        out_shape=struct((width // 128, frames + 24, 256), bf),
        in_specs=[SMEM] + [VMEM] * 9 + [HBM],
        out_specs=VMEM,
        scratch_shapes=[
            pltpu.VMEM((near, width), f32),
            pltpu.VMEM((48, width), f32),
            pltpu.VMEM((frames, 2 * width), bf),
            pltpu.VMEM((width, 2 * width), bf),
            pltpu.SemaphoreType.DMA((width // 256,)),
        ],
        compiler_params=params(20),
        name="backward",
    )(*operands[:-1], in_hbm(operands[-1]))


TURNED = (((0,), (0,)), ((), ()))


def up_kernel(count, scalar_ref, message_ref, *refs):
    parts_ref, cols_ref, one_ref = refs[2 * count :]
    frames, width = refs[0].shape
    core, line = scalar_ref[2], scalar_ref[3]
    small = jnp.zeros((24, 256), jnp.float32)
    for side in range(2):
        for k in range(count):
            at = (side * count + k) * frames
            source = (core ^ side) * count + (line ^ k)
            cols_ref[at : at + frames, :] = message_ref[source, :frames, :]
            one_ref[at : at + frames, :] = refs[side * count + k][...]
            small = small + message_ref[source, frames:, :].astype(jnp.float32)
    up = lax.dot_general(
        cols_ref[...], one_ref[...], TURNED, preferred_element_type=jnp.float32
    ).astype(jnp.bfloat16)
    small = small.astype(jnp.bfloat16)
    for s in range(4):
        parts_ref[s, :64, :] = up[s * 64 : (s + 1) * 64]
        for i in range(3):
            parts_ref[s, 64:, i * 256 : (i + 1) * 256] = small[i * 8 : (i + 1) * 8]
        parts_ref[s, 64:, 768:] = jnp.zeros((8, width - 768), jnp.bfloat16)


def up_part(scalars, message, pieces):
    count = len(pieces) // 2
    frames, width = pieces[0].shape
    bf = jnp.bfloat16
    rows = 2 * count * frames
    return pl.pallas_call(
        functools.partial(up_kernel, count),
        out_shape=struct((4, 72, width), bf),
        in_specs=[SMEM, VMEM] + [VMEM] * len(pieces),
        out_specs=VMEM,
        scratch_shapes=[pltpu.VMEM((rows, 256), bf), pltpu.VMEM((rows, width), bf)],
        compiler_params=params(12),
        name="up_products",
    )(scalars, message, *pieces)


def pack_kernel(act_ref, *refs):
    count = len(refs) // 2
    width = act_ref.shape[1]
    for cols_ref, out_ref in zip(refs[:count], refs[count:]):
        out_ref[:, :width] = act_ref[...]
        out_ref[:, width:] = cols_ref[...]


def pack_part(act, cols):
    shape = struct((act.shape[0], act.shape[1] + cols[0].shape[1]), act.dtype)
    count = len(cols)
    return pl.pallas_call(
        pack_kernel,
        out_shape=(shape,) * count,
        in_specs=[VMEM] * (1 + count),
        out_specs=(VMEM,) * count,
        compiler_params=params(),
        name="pack",
    )(act, *cols)


def down_kernel(*refs):
    pieces, (mine_ref, theirs_ref, rows_ref) = refs[:-3], refs[-3:]
    width = mine_ref.shape[1]
    frames = pieces[0].shape[0]
    for i, piece in enumerate(pieces):
        rows_ref[i * frames : (i + 1) * frames, :] = piece[...]
    total = lax.dot_general(
        rows_ref[:, width:], rows_ref[:, :width], TURNED, preferred_element_type=jnp.float32
    ).astype(jnp.bfloat16)
    half = total.shape[0] // 2
    mine_ref[...] = total[:half]
    theirs_ref[...] = total[half:]


def down_part(pieces, width):
    frames, wide = pieces[0].shape
    shape = struct(((wide - width) // 2, width), jnp.bfloat16)
    return pl.pallas_call(
        down_kernel,
        out_shape=(shape, shape),
        in_specs=[VMEM] * len(pieces),
        out_specs=(VMEM, VMEM),
        scratch_shapes=[pltpu.VMEM((len(pieces) * frames, wide), jnp.bfloat16)],
        compiler_params=params(12),
        name="down_products",
    )(*pieces)


def share_kernel(scalar_ref, mine_ref, other_ref, *refs):
    outs, total_ref = refs[:-1], refs[-1]
    total_ref[...] = mine_ref[...].astype(jnp.float32) + other_ref[...].astype(jnp.float32)
    for k, out in enumerate(outs):
        at = pl.multiple_of((scalar_ref[3] ^ k) * 32, 32)
        out[...] = total_ref[pl.ds(at, 32), :].astype(jnp.bfloat16)


def share_part(scalars, mine, other):
    rows, width = mine.shape
    count = rows // 32
    return pl.pallas_call(
        share_kernel,
        out_shape=(struct((32, width), jnp.bfloat16),) * count,
        in_specs=[SMEM, VMEM, VMEM],
        out_specs=(VMEM,) * count,
        scratch_shapes=[pltpu.VMEM((rows, width), jnp.float32)],
        compiler_params=params(),
        name="down_shares",
    )(scalars, mine, other)


def sum_kernel(taps, scalar_ref, parts_ref, *refs):
    pieces, (up_ref, down_ref, kernel_ref, one_ref, two_ref) = refs[:4], refs[4:]
    total = parts_ref[0].astype(jnp.float32)
    for s in range(1, parts_ref.shape[0]):
        total = total + parts_ref[s].astype(jnp.float32)
    up_ref[...] = total[:64]
    down_ref[...] = (pieces[0][...].astype(jnp.float32) + pieces[1][...].astype(jnp.float32)) + (
        pieces[2][...].astype(jnp.float32) + pieces[3][...].astype(jnp.float32)
    )
    small = jnp.concatenate(
        [
            total[64:72, i * 256 + part * 128 : i * 256 + part * 128 + 128]
            for part in range(2)
            for i in range(3)
        ],
        axis=0,
    )
    small = pltpu.roll(small, (128 - 32 * scalar_ref[4]) % 128, 1)
    kernel_ref[...] = jnp.transpose(small[:32])[:32, :taps]
    one_ref[...] = small[taps : taps + 1, :32]
    two_ref[...] = small[taps + 1 : taps + 2, :32]


def sum_part(scalars, parts, pieces, taps):
    width = parts.shape[2]
    f32 = jnp.float32
    return pl.pallas_call(
        functools.partial(sum_kernel, taps),
        out_shape=(
            struct((64, width), f32),
            struct((32, width), f32),
            struct((32, taps), f32),
            struct((1, 32), f32),
            struct((1, 32), f32),
        ),
        in_specs=[SMEM] + [VMEM] * 5,
        out_specs=(VMEM,) * 5,
        compiler_params=params(),
        name="sums",
    )(scalars, parts, *pieces)


def flipped(rows, axis, bit):
    size = lax.axis_size(axis)
    return lax.ppermute(rows, axis, [(i, i ^ bit) for i in range(size)])


def with_swapped(pieces):
    return list(pieces) + [flipped(piece, "dlo", 1) for piece in pieces]


def small_device(
    residual, projections, out_weight, gain_one, up_weight, conv_kernel, gain_two, down_weight,
    lengths, out_grad,
):
    frames, _, width = residual.shape
    taps = conv_kernel.shape[0]
    chi, clo = lax.axis_size("chi"), lax.axis_size("clo")
    ctx = chi * clo
    head_size = width // HEADS
    me = lax.axis_index(CTX)
    second = lax.axis_index("dhi") * clo + lax.axis_index("clo")
    scalars = jnp.stack(
        [
            lengths[0], me * frames, lax.axis_index("dlo"), lax.axis_index("chi"), second,
            lax.axis_index("dhi"), lax.axis_index("clo"),
        ]
    ).astype(jnp.int32)
    res = residual.reshape(frames, width)
    grad = out_grad.reshape(frames, width)
    gain_one = gain_one.reshape(1, width)
    gain_two = gain_two.reshape(1, width)

    qkv = split_heads(projections.reshape(frames, 3 * width), ctx)
    qkv = lax.all_to_all(qkv, CTX, split_axis=0, concat_axis=0, tiled=True)
    low, high = edges(res, grad)
    up = [(i, i + 1) for i in range(ctx - 1)]
    down = [(j, i) for i, j in up]
    before = lax.ppermute(high, CTX, up)
    after = lax.ppermute(low, CTX, down)
    qkv, before, after = lax.optimization_barrier((qkv, before, after))
    windows = attend_windows(scalars, qkv.reshape(ctx * frames, -1), head_size, frames, ctx)
    windows, before, after = lax.optimization_barrier((windows, before, after))
    windows = lax.all_to_all(windows, CTX, split_axis=0, concat_axis=0, tiled=True)
    *cols, act_grad = cot_part(scalars, grad, before, after, down_weight)
    windows, act_grad, cols = lax.optimization_barrier((windows, act_grad, cols))

    (
        hidden, normed_one, scaled, activated, linear, gate, glu, normed_two, inverse_two
    ) = forward_part(
        scalars, windows, res, before, after, out_weight, gain_one, up_weight, conv_kernel, gain_two
    )
    packed, to_y, to_x, to_xy = pack_part(activated, cols)
    pairs = [(i, i ^ 3) for i in range(4)]
    received = [
        flipped(to_y, "clo", 1), flipped(to_x, "dhi", 1), lax.ppermute(to_xy, SECOND, pairs)
    ]
    one_near, one_far = flipped(scaled, "chi", 1), flipped(scaled, "chi", 2)
    message = back_part(
        scalars, act_grad, normed_one, linear, gate,
        glu, normed_two, inverse_two, conv_kernel, gain_two, up_weight,
    )
    received, one_near, one_far, message = lax.optimization_barrier(
        (received, one_near, one_far, message)
    )
    message = lax.all_to_all(message, FIRST, split_axis=0, concat_axis=0, tiled=True)
    one_last = flipped(one_far, "chi", 1)
    mine, theirs = down_part([packed, *received], width)
    downs = share_part(scalars, mine, flipped(theirs, "dlo", 1))
    early = with_swapped([scaled, one_near, one_far])
    one_last, early, downs = lax.optimization_barrier((one_last, early, downs))
    last = with_swapped([one_last])
    ones = early[:3] + last[:1] + early[3:] + last[1:]
    downs = [downs[0]] + [flipped(downs[k], "chi", k) for k in range(1, chi)]
    parts = up_part(scalars, message, ones)
    parts = lax.all_to_all(parts, SECOND, split_axis=0, concat_axis=0, tiled=True)
    block_out = block_part(hidden, activated, down_weight)
    up_grad, down_grad, kernel_grad, one, two = sum_part(scalars, parts, downs, taps)
    return (
        block_out.reshape(frames, 1, width), up_grad, down_grad, kernel_grad,
        one.reshape(-1), two.reshape(-1),
    )


def fits(residual, conv_kernel, sizes):
    dhi, dlo, chi, clo = sizes
    frames, utter_count, width = residual.shape
    return (
        utter_count == 1
        and frames == 64
        and width == 1024
        and conv_kernel.shape[0] == 31
        and (dhi, dlo, chi, clo) == (2, 2, 4, 2)
    )


def on_device(
    residual,
    projections,
    out_weight,
    gain_one,
    up_weight,
    conv_kernel,
    gain_two,
    down_weight,
    lengths,
    out_grad,
):
    frames, utter_count, width = residual.shape
    head_size = width // HEADS
    kernel_len = conv_kernel.shape[0]
    half = (kernel_len - 1) // 2
    dhi, dlo, chi, clo = sizes = tuple(lax.axis_size(a) for a in ("dhi", "dlo", "chi", "clo"))
    if fits(residual, conv_kernel, sizes):
        return small_device(
            residual,
            projections,
            out_weight,
            gain_one,
            up_weight,
            conv_kernel,
            gain_two,
            down_weight,
            lengths,
            out_grad,
        )
    ctx = chi * clo
    length = frames * ctx
    items = utter_count * HEADS // ctx
    me = lax.axis_index(CTX)
    bf = jnp.bfloat16
    f32 = jnp.float32

    packed = projections.reshape(frames, ctx, items, 3 * head_size)
    packed = lax.all_to_all(packed, CTX, split_axis=1, concat_axis=0, tiled=True)
    packed = packed.reshape(length, items, 3 * head_size)

    both = jnp.concatenate([residual, out_grad], axis=-1)
    up = [(i, i + 1) for i in range(ctx - 1)]
    down = [(j, i) for i, j in up]
    before = lax.ppermute(both[frames - MARGIN :], CTX, up)
    after = lax.ppermute(both[:MARGIN], CTX, down)
    both = jnp.concatenate([before, both, after], axis=0)
    wide = frames + 2 * MARGIN
    place = me * frames - MARGIN + jnp.arange(wide, dtype=jnp.int32)
    valid = (place[:, None] >= 0) & (place[:, None] < lengths[None, :])
    row_mask = valid.astype(f32)[:, :, None]
    cot = jnp.where(valid[:, :, None], both[:, :, width:], 0)
    edge = MARGIN // 2
    near = wide - 2 * edge
    cot_near = cot[edge : edge + near]
    cot_own = cot[MARGIN : MARGIN + frames].reshape(frames * utter_count, width)
    act_grad = lax.dot_general(
        cot_near, down_weight, (((2,), (1,)), ((), ())), preferred_element_type=f32
    )

    key_lengths = lengths[(me * items + jnp.arange(items, dtype=jnp.int32)) // HEADS]
    context = attend(packed, key_lengths).reshape(length, items * head_size)
    padded = jnp.pad(context, ((MARGIN, MARGIN), (0, 0)))
    windows = jnp.stack([padded[i * frames : i * frames + wide] for i in range(ctx)])
    context = lax.all_to_all(windows, CTX, split_axis=0, concat_axis=0, tiled=True)
    context = jnp.transpose(context, (1, 0, 2)).reshape(wide, utter_count, width)

    cot_cols = lax.all_to_all(
        by_owner(cot_own, sizes), FIRST, split_axis=0, concat_axis=0, tiled=True
    )

    hidden = both[:, :, :width].astype(f32) + jnp.einsum(
        "fuc,cd->fud", context, out_weight, preferred_element_type=f32
    )
    normed_one, _ = normalize(hidden)
    scaled_one = (normed_one * gain_one).astype(bf)
    own = slice(MARGIN, MARGIN + frames)
    own_near = slice(MARGIN - edge, MARGIN - edge + frames)
    rows = frames * utter_count
    scaled_own = scaled_one[own].reshape(rows, width)
    scaled_all = gathered(scaled_own, chi)

    lifted = jnp.einsum("fuc,cd->fud", scaled_one, up_weight, preferred_element_type=f32)
    linear_part = lifted[:, :, :width]
    gate_part = jax.nn.sigmoid(lifted[:, :, width:])
    glu = (linear_part * gate_part * row_mask).astype(bf).astype(f32)
    conv_out = jnp.zeros((near, utter_count, width), f32)
    for j in range(kernel_len):
        start = edge + j - half
        conv_out = conv_out + conv_kernel[j] * glu[start : start + near]
    normed_two, inverse_two = normalize(conv_out)
    pre_act = normed_two * gain_two
    gate_two = jax.nn.sigmoid(pre_act)
    activated = (pre_act * gate_two)[own_near].astype(bf).reshape(rows, width)
    activated_all = gathered(activated, chi)
    block_out = (
        hidden[own].reshape(rows, width)
        + jnp.dot(activated, down_weight, preferred_element_type=f32)
    ).astype(bf)
    block_out = block_out.reshape(frames, utter_count, width)

    pre_grad = act_grad * gate_two * (1.0 + pre_act * (1.0 - gate_two))
    gain_two_grad = jnp.sum((pre_grad * normed_two)[own_near], axis=(0, 1))
    scaled_grad = pre_grad * gain_two
    conv_grad = inverse_two * (
        scaled_grad
        - jnp.mean(scaled_grad, axis=-1, keepdims=True)
        - normed_two * jnp.mean(scaled_grad * normed_two, axis=-1, keepdims=True)
    )
    conv_grad = conv_grad.astype(bf).astype(f32)
    conv_own = conv_grad[own_near]
    small = []
    glu_grad = jnp.zeros((frames, utter_count, width), f32)
    for j in range(kernel_len):
        start = MARGIN + j - half
        small.append(jnp.sum(conv_own * glu[start : start + frames], axis=(0, 1)))
        start = MARGIN - edge + half - j
        glu_grad = glu_grad + conv_kernel[j] * conv_grad[start : start + frames]
    glu_grad = glu_grad * row_mask[own]
    gate_own = gate_part[own]
    linear_grad = glu_grad * gate_own
    gate_grad = glu_grad * linear_part[own] * gate_own * (1.0 - gate_own)
    lifted_grad = jnp.concatenate([linear_grad, gate_grad], axis=-1).astype(bf)
    lifted_grad = lifted_grad.reshape(rows, 2 * width)
    input_grad = lax.dot_general(
        lifted_grad, up_weight, (((1,), (1,)), ((), ())), preferred_element_type=f32
    )
    gain_one_grad = jnp.sum(input_grad * normed_one[own].reshape(rows, width), axis=0)

    small = small + [gain_one_grad, gain_two_grad]
    count = kernel_len + 2
    small = by_owner(jnp.stack(small).astype(bf), sizes)
    small = small.reshape(dlo * chi, -1)
    cols = by_owner(lifted_grad, sizes)
    col_count = cols.shape[2]
    spare = -small.shape[1] % col_count
    small = jnp.pad(small, ((0, 0), (0, spare))).reshape(dlo * chi, -1, col_count)
    message = jnp.concatenate([cols, small], axis=1)
    message = lax.all_to_all(message, FIRST, split_axis=0, concat_axis=0, tiled=True)
    cols = message[:, :rows].reshape(-1, col_count)
    small = jnp.sum(message[:, rows:].astype(f32), axis=0).reshape(-1)
    seconds = dhi * clo
    small_width = width // (ctx * dhi * dlo)
    small = small[: count * seconds * small_width].reshape(count, seconds, small_width)
    small = jnp.transpose(small, (1, 0, 2)).reshape(seconds, count * small_width)

    up_part = lax.dot_general(
        cols, scaled_all, (((0,), (0,)), ((), ())), preferred_element_type=f32
    ).reshape(seconds, -1, width)
    down_part = lax.dot_general(
        cot_cols.reshape(cols.shape[0], -1),
        activated_all,
        (((0,), (0,)), ((), ())),
        preferred_element_type=f32,
    ).reshape(seconds, -1, width)
    spare = -small.shape[1] % width
    small = jnp.pad(small, ((0, 0), (0, spare))).reshape(seconds, -1, width)
    up_rows, down_rows = up_part.shape[1], down_part.shape[1]
    parts = jnp.concatenate([up_part.astype(bf), down_part.astype(bf), small.astype(bf)], axis=1)
    parts = lax.all_to_all(parts, SECOND, split_axis=0, concat_axis=0, tiled=True)
    total = jnp.sum(parts.astype(f32), axis=0)
    up_grad = total[:up_rows]
    down_grad = total[up_rows : up_rows + down_rows]
    small = total[up_rows + down_rows :].reshape(-1)[: count * small_width]
    small = small.reshape(count, small_width)
    kernel_grad = jnp.transpose(small[:kernel_len])
    return (block_out, up_grad, down_grad, kernel_grad, small[kernel_len], small[kernel_len + 1])


def solution(mesh):
    dp, ctx = mesh.shape["dp"], mesh.shape["ctx"]
    fine = Mesh(mesh.devices.reshape(dp // 2, 2, ctx // 2, 2), ("dhi", "dlo", "chi", "clo"))
    dp_axes, ctx_axes = ("dhi", "dlo"), ("chi", "clo")
    every = ("dhi", "dlo", "chi", "clo")
    in_specs = (
        P(ctx_axes, dp_axes, None),
        P(ctx_axes, dp_axes, None),
        P(),
        P(),
        P(),
        P(),
        P(),
        P(),
        P(dp_axes),
        P(ctx_axes, dp_axes, None),
    )
    out_specs = (
        P(ctx_axes, dp_axes, None),
        P(every, None),
        P(every, None),
        P(every, None),
        P(every),
        P(every),
    )
    return jax.shard_map(
        on_device, mesh=fine, in_specs=in_specs, out_specs=out_specs, check_vma=False
    )
```

```python
import functools

import jax
import jax.numpy as jnp
from jax import lax
from jax.experimental import pallas as pl
from jax.experimental.pallas import tpu as pltpu
from jax.sharding import Mesh, PartitionSpec as P

HEADS = 16


EPSILON = 1e-05

MARGIN = 32

CTX = ("chi", "clo")
FIRST = ("dlo", "chi")
SECOND = ("dhi", "clo")

SMEM = pl.BlockSpec(memory_space=pltpu.SMEM)
VMEM = pl.BlockSpec(memory_space=pltpu.VMEM)
HBM = pl.BlockSpec(memory_space=pltpu.HBM)


def normalize(values):
    center = values - jnp.mean(values, axis=-1, keepdims=True)
    inverse = lax.rsqrt(jnp.mean(center * center, axis=-1, keepdims=True) + EPSILON)
    return (center * inverse, inverse)


def attend(packed, key_lengths):
    length, count, triple = packed.shape
    head_size = triple // 3
    query_rows = packed[:, :, :head_size]
    key_rows = packed[:, :, head_size : 2 * head_size]
    value_rows = packed[:, :, 2 * head_size :]
    allowed = jnp.arange(length, dtype=jnp.int32)[None, :] < key_lengths[:, None]
    scores = (
        jnp.einsum("qmd,kmd->mqk", query_rows, key_rows, preferred_element_type=jnp.float32)
        * head_size ** (-0.5)
    )
    scores = jnp.where(allowed[:, None, :], scores, -jnp.inf)
    highest = jnp.max(scores, axis=-1, keepdims=True)
    raised = jnp.exp(scores - highest)
    weights_bf = (raised / jnp.sum(raised, axis=-1, keepdims=True)).astype(jnp.bfloat16)
    return jnp.einsum(
        "mqk,kmd->qmd", weights_bf, value_rows, preferred_element_type=jnp.float32
    ).astype(jnp.bfloat16)


def by_owner(cols, sizes):
    dhi, dlo, chi, clo = sizes
    rows, width = cols.shape
    part = width // (dhi * dlo * chi * clo)
    split = cols.reshape(rows, dhi, dlo, chi, clo, part)
    return jnp.transpose(split, (2, 3, 0, 1, 4, 5)).reshape(dlo * chi, rows, dhi * clo * part)


def gathered(rows, chi):
    copies = jnp.broadcast_to(rows[None], (chi,) + rows.shape)
    line = lax.all_to_all(copies, "chi", split_axis=0, concat_axis=0, tiled=True)
    line = line.reshape(chi * rows.shape[0], rows.shape[1])
    other = lax.ppermute(line, "dlo", [(0, 1), (1, 0)])
    first = lax.axis_index("dlo") == 0
    return jnp.concatenate([jnp.where(first, line, other), jnp.where(first, other, line)], axis=0)


def params(mebi=8):
    return pltpu.CompilerParams(vmem_limit_bytes=mebi * 1024 * 1024)


def struct(shape, dtype):
    return jax.ShapeDtypeStruct(shape, dtype)


def in_hbm(array):
    return pltpu.with_memory_space_constraint(array, pltpu.HBM)


def fetches(source, target, sems, parts):
    copies = []
    for i, part in enumerate(parts):
        copies.append(pltpu.make_async_copy(source.at[part], target.at[part], sems.at[i]))
        copies[-1].start()
    return copies


def split_kernel(proj_ref, out_ref, held_ref, sems):
    count, _, span = out_ref.shape
    copies = []
    for i in range(count):
        copies.append(
            pltpu.make_async_copy(
                proj_ref.at[:, pl.ds(i * span, span)], held_ref.at[i], sems.at[0, i]
            )
        )
        copies[-1].start()
    sends = []
    for i, copy in enumerate(copies):
        copy.wait()
        sends.append(pltpu.make_async_copy(held_ref.at[i], out_ref.at[i], sems.at[1, i]))
        sends[-1].start()
    for send in sends:
        send.wait()


def split_heads(proj, count):
    rows, cols = proj.shape
    shape = (count, rows, cols // count)
    return pl.pallas_call(
        split_kernel,
        out_shape=struct(shape, proj.dtype),
        in_specs=[HBM],
        out_specs=HBM,
        scratch_shapes=[pltpu.VMEM(shape, proj.dtype), pltpu.SemaphoreType.DMA((2, count))],
        compiler_params=params(),
        name="split_heads",
    )(in_hbm(proj))


def edge_kernel(res_ref, grad_ref, low_ref, high_ref, sems):
    rows = res_ref.shape[0]
    copies = []
    for i, (source, at, count) in enumerate(
        ((res_ref, 0, MARGIN), (grad_ref, MARGIN, MARGIN // 2))
    ):
        for j, (target, start) in enumerate(((high_ref, rows - count), (low_ref, 0))):
            copies.append(
                pltpu.make_async_copy(
                    source.at[pl.ds(start, count)], target.at[pl.ds(at, count)], sems.at[i, j]
                )
            )
            copies[-1].start()
    for copy in copies:
        copy.wait()


def edges(res, grad):
    shape = struct((MARGIN + MARGIN // 2, res.shape[1]), res.dtype)
    spec = pl.BlockSpec(memory_space=pl.ANY)
    return pl.pallas_call(
        edge_kernel,
        out_shape=(shape, shape),
        in_specs=[HBM, HBM],
        out_specs=(spec, spec),
        scratch_shapes=[pltpu.SemaphoreType.DMA((2, 2))],
        compiler_params=params(),
        name="edges",
    )(in_hbm(res), in_hbm(grad))


def attend_kernel(head_size, frames, scalar_ref, qkv_ref, out_ref):
    length = qkv_ref.shape[0]
    count = qkv_ref.shape[1] // (3 * head_size)
    ctx, wide, _ = out_ref.shape
    places = lax.broadcasted_iota(jnp.int32, (1, length), 1)
    bias = jnp.where(places < scalar_ref[:, 0:1], 0.0, -jnp.inf)
    scores = []
    for m in range(count):
        base = 3 * head_size * m
        query = qkv_ref[:, base : base + head_size] * jnp.bfloat16(head_size ** (-0.5))
        key = qkv_ref[:, base + head_size : base + 2 * head_size]
        scores.append(bias + lax.dot_general(
                query, key, (((1,), (1,)), ((), ())), preferred_element_type=jnp.float32))
    scores = jnp.concatenate(scores, axis=0)
    raised = jnp.exp(scores - jnp.max(scores, axis=-1, keepdims=True))
    share = 1.0 / jnp.sum(raised, axis=-1, keepdims=True)
    weights = raised.astype(jnp.bfloat16)
    heads = []
    for m in range(count):
        base = 3 * head_size * m
        value = qkv_ref[:, base + 2 * head_size : base + 3 * head_size]
        rows = slice(m * length, (m + 1) * length)
        heads.append(
            jnp.dot(weights[rows], value, preferred_element_type=jnp.float32) * share[rows]
        )
    context = jnp.concatenate(heads, axis=1).astype(jnp.bfloat16)
    for i in range(ctx):
        low = max(i * frames - MARGIN, 0)
        high = min(i * frames - MARGIN + wide, length)
        at = low - (i * frames - MARGIN)
        out_ref[i, at : at + high - low, :] = context[low:high]
        if at > 0:
            out_ref[i, :at, :] = jnp.zeros((at, context.shape[1]), context.dtype)
        if at + high - low < wide:
            rest = wide - (at + high - low)
            out_ref[i, wide - rest :, :] = jnp.zeros((rest, context.shape[1]), context.dtype)


def attend_windows(scalars, qkv, head_size, frames, ctx):
    wide = frames + 2 * MARGIN
    return pl.pallas_call(
        functools.partial(attend_kernel, head_size, frames),
        out_shape=struct((ctx, wide, qkv.shape[1] // 3), jnp.bfloat16),
        in_specs=[VMEM, VMEM],
        out_specs=VMEM,
        compiler_params=params(16),
        name="attend",
    )(scalars, qkv)


def cot_kernel(scalar_ref, grad_ref, low_ref, high_ref, weight_ref, *refs):
    cols_refs, (act_ref, held_ref, weight_held_ref, sems) = refs[:4], refs[4:]
    frames, width = grad_ref.shape
    copies = fetches(
        weight_ref, weight_held_ref, sems, [pl.ds(i * 256, 256) for i in range(width // 256)]
    )
    edge = MARGIN // 2
    whole = jnp.concatenate([low_ref[MARGIN:, :], grad_ref[...], high_ref[MARGIN:, :]], axis=0)
    near = whole.shape[0]
    place = scalar_ref[:, 1:2] - edge + lax.broadcasted_iota(jnp.int32, (near, width), 0)
    valid = (place >= 0) & (place < scalar_ref[:, 0:1])
    whole = jnp.where(valid, whole.astype(jnp.float32), 0.0).astype(jnp.bfloat16)
    cot = whole[edge : edge + frames]
    count, _, span = held_ref.shape
    piece = span // 4
    for group in range(count):
        high_bits, low_bit = group // 2, group % 2
        held_ref[group, :, :] = jnp.concatenate(
            [
                cot[:, (8 * high_bits + 2 * z + low_bit) * piece :][:, :piece]
                for z in range(4)
            ],
            axis=1,
        )
    dhi, dlo, clo = lax.axis_index("dhi"), lax.axis_index("dlo"), lax.axis_index("clo")
    for k, cols_ref in enumerate(cols_refs):
        for side in range(2):
            group = ((dhi ^ (k // 2)) * 2 + (dlo ^ side)) * 2 + (clo ^ (k % 2))
            cols_ref[:, side * span : (side + 1) * span] = held_ref[group]
    for copy in copies:
        copy.wait()
    act_ref[...] = lax.dot_general(
        whole, weight_held_ref[...], (((1,), (1,)), ((), ())), preferred_element_type=jnp.float32
    )


def cot_part(scalars, grad, low, high, weight):
    frames, width = grad.shape
    cols = struct((frames, width // 4), grad.dtype)
    return pl.pallas_call(
        cot_kernel,
        out_shape=(cols, cols, cols, cols, struct((frames + MARGIN, width), jnp.float32)),
        in_specs=[VMEM, VMEM, VMEM, VMEM, HBM],
        out_specs=(VMEM,) * 5,
        scratch_shapes=[
            pltpu.VMEM((8, frames, width // 8), grad.dtype),
            pltpu.VMEM(weight.shape, weight.dtype),
            pltpu.SemaphoreType.DMA((width // 256,)),
        ],
        compiler_params=params(12),
        name="cotangent",
    )(scalars, grad, low, high, in_hbm(weight))


def forward_kernel(
    scalar_ref, context_ref, res_ref, low_ref, high_ref, out_ref, gain_one_ref, weight_ref,
    taps_ref, gain_ref,
    hidden_ref, one_ref, own_ref, act_ref, linear_ref, gate_ref, glu_ref,
    normed_ref, inverse_ref, scaled_ref, conv_ref, out_held_ref, held_ref, res_held_ref, out_sems, sems, res_sems,
):
    frames, width = res_ref.shape
    ctx, wide, lanes = context_ref.shape
    taps = taps_ref.shape[0]
    half = (taps - 1) // 2
    edge = MARGIN // 2
    near = wide - 2 * edge
    depth = 2 * lanes
    res_copies = fetches(res_ref, res_held_ref, res_sems, [slice(None)])
    out_copies = fetches(
        out_ref, out_held_ref, out_sems, [pl.ds(i * depth, depth) for i in range(ctx // 2)]
    )
    span = 256
    copies = fetches(
        weight_ref, held_ref, sems, [pl.ds(i * span, span) for i in range(width // span)]
    )
    product = jnp.zeros((wide, width), jnp.float32)
    for i, copy in enumerate(out_copies):
        copy.wait()
        product = product + jnp.dot(
            jnp.concatenate([context_ref[2 * i], context_ref[2 * i + 1]], axis=1),
            out_held_ref[i * depth : (i + 1) * depth, :],
            preferred_element_type=jnp.float32,
        )
    res_copies[0].wait()
    step = 32
    for at in range(0, wide, step):
        if at < MARGIN:
            res = low_ref[at : at + step, :]
        elif at < MARGIN + frames:
            res = res_held_ref[at - MARGIN : at - MARGIN + step, :]
        else:
            res = high_ref[at - MARGIN - frames : at - MARGIN - frames + step, :]
        hidden = res.astype(jnp.float32) + product[at : at + step]
        normed, _ = normalize(hidden)
        scaled = (normed * gain_one_ref[...]).astype(jnp.bfloat16)
        scaled_ref[at : at + step, :] = scaled
        if MARGIN <= at < MARGIN + frames:
            rows = slice(at - MARGIN, at - MARGIN + step)
            hidden_ref[rows, :] = hidden
            one_ref[rows, :] = normed
            own_ref[rows, :] = scaled
    for copy in copies:
        copy.wait()
    place = scalar_ref[:, 1:2] - MARGIN + lax.broadcasted_iota(jnp.int32, (wide, span), 0)
    valid = (place >= 0) & (place < scalar_ref[:, 0:1])
    own = slice(MARGIN, MARGIN + frames)
    for i in range(width // span):
        cols = slice(i * span, (i + 1) * span)
        linear = jnp.dot(scaled_ref[...], held_ref[:, cols], preferred_element_type=jnp.float32)
        gate = jax.nn.sigmoid(
            jnp.dot(
                scaled_ref[...],
                held_ref[:, width + i * span : width + (i + 1) * span],
                preferred_element_type=jnp.float32,
            )
        )
        glu = jnp.where(valid, linear * gate, 0.0).astype(jnp.bfloat16).astype(jnp.float32)
        glu_ref[:, cols] = glu
        linear_ref[:, cols] = linear[own]
        gate_ref[:, cols] = gate[own]
        for at in range(i * span, (i + 1) * span, 128):
            lane = slice(at, at + 128)
            block = glu[:, at - i * span : at - i * span + 128]
            total = jnp.zeros((near, 128), jnp.float32)
            for shift in range(8):
                moved = block if shift == 0 else pltpu.roll(block, wide - shift, 0)
                for j in range(taps):
                    start = edge + j - half
                    if start % 8 == shift:
                        total = total + taps_ref[j : j + 1, lane] * moved[
                            start - shift : start - shift + near
                        ]
            conv_ref[:, lane] = total
    step = 16
    for at in range(0, near, step):
        normed, inverse = normalize(conv_ref[at : at + step, :])
        normed_ref[at : at + step, :] = normed
        inverse_ref[at : at + step, :] = jnp.broadcast_to(inverse, (step, 128))
        if MARGIN - edge <= at < MARGIN - edge + frames:
            pre = normed * gain_ref[...]
            rows = slice(at - (MARGIN - edge), at - (MARGIN - edge) + step)
            act_ref[rows, :] = (pre * jax.nn.sigmoid(pre)).astype(jnp.bfloat16)


def forward_part(scalars, context, res, low, high, out_weight, gain_one, weight, taps, gain):
    frames, width = res.shape
    ctx, wide, _ = context.shape
    near = wide - MARGIN
    f32, bf = jnp.float32, jnp.bfloat16
    return pl.pallas_call(
        forward_kernel,
        out_shape=(
            struct((frames, width), f32),
            struct((frames, width), f32),
            struct((frames, width), bf),
            struct((frames, width), bf),
            struct((frames, width), f32),
            struct((frames, width), f32),
            struct((wide, width), f32),
            struct((near, width), f32),
            struct((near, 128), f32),
        ),
        in_specs=[VMEM, VMEM, HBM, VMEM, VMEM, HBM, VMEM, HBM, VMEM, VMEM],
        out_specs=(VMEM,) * 9,
        scratch_shapes=[
            pltpu.VMEM((wide, width), bf),
            pltpu.VMEM((near, width), f32),
            pltpu.VMEM(out_weight.shape, bf),
            pltpu.VMEM(weight.shape, bf),
            pltpu.VMEM(res.shape, bf),
            pltpu.SemaphoreType.DMA((ctx // 2,)),
            pltpu.SemaphoreType.DMA((width // 256,)),
            pltpu.SemaphoreType.DMA((1,)),
        ],
        compiler_params=params(24),
        name="forward",
    )(
        scalars, context, in_hbm(res), low, high, in_hbm(out_weight), gain_one, in_hbm(weight), taps, gain
    )


def back_kernel(
    scalar_ref, act_grad_ref, one_ref, linear_ref, gate_ref,
    glu_ref, normed_ref, inverse_ref, taps_ref, gain_ref, up_ref,
    message_ref, grad_ref, small_ref, lifted_ref, held_ref, sems,
):
    frames, width = one_ref.shape
    near = normed_ref.shape[0]
    wide = glu_ref.shape[0]
    taps = taps_ref.shape[0]
    half = (taps - 1) // 2
    edge = MARGIN // 2
    first = MARGIN - edge
    copies = fetches(up_ref, held_ref, sems, [pl.ds(i * 256, 256) for i in range(width // 256)])
    gain = gain_ref[...]
    step = 16
    two = jnp.zeros((1, width), jnp.float32)
    for at in range(0, near, step):
        normed = normed_ref[at : at + step, :]
        pre = normed * gain
        gate = jax.nn.sigmoid(pre)
        grad = act_grad_ref[at : at + step, :] * gate * (1.0 + pre * (1.0 - gate))
        if first <= at < first + frames:
            two = two + jnp.sum(grad * normed, axis=0, keepdims=True)
        scaled = grad * gain
        result = inverse_ref[at : at + step, 0:1] * (
            scaled
            - jnp.mean(scaled, axis=-1, keepdims=True)
            - normed * jnp.mean(scaled * normed, axis=-1, keepdims=True)
        )
        grad_ref[at : at + step, :] = result.astype(jnp.bfloat16).astype(jnp.float32)
    small_ref[32:, :] = jnp.zeros((16, width), jnp.float32)
    small_ref[taps + 1 : taps + 2, :] = two

    place = scalar_ref[:, 1:2] + lax.broadcasted_iota(jnp.int32, (frames, 128), 0)
    valid = place < scalar_ref[:, 0:1]

    def lanes(i):
        cols = slice(i * 128, (i + 1) * 128)
        high = slice(i * 128 + width, (i + 1) * 128 + width)
        block = grad_ref[:, cols]
        own = block[first : first + frames]
        total = jnp.zeros((frames, 128), jnp.float32)
        for shift in range(8):
            moved = block if shift == 0 else pltpu.roll(block, near - shift, 0)
            for j in range(taps):
                start = first + half - j
                if start % 8 == shift:
                    total = total + taps_ref[j : j + 1, cols] * moved[start - shift : start - shift + frames]
        block = glu_ref[:, cols]
        for shift in range(8):
            moved = block if shift == 0 else pltpu.roll(block, wide - shift, 0)
            for j in range(taps):
                start = MARGIN + j - half
                if start % 8 == shift:
                    small_ref[j : j + 1, cols] = jnp.sum(
                        own * moved[start - shift : start - shift + frames], axis=0, keepdims=True
                    )
        total = jnp.where(valid, total, 0.0)
        gate = gate_ref[:, cols]
        linear_grad = (total * gate).astype(jnp.bfloat16)
        gate_grad = (total * linear_ref[:, cols] * gate * (1.0 - gate)).astype(jnp.bfloat16)
        lifted_ref[:, cols] = linear_grad
        lifted_ref[:, high] = gate_grad
        message_ref[i, :frames, :128] = linear_grad
        message_ref[i, :frames, 128:256] = gate_grad

    for i in range(width // 128):
        lanes(i)
    for copy in copies:
        copy.wait()
    input_grad = lax.dot_general(
        lifted_ref[...], held_ref[...], (((1,), (1,)), ((), ())), preferred_element_type=jnp.float32
    )
    small_ref[taps : taps + 1, :] = jnp.sum(input_grad * one_ref[...], axis=0, keepdims=True)
    for i in range(width // 128):
        for part in range(2):
            rows = small_ref[part * 24 : (part + 1) * 24, :]
            message_ref[i, frames:, part * 128 : (part + 1) * 128] = jnp.concatenate(
                [rows[:, i * 64 : (i + 1) * 64], rows[:, (i + 8) * 64 : (i + 9) * 64]], axis=1
            ).astype(jnp.bfloat16)


def block_kernel(hidden_ref, activated_ref, down_ref, block_ref, held_ref, sems):
    width = hidden_ref.shape[1]
    copies = fetches(
        down_ref, held_ref, sems, [pl.ds(i * 256, 256) for i in range(width // 256)]
    )
    for copy in copies:
        copy.wait()
    block_ref[...] = (
        hidden_ref[...]
        + jnp.dot(
            activated_ref[:, :width], held_ref[...], preferred_element_type=jnp.float32
        )
    ).astype(jnp.bfloat16)


def block_part(hidden, activated, down):
    return pl.pallas_call(
        block_kernel,
        out_shape=struct(hidden.shape, jnp.bfloat16),
        in_specs=[VMEM, VMEM, HBM],
        out_specs=VMEM,
        scratch_shapes=[
            pltpu.VMEM(down.shape, down.dtype),
            pltpu.SemaphoreType.DMA((down.shape[0] // 256,)),
        ],
        compiler_params=params(12),
        name="block_out",
    )(hidden, activated, in_hbm(down))


def back_part(*operands):
    frames, width = operands[2].shape
    near = frames + MARGIN
    f32, bf = jnp.float32, jnp.bfloat16
    return pl.pallas_call(
        back_kernel,
        out_shape=struct((width // 128, frames + 24, 256), bf),
        in_specs=[VMEM] * 10 + [HBM],
        out_specs=VMEM,
        scratch_shapes=[
            pltpu.VMEM((near, width), f32),
            pltpu.VMEM((48, width), f32),
            pltpu.VMEM((frames, 2 * width), bf),
            pltpu.VMEM((width, 2 * width), bf),
            pltpu.SemaphoreType.DMA((width // 256,)),
        ],
        compiler_params=params(20),
        name="backward",
    )(*operands[:-1], in_hbm(operands[-1]))


TURNED = (((0,), (0,)), ((), ()))


def up_kernel(count, message_ref, *refs):
    parts_ref, cols_ref, one_ref = refs[2 * count :]
    frames, width = refs[0].shape
    core, line = lax.axis_index("dlo"), lax.axis_index("chi")
    small = jnp.zeros((24, 256), jnp.float32)
    for side in range(2):
        for k in range(count):
            at = (side * count + k) * frames
            source = (core ^ side) * count + (line ^ k)
            cols_ref[at : at + frames, :] = message_ref[source, :frames, :]
            one_ref[at : at + frames, :] = refs[side * count + k][...]
            small = small + message_ref[source, frames:, :].astype(jnp.float32)
    up = lax.dot_general(
        cols_ref[...], one_ref[...], TURNED, preferred_element_type=jnp.float32
    ).astype(jnp.bfloat16)
    small = small.astype(jnp.bfloat16)
    for s in range(4):
        parts_ref[s, :64, :] = up[s * 64 : (s + 1) * 64]
        for i in range(6):
            at = (i // 3) * 128 + s * 32
            parts_ref[s, 64:, i * 128 : (i + 1) * 128] = jnp.concatenate(
                [small[(i % 3) * 8 : (i % 3 + 1) * 8, at : at + 32]] * 4, axis=1
            )
        parts_ref[s, 64:, 768:] = jnp.zeros((8, width - 768), jnp.bfloat16)


def up_part(message, pieces):
    count = len(pieces) // 2
    frames, width = pieces[0].shape
    bf = jnp.bfloat16
    rows = 2 * count * frames
    return pl.pallas_call(
        functools.partial(up_kernel, count),
        out_shape=struct((4, 72, width), bf),
        in_specs=[VMEM] * (1 + len(pieces)),
        out_specs=VMEM,
        scratch_shapes=[pltpu.VMEM((rows, 256), bf), pltpu.VMEM((rows, width), bf)],
        compiler_params=params(12),
        name="up_products",
    )(message, *pieces)


def pack_kernel(act_ref, *refs):
    count = len(refs) // 2
    width = act_ref.shape[1]
    for cols_ref, out_ref in zip(refs[:count], refs[count:]):
        out_ref[:, :width] = act_ref[...]
        out_ref[:, width:] = cols_ref[...]


def pack_part(act, cols):
    shape = struct((act.shape[0], act.shape[1] + cols[0].shape[1]), act.dtype)
    count = len(cols)
    return pl.pallas_call(
        pack_kernel,
        out_shape=(shape,) * count,
        in_specs=[VMEM] * (1 + count),
        out_specs=(VMEM,) * count,
        compiler_params=params(),
        name="pack",
    )(act, *cols)


def down_kernel(*refs):
    pieces, (mine_ref, theirs_ref, rows_ref) = refs[:-3], refs[-3:]
    width = mine_ref.shape[1]
    frames = pieces[0].shape[0]
    for i, piece in enumerate(pieces):
        rows_ref[i * frames : (i + 1) * frames, :] = piece[...]
    total = lax.dot_general(
        rows_ref[:, width:], rows_ref[:, :width], TURNED, preferred_element_type=jnp.float32
    ).astype(jnp.bfloat16)
    half = total.shape[0] // 2
    mine_ref[...] = total[:half]
    theirs_ref[...] = total[half:]


def down_part(pieces, width):
    frames, wide = pieces[0].shape
    shape = struct(((wide - width) // 2, width), jnp.bfloat16)
    return pl.pallas_call(
        down_kernel,
        out_shape=(shape, shape),
        in_specs=[VMEM] * len(pieces),
        out_specs=(VMEM, VMEM),
        scratch_shapes=[pltpu.VMEM((len(pieces) * frames, wide), jnp.bfloat16)],
        compiler_params=params(12),
        name="down_products",
    )(*pieces)


def share_kernel(mine_ref, other_ref, *refs):
    outs, total_ref = refs[:-1], refs[-1]
    total_ref[...] = mine_ref[...].astype(jnp.float32) + other_ref[...].astype(jnp.float32)
    for k, out in enumerate(outs):
        at = pl.multiple_of((lax.axis_index("chi") ^ k) * 32, 32)
        out[...] = total_ref[pl.ds(at, 32), :].astype(jnp.bfloat16)


def share_part(mine, other):
    rows, width = mine.shape
    count = rows // 32
    return pl.pallas_call(
        share_kernel,
        out_shape=(struct((32, width), jnp.bfloat16),) * count,
        in_specs=[VMEM, VMEM],
        out_specs=(VMEM,) * count,
        scratch_shapes=[pltpu.VMEM((rows, width), jnp.float32)],
        compiler_params=params(),
        name="down_shares",
    )(mine, other)


def sum_kernel(taps, parts_ref, *refs):
    pieces, (up_ref, down_ref, kernel_ref, one_ref, two_ref) = refs[:4], refs[4:]
    total = parts_ref[0].astype(jnp.float32)
    for s in range(1, parts_ref.shape[0]):
        total = total + parts_ref[s].astype(jnp.float32)
    up_ref[...] = total[:64]
    down_ref[...] = (pieces[0][...].astype(jnp.float32) + pieces[1][...].astype(jnp.float32)) + (
        pieces[2][...].astype(jnp.float32) + pieces[3][...].astype(jnp.float32)
    )
    small = jnp.concatenate(
        [total[64:72, i * 128 : (i + 1) * 128] for i in range(6)], axis=0
    )
    kernel_ref[...] = jnp.transpose(small[:32])[:32, :taps]
    one_ref[...] = small[taps : taps + 1, :32]
    two_ref[...] = small[taps + 1 : taps + 2, :32]


def sum_part(parts, pieces, taps):
    width = parts.shape[2]
    f32 = jnp.float32
    return pl.pallas_call(
        functools.partial(sum_kernel, taps),
        out_shape=(
            struct((64, width), f32),
            struct((32, width), f32),
            struct((32, taps), f32),
            struct((1, 32), f32),
            struct((1, 32), f32),
        ),
        in_specs=[VMEM] * 5,
        out_specs=(VMEM,) * 5,
        compiler_params=params(),
        name="sums",
    )(parts, *pieces)


def flipped(rows, axis, bit):
    size = lax.axis_size(axis)
    return lax.ppermute(rows, axis, [(i, i ^ bit) for i in range(size)])


def with_swapped(pieces):
    return list(pieces) + [flipped(piece, "dlo", 1) for piece in pieces]


def small_device(
    residual, projections, out_weight, gain_one, up_weight, conv_kernel, gain_two, down_weight,
    lengths, out_grad,
):
    frames, _, width = residual.shape
    taps = conv_kernel.shape[0]
    chi, clo = lax.axis_size("chi"), lax.axis_size("clo")
    ctx = chi * clo
    head_size = width // HEADS
    me = lax.axis_index(CTX)
    scalars = jnp.stack([lengths[0], me * frames]).astype(jnp.int32).reshape(1, 2)
    res = residual.reshape(frames, width)
    grad = out_grad.reshape(frames, width)
    gain_one = gain_one.reshape(1, width)
    gain_two = gain_two.reshape(1, width)

    qkv = split_heads(projections.reshape(frames, 3 * width), ctx)
    qkv = lax.all_to_all(qkv, CTX, split_axis=0, concat_axis=0, tiled=True)
    low, high = edges(res, grad)
    up = [(i, i + 1) for i in range(ctx - 1)]
    down = [(j, i) for i, j in up]
    before = lax.ppermute(high, CTX, up)
    after = lax.ppermute(low, CTX, down)
    qkv, before, after = lax.optimization_barrier((qkv, before, after))
    windows = attend_windows(scalars, qkv.reshape(ctx * frames, -1), head_size, frames, ctx)
    windows, before, after = lax.optimization_barrier((windows, before, after))
    windows = lax.all_to_all(windows, CTX, split_axis=0, concat_axis=0, tiled=True)
    *cols, act_grad = cot_part(scalars, grad, before, after, down_weight)
    windows, act_grad, cols = lax.optimization_barrier((windows, act_grad, cols))

    (
        hidden, normed_one, scaled, activated, linear, gate, glu, normed_two, inverse_two
    ) = forward_part(
        scalars, windows, res, before, after, out_weight, gain_one, up_weight, conv_kernel, gain_two
    )
    packed, to_y, to_x, to_xy = pack_part(activated, cols)
    pairs = [(i, i ^ 3) for i in range(4)]
    received = [
        flipped(to_y, "clo", 1), flipped(to_x, "dhi", 1), lax.ppermute(to_xy, SECOND, pairs)
    ]
    one_near, one_far = flipped(scaled, "chi", 1), flipped(scaled, "chi", 2)
    message = back_part(
        scalars, act_grad, normed_one, linear, gate,
        glu, normed_two, inverse_two, conv_kernel, gain_two, up_weight,
    )
    received, one_near, one_far, message = lax.optimization_barrier(
        (received, one_near, one_far, message)
    )
    message = lax.all_to_all(message, FIRST, split_axis=0, concat_axis=0, tiled=True)
    one_last = flipped(one_far, "chi", 1)
    mine, theirs = down_part([packed, *received], width)
    downs = share_part(mine, flipped(theirs, "dlo", 1))
    early = with_swapped([scaled, one_near, one_far])
    one_last, early, downs = lax.optimization_barrier((one_last, early, downs))
    last = with_swapped([one_last])
    ones = early[:3] + last[:1] + early[3:] + last[1:]
    downs = [downs[0]] + [flipped(downs[k], "chi", k) for k in range(1, chi)]
    parts = up_part(message, ones)
    parts = lax.all_to_all(parts, SECOND, split_axis=0, concat_axis=0, tiled=True)
    block_out = block_part(hidden, activated, down_weight)
    up_grad, down_grad, kernel_grad, one, two = sum_part(parts, downs, taps)
    return (
        block_out.reshape(frames, 1, width), up_grad, down_grad, kernel_grad,
        one.reshape(-1), two.reshape(-1),
    )


def fits(residual, conv_kernel, sizes):
    dhi, dlo, chi, clo = sizes
    frames, utter_count, width = residual.shape
    return (
        utter_count == 1
        and frames == 64
        and width == 1024
        and conv_kernel.shape[0] == 31
        and (dhi, dlo, chi, clo) == (2, 2, 4, 2)
    )


def on_device(
    residual,
    projections,
    out_weight,
    gain_one,
    up_weight,
    conv_kernel,
    gain_two,
    down_weight,
    lengths,
    out_grad,
):
    frames, utter_count, width = residual.shape
    head_size = width // HEADS
    kernel_len = conv_kernel.shape[0]
    half = (kernel_len - 1) // 2
    dhi, dlo, chi, clo = sizes = tuple(lax.axis_size(a) for a in ("dhi", "dlo", "chi", "clo"))
    if fits(residual, conv_kernel, sizes):
        return small_device(
            residual,
            projections,
            out_weight,
            gain_one,
            up_weight,
            conv_kernel,
            gain_two,
            down_weight,
            lengths,
            out_grad,
        )
    ctx = chi * clo
    length = frames * ctx
    items = utter_count * HEADS // ctx
    me = lax.axis_index(CTX)
    bf = jnp.bfloat16
    f32 = jnp.float32

    packed = projections.reshape(frames, ctx, items, 3 * head_size)
    packed = lax.all_to_all(packed, CTX, split_axis=1, concat_axis=0, tiled=True)
    packed = packed.reshape(length, items, 3 * head_size)

    both = jnp.concatenate([residual, out_grad], axis=-1)
    up = [(i, i + 1) for i in range(ctx - 1)]
    down = [(j, i) for i, j in up]
    before = lax.ppermute(both[frames - MARGIN :], CTX, up)
    after = lax.ppermute(both[:MARGIN], CTX, down)
    both = jnp.concatenate([before, both, after], axis=0)
    wide = frames + 2 * MARGIN
    place = me * frames - MARGIN + jnp.arange(wide, dtype=jnp.int32)
    valid = (place[:, None] >= 0) & (place[:, None] < lengths[None, :])
    row_mask = valid.astype(f32)[:, :, None]
    cot = jnp.where(valid[:, :, None], both[:, :, width:], 0)
    edge = MARGIN // 2
    near = wide - 2 * edge
    cot_near = cot[edge : edge + near]
    cot_own = cot[MARGIN : MARGIN + frames].reshape(frames * utter_count, width)
    act_grad = lax.dot_general(
        cot_near, down_weight, (((2,), (1,)), ((), ())), preferred_element_type=f32
    )

    key_lengths = lengths[(me * items + jnp.arange(items, dtype=jnp.int32)) // HEADS]
    context = attend(packed, key_lengths).reshape(length, items * head_size)
    padded = jnp.pad(context, ((MARGIN, MARGIN), (0, 0)))
    windows = jnp.stack([padded[i * frames : i * frames + wide] for i in range(ctx)])
    context = lax.all_to_all(windows, CTX, split_axis=0, concat_axis=0, tiled=True)
    context = jnp.transpose(context, (1, 0, 2)).reshape(wide, utter_count, width)

    cot_cols = lax.all_to_all(
        by_owner(cot_own, sizes), FIRST, split_axis=0, concat_axis=0, tiled=True
    )

    hidden = both[:, :, :width].astype(f32) + jnp.einsum(
        "fuc,cd->fud", context, out_weight, preferred_element_type=f32
    )
    normed_one, _ = normalize(hidden)
    scaled_one = (normed_one * gain_one).astype(bf)
    own = slice(MARGIN, MARGIN + frames)
    own_near = slice(MARGIN - edge, MARGIN - edge + frames)
    rows = frames * utter_count
    scaled_own = scaled_one[own].reshape(rows, width)
    scaled_all = gathered(scaled_own, chi)

    lifted = jnp.einsum("fuc,cd->fud", scaled_one, up_weight, preferred_element_type=f32)
    linear_part = lifted[:, :, :width]
    gate_part = jax.nn.sigmoid(lifted[:, :, width:])
    glu = (linear_part * gate_part * row_mask).astype(bf).astype(f32)
    conv_out = jnp.zeros((near, utter_count, width), f32)
    for j in range(kernel_len):
        start = edge + j - half
        conv_out = conv_out + conv_kernel[j] * glu[start : start + near]
    normed_two, inverse_two = normalize(conv_out)
    pre_act = normed_two * gain_two
    gate_two = jax.nn.sigmoid(pre_act)
    activated = (pre_act * gate_two)[own_near].astype(bf).reshape(rows, width)
    activated_all = gathered(activated, chi)
    block_out = (
        hidden[own].reshape(rows, width)
        + jnp.dot(activated, down_weight, preferred_element_type=f32)
    ).astype(bf)
    block_out = block_out.reshape(frames, utter_count, width)

    pre_grad = act_grad * gate_two * (1.0 + pre_act * (1.0 - gate_two))
    gain_two_grad = jnp.sum((pre_grad * normed_two)[own_near], axis=(0, 1))
    scaled_grad = pre_grad * gain_two
    conv_grad = inverse_two * (
        scaled_grad
        - jnp.mean(scaled_grad, axis=-1, keepdims=True)
        - normed_two * jnp.mean(scaled_grad * normed_two, axis=-1, keepdims=True)
    )
    conv_grad = conv_grad.astype(bf).astype(f32)
    conv_own = conv_grad[own_near]
    small = []
    glu_grad = jnp.zeros((frames, utter_count, width), f32)
    for j in range(kernel_len):
        start = MARGIN + j - half
        small.append(jnp.sum(conv_own * glu[start : start + frames], axis=(0, 1)))
        start = MARGIN - edge + half - j
        glu_grad = glu_grad + conv_kernel[j] * conv_grad[start : start + frames]
    glu_grad = glu_grad * row_mask[own]
    gate_own = gate_part[own]
    linear_grad = glu_grad * gate_own
    gate_grad = glu_grad * linear_part[own] * gate_own * (1.0 - gate_own)
    lifted_grad = jnp.concatenate([linear_grad, gate_grad], axis=-1).astype(bf)
    lifted_grad = lifted_grad.reshape(rows, 2 * width)
    input_grad = lax.dot_general(
        lifted_grad, up_weight, (((1,), (1,)), ((), ())), preferred_element_type=f32
    )
    gain_one_grad = jnp.sum(input_grad * normed_one[own].reshape(rows, width), axis=0)

    small = small + [gain_one_grad, gain_two_grad]
    count = kernel_len + 2
    small = by_owner(jnp.stack(small).astype(bf), sizes)
    small = small.reshape(dlo * chi, -1)
    cols = by_owner(lifted_grad, sizes)
    col_count = cols.shape[2]
    spare = -small.shape[1] % col_count
    small = jnp.pad(small, ((0, 0), (0, spare))).reshape(dlo * chi, -1, col_count)
    message = jnp.concatenate([cols, small], axis=1)
    message = lax.all_to_all(message, FIRST, split_axis=0, concat_axis=0, tiled=True)
    cols = message[:, :rows].reshape(-1, col_count)
    small = jnp.sum(message[:, rows:].astype(f32), axis=0).reshape(-1)
    seconds = dhi * clo
    small_width = width // (ctx * dhi * dlo)
    small = small[: count * seconds * small_width].reshape(count, seconds, small_width)
    small = jnp.transpose(small, (1, 0, 2)).reshape(seconds, count * small_width)

    up_part = lax.dot_general(
        cols, scaled_all, (((0,), (0,)), ((), ())), preferred_element_type=f32
    ).reshape(seconds, -1, width)
    down_part = lax.dot_general(
        cot_cols.reshape(cols.shape[0], -1),
        activated_all,
        (((0,), (0,)), ((), ())),
        preferred_element_type=f32,
    ).reshape(seconds, -1, width)
    spare = -small.shape[1] % width
    small = jnp.pad(small, ((0, 0), (0, spare))).reshape(seconds, -1, width)
    up_rows, down_rows = up_part.shape[1], down_part.shape[1]
    parts = jnp.concatenate([up_part.astype(bf), down_part.astype(bf), small.astype(bf)], axis=1)
    parts = lax.all_to_all(parts, SECOND, split_axis=0, concat_axis=0, tiled=True)
    total = jnp.sum(parts.astype(f32), axis=0)
    up_grad = total[:up_rows]
    down_grad = total[up_rows : up_rows + down_rows]
    small = total[up_rows + down_rows :].reshape(-1)[: count * small_width]
    small = small.reshape(count, small_width)
    kernel_grad = jnp.transpose(small[:kernel_len])
    return (block_out, up_grad, down_grad, kernel_grad, small[kernel_len], small[kernel_len + 1])


def solution(mesh):
    dp, ctx = mesh.shape["dp"], mesh.shape["ctx"]
    fine = Mesh(mesh.devices.reshape(dp // 2, 2, ctx // 2, 2), ("dhi", "dlo", "chi", "clo"))
    dp_axes, ctx_axes = ("dhi", "dlo"), ("chi", "clo")
    every = ("dhi", "dlo", "chi", "clo")
    in_specs = (
        P(ctx_axes, dp_axes, None),
        P(ctx_axes, dp_axes, None),
        P(),
        P(),
        P(),
        P(),
        P(),
        P(),
        P(dp_axes),
        P(ctx_axes, dp_axes, None),
    )
    out_specs = (
        P(ctx_axes, dp_axes, None),
        P(every, None),
        P(every, None),
        P(every, None),
        P(every),
        P(every),
    )
    return jax.shard_map(
        on_device, mesh=fine, in_specs=in_specs, out_specs=out_specs, check_vma=False
    )
```

```python
import functools

import jax
import jax.numpy as jnp
from jax import lax
from jax.experimental import pallas as pl
from jax.experimental.pallas import tpu as pltpu
from jax.sharding import Mesh, PartitionSpec as P

HEADS = 16


EPSILON = 1e-05

MARGIN = 32

CTX = ("chi", "clo")
FIRST = ("dlo", "chi")
SECOND = ("dhi", "clo")

SMEM = pl.BlockSpec(memory_space=pltpu.SMEM)
VMEM = pl.BlockSpec(memory_space=pltpu.VMEM)
HBM = pl.BlockSpec(memory_space=pltpu.HBM)


def normalize(values):
    center = values - jnp.mean(values, axis=-1, keepdims=True)
    inverse = lax.rsqrt(jnp.mean(center * center, axis=-1, keepdims=True) + EPSILON)
    return (center * inverse, inverse)


def attend(packed, key_lengths):
    length, count, triple = packed.shape
    head_size = triple // 3
    query_rows = packed[:, :, :head_size]
    key_rows = packed[:, :, head_size : 2 * head_size]
    value_rows = packed[:, :, 2 * head_size :]
    allowed = jnp.arange(length, dtype=jnp.int32)[None, :] < key_lengths[:, None]
    scores = (
        jnp.einsum("qmd,kmd->mqk", query_rows, key_rows, preferred_element_type=jnp.float32)
        * head_size ** (-0.5)
    )
    scores = jnp.where(allowed[:, None, :], scores, -jnp.inf)
    highest = jnp.max(scores, axis=-1, keepdims=True)
    raised = jnp.exp(scores - highest)
    weights_bf = (raised / jnp.sum(raised, axis=-1, keepdims=True)).astype(jnp.bfloat16)
    return jnp.einsum(
        "mqk,kmd->qmd", weights_bf, value_rows, preferred_element_type=jnp.float32
    ).astype(jnp.bfloat16)


def by_owner(cols, sizes):
    dhi, dlo, chi, clo = sizes
    rows, width = cols.shape
    part = width // (dhi * dlo * chi * clo)
    split = cols.reshape(rows, dhi, dlo, chi, clo, part)
    return jnp.transpose(split, (2, 3, 0, 1, 4, 5)).reshape(dlo * chi, rows, dhi * clo * part)


def gathered(rows, chi):
    copies = jnp.broadcast_to(rows[None], (chi,) + rows.shape)
    line = lax.all_to_all(copies, "chi", split_axis=0, concat_axis=0, tiled=True)
    line = line.reshape(chi * rows.shape[0], rows.shape[1])
    other = lax.ppermute(line, "dlo", [(0, 1), (1, 0)])
    first = lax.axis_index("dlo") == 0
    return jnp.concatenate([jnp.where(first, line, other), jnp.where(first, other, line)], axis=0)


def params(mebi=8):
    return pltpu.CompilerParams(vmem_limit_bytes=mebi * 1024 * 1024)


def struct(shape, dtype):
    return jax.ShapeDtypeStruct(shape, dtype)


def in_hbm(array):
    return pltpu.with_memory_space_constraint(array, pltpu.HBM)


def fetches(source, target, sems, parts):
    copies = []
    for i, part in enumerate(parts):
        copies.append(pltpu.make_async_copy(source.at[part], target.at[part], sems.at[i]))
        copies[-1].start()
    return copies


def split_kernel(proj_ref, out_ref, held_ref, sems):
    count, _, span = out_ref.shape
    copies = []
    for i in range(count):
        copies.append(
            pltpu.make_async_copy(
                proj_ref.at[:, pl.ds(i * span, span)], held_ref.at[i], sems.at[0, i]
            )
        )
        copies[-1].start()
    sends = []
    for i, copy in enumerate(copies):
        copy.wait()
        sends.append(pltpu.make_async_copy(held_ref.at[i], out_ref.at[i], sems.at[1, i]))
        sends[-1].start()
    for send in sends:
        send.wait()


def split_heads(proj, count):
    rows, cols = proj.shape
    shape = (count, rows, cols // count)
    return pl.pallas_call(
        split_kernel,
        out_shape=struct(shape, proj.dtype),
        in_specs=[HBM],
        out_specs=HBM,
        scratch_shapes=[pltpu.VMEM(shape, proj.dtype), pltpu.SemaphoreType.DMA((2, count))],
        compiler_params=params(),
        name="split_heads",
    )(in_hbm(proj))


def edge_kernel(res_ref, grad_ref, low_ref, high_ref, sems):
    rows = res_ref.shape[0]
    copies = []
    for i, (source, at, count) in enumerate(
        ((res_ref, 0, MARGIN), (grad_ref, MARGIN, MARGIN // 2))
    ):
        for j, (target, start) in enumerate(((high_ref, rows - count), (low_ref, 0))):
            copies.append(
                pltpu.make_async_copy(
                    source.at[pl.ds(start, count)], target.at[pl.ds(at, count)], sems.at[i, j]
                )
            )
            copies[-1].start()
    for copy in copies:
        copy.wait()


def edges(res, grad):
    shape = struct((MARGIN + MARGIN // 2, res.shape[1]), res.dtype)
    spec = pl.BlockSpec(memory_space=pl.ANY)
    return pl.pallas_call(
        edge_kernel,
        out_shape=(shape, shape),
        in_specs=[HBM, HBM],
        out_specs=(spec, spec),
        scratch_shapes=[pltpu.SemaphoreType.DMA((2, 2))],
        compiler_params=params(),
        name="edges",
    )(in_hbm(res), in_hbm(grad))


def attend_kernel(head_size, frames, scalar_ref, qkv_ref, out_ref):
    length = qkv_ref.shape[0]
    count = qkv_ref.shape[1] // (3 * head_size)
    ctx, wide, _ = out_ref.shape
    places = lax.broadcasted_iota(jnp.int32, (1, length), 1)
    bias = jnp.where(places < scalar_ref[:, 0:1], 0.0, -jnp.inf)
    scores = []
    for m in range(count):
        base = 3 * head_size * m
        query = qkv_ref[:, base : base + head_size] * jnp.bfloat16(head_size ** (-0.5))
        key = qkv_ref[:, base + head_size : base + 2 * head_size]
        scores.append(bias + lax.dot_general(
                query, key, (((1,), (1,)), ((), ())), preferred_element_type=jnp.float32))
    scores = jnp.concatenate(scores, axis=0)
    raised = jnp.exp(scores - jnp.max(scores, axis=-1, keepdims=True))
    share = 1.0 / jnp.sum(raised, axis=-1, keepdims=True)
    weights = raised.astype(jnp.bfloat16)
    heads = []
    for m in range(count):
        base = 3 * head_size * m
        value = qkv_ref[:, base + 2 * head_size : base + 3 * head_size]
        rows = slice(m * length, (m + 1) * length)
        heads.append(
            jnp.dot(weights[rows], value, preferred_element_type=jnp.float32) * share[rows]
        )
    context = jnp.concatenate(heads, axis=1).astype(jnp.bfloat16)
    for i in range(ctx):
        low = max(i * frames - MARGIN, 0)
        high = min(i * frames - MARGIN + wide, length)
        at = low - (i * frames - MARGIN)
        out_ref[i, at : at + high - low, :] = context[low:high]
        if at > 0:
            out_ref[i, :at, :] = jnp.zeros((at, context.shape[1]), context.dtype)
        if at + high - low < wide:
            rest = wide - (at + high - low)
            out_ref[i, wide - rest :, :] = jnp.zeros((rest, context.shape[1]), context.dtype)


def attend_windows(scalars, qkv, head_size, frames, ctx):
    wide = frames + 2 * MARGIN
    return pl.pallas_call(
        functools.partial(attend_kernel, head_size, frames),
        out_shape=struct((ctx, wide, qkv.shape[1] // 3), jnp.bfloat16),
        in_specs=[VMEM, VMEM],
        out_specs=VMEM,
        compiler_params=params(16),
        name="attend",
    )(scalars, qkv)


def cot_kernel(scalar_ref, grad_ref, low_ref, high_ref, weight_ref, *refs):
    out_ref, cols_refs = refs[0], refs[1:5]
    act_ref, ready_ref, held_ref, weight_held_ref, sems, ready_sems = refs[5:]
    ready = fetches(
        out_ref,
        ready_ref,
        ready_sems,
        [pl.ds(i * 256, 256) for i in range(ready_ref.shape[0] // 256)],
    )
    frames, width = grad_ref.shape
    copies = fetches(
        weight_ref, weight_held_ref, sems, [pl.ds(i * 256, 256) for i in range(width // 256)]
    )
    edge = MARGIN // 2
    whole = jnp.concatenate([low_ref[MARGIN:, :], grad_ref[...], high_ref[MARGIN:, :]], axis=0)
    near = whole.shape[0]
    place = scalar_ref[:, 1:2] - edge + lax.broadcasted_iota(jnp.int32, (near, width), 0)
    valid = (place >= 0) & (place < scalar_ref[:, 0:1])
    whole = jnp.where(valid, whole.astype(jnp.float32), 0.0).astype(jnp.bfloat16)
    cot = whole[edge : edge + frames]
    count, _, span = held_ref.shape
    piece = span // 4
    for group in range(count):
        high_bits, low_bit = group // 2, group % 2
        held_ref[group, :, :] = jnp.concatenate(
            [
                cot[:, (8 * high_bits + 2 * z + low_bit) * piece :][:, :piece]
                for z in range(4)
            ],
            axis=1,
        )
    dhi, dlo, clo = lax.axis_index("dhi"), lax.axis_index("dlo"), lax.axis_index("clo")
    for k, cols_ref in enumerate(cols_refs):
        for side in range(2):
            group = ((dhi ^ (k // 2)) * 2 + (dlo ^ side)) * 2 + (clo ^ (k % 2))
            cols_ref[:, side * span : (side + 1) * span] = held_ref[group]
    for copy in copies:
        copy.wait()
    act_ref[...] = lax.dot_general(
        whole, weight_held_ref[...], (((1,), (1,)), ((), ())), preferred_element_type=jnp.float32
    )
    for copy in ready:
        copy.wait()


def cot_part(scalars, grad, low, high, weight, out_weight):
    frames, width = grad.shape
    cols = struct((frames, width // 4), grad.dtype)
    return pl.pallas_call(
        cot_kernel,
        out_shape=(
            cols, cols, cols, cols,
            struct((frames + MARGIN, width), jnp.float32),
            struct((width * 3 // 4, width), weight.dtype),
        ),
        in_specs=[VMEM, VMEM, VMEM, VMEM, HBM, HBM],
        out_specs=(VMEM,) * 6,
        scratch_shapes=[
            pltpu.VMEM((8, frames, width // 8), grad.dtype),
            pltpu.VMEM(weight.shape, weight.dtype),
            pltpu.SemaphoreType.DMA((width // 256,)),
            pltpu.SemaphoreType.DMA((3,)),
        ],
        compiler_params=params(12),
        name="cotangent",
    )(scalars, grad, low, high, in_hbm(weight), in_hbm(out_weight))


def forward_kernel(
    scalar_ref, context_ref, res_ref, low_ref, high_ref, out_ref, ready_ref, gain_one_ref, weight_ref,
    taps_ref, gain_ref,
    hidden_ref, one_ref, own_ref, act_ref, linear_ref, gate_ref, glu_ref,
    normed_ref, inverse_ref, scaled_ref, conv_ref, out_held_ref, held_ref, res_held_ref, out_sems, sems, res_sems,
):
    frames, width = res_ref.shape
    ctx, wide, lanes = context_ref.shape
    taps = taps_ref.shape[0]
    half = (taps - 1) // 2
    edge = MARGIN // 2
    near = wide - 2 * edge
    depth = 2 * lanes
    res_copies = fetches(res_ref, res_held_ref, res_sems, [slice(None)])
    held_rows = ready_ref.shape[0]
    out_copies = fetches(
        out_ref, out_held_ref, out_sems, [pl.ds(held_rows, width - held_rows)]
    )
    span = 256
    copies = fetches(
        weight_ref, held_ref, sems, [pl.ds(i * span, span) for i in range(width // span)]
    )
    context = jnp.concatenate([context_ref[i] for i in range(ctx)], axis=1)
    product = jnp.dot(
        context[:, :held_rows], ready_ref[...], preferred_element_type=jnp.float32
    )
    out_copies[0].wait()
    product = product + jnp.dot(
        context[:, held_rows:], out_held_ref[held_rows:, :], preferred_element_type=jnp.float32
    )
    res_copies[0].wait()
    step = 32
    for at in range(0, wide, step):
        if at < MARGIN:
            res = low_ref[at : at + step, :]
        elif at < MARGIN + frames:
            res = res_held_ref[at - MARGIN : at - MARGIN + step, :]
        else:
            res = high_ref[at - MARGIN - frames : at - MARGIN - frames + step, :]
        hidden = res.astype(jnp.float32) + product[at : at + step]
        normed, _ = normalize(hidden)
        scaled = (normed * gain_one_ref[...]).astype(jnp.bfloat16)
        scaled_ref[at : at + step, :] = scaled
        if MARGIN <= at < MARGIN + frames:
            rows = slice(at - MARGIN, at - MARGIN + step)
            hidden_ref[rows, :] = hidden
            one_ref[rows, :] = normed
            own_ref[rows, :] = scaled
    for copy in copies:
        copy.wait()
    place = scalar_ref[:, 1:2] - MARGIN + lax.broadcasted_iota(jnp.int32, (wide, span), 0)
    valid = (place >= 0) & (place < scalar_ref[:, 0:1])
    own = slice(MARGIN, MARGIN + frames)
    for i in range(width // span):
        cols = slice(i * span, (i + 1) * span)
        linear = jnp.dot(scaled_ref[...], held_ref[:, cols], preferred_element_type=jnp.float32)
        gate = jax.nn.sigmoid(
            jnp.dot(
                scaled_ref[...],
                held_ref[:, width + i * span : width + (i + 1) * span],
                preferred_element_type=jnp.float32,
            )
        )
        glu = jnp.where(valid, linear * gate, 0.0).astype(jnp.bfloat16).astype(jnp.float32)
        glu_ref[:, cols] = glu
        linear_ref[:, cols] = linear[own]
        gate_ref[:, cols] = gate[own]
        for at in range(i * span, (i + 1) * span, 128):
            lane = slice(at, at + 128)
            block = glu[:, at - i * span : at - i * span + 128]
            total = jnp.zeros((near, 128), jnp.float32)
            for shift in range(8):
                moved = block if shift == 0 else pltpu.roll(block, wide - shift, 0)
                for j in range(taps):
                    start = edge + j - half
                    if start % 8 == shift:
                        total = total + taps_ref[j : j + 1, lane] * moved[
                            start - shift : start - shift + near
                        ]
            conv_ref[:, lane] = total
    step = 16
    for at in range(0, near, step):
        normed, inverse = normalize(conv_ref[at : at + step, :])
        normed_ref[at : at + step, :] = normed
        inverse_ref[at : at + step, :] = jnp.broadcast_to(inverse, (step, 128))
        if MARGIN - edge <= at < MARGIN - edge + frames:
            pre = normed * gain_ref[...]
            rows = slice(at - (MARGIN - edge), at - (MARGIN - edge) + step)
            act_ref[rows, :] = (pre * jax.nn.sigmoid(pre)).astype(jnp.bfloat16)


def forward_part(
    scalars, context, res, low, high, out_weight, ready, gain_one, weight, taps, gain
):
    frames, width = res.shape
    ctx, wide, _ = context.shape
    near = wide - MARGIN
    f32, bf = jnp.float32, jnp.bfloat16
    return pl.pallas_call(
        forward_kernel,
        out_shape=(
            struct((frames, width), f32),
            struct((frames, width), f32),
            struct((frames, width), bf),
            struct((frames, width), bf),
            struct((frames, width), f32),
            struct((frames, width), f32),
            struct((wide, width), f32),
            struct((near, width), f32),
            struct((near, 128), f32),
        ),
        in_specs=[VMEM, VMEM, HBM, VMEM, VMEM, HBM, VMEM, VMEM, HBM, VMEM, VMEM],
        out_specs=(VMEM,) * 9,
        scratch_shapes=[
            pltpu.VMEM((wide, width), bf),
            pltpu.VMEM((near, width), f32),
            pltpu.VMEM(out_weight.shape, bf),
            pltpu.VMEM(weight.shape, bf),
            pltpu.VMEM(res.shape, bf),
            pltpu.SemaphoreType.DMA((ctx // 2,)),
            pltpu.SemaphoreType.DMA((width // 256,)),
            pltpu.SemaphoreType.DMA((1,)),
        ],
        compiler_params=params(24),
        name="forward",
    )(
        scalars, context, in_hbm(res), low, high, in_hbm(out_weight), ready, gain_one,
        in_hbm(weight), taps, gain
    )


def back_kernel(
    scalar_ref, act_grad_ref, one_ref, linear_ref, gate_ref,
    glu_ref, normed_ref, inverse_ref, taps_ref, gain_ref, up_ref,
    message_ref, grad_ref, small_ref, lifted_ref, held_ref, sems,
):
    frames, width = one_ref.shape
    near = normed_ref.shape[0]
    wide = glu_ref.shape[0]
    taps = taps_ref.shape[0]
    half = (taps - 1) // 2
    edge = MARGIN // 2
    first = MARGIN - edge
    copies = fetches(up_ref, held_ref, sems, [pl.ds(i * 256, 256) for i in range(width // 256)])
    gain = gain_ref[...]
    step = 16
    two = jnp.zeros((1, width), jnp.float32)
    for at in range(0, near, step):
        normed = normed_ref[at : at + step, :]
        pre = normed * gain
        gate = jax.nn.sigmoid(pre)
        grad = act_grad_ref[at : at + step, :] * gate * (1.0 + pre * (1.0 - gate))
        if first <= at < first + frames:
            two = two + jnp.sum(grad * normed, axis=0, keepdims=True)
        scaled = grad * gain
        result = inverse_ref[at : at + step, 0:1] * (
            scaled
            - jnp.mean(scaled, axis=-1, keepdims=True)
            - normed * jnp.mean(scaled * normed, axis=-1, keepdims=True)
        )
        grad_ref[at : at + step, :] = result.astype(jnp.bfloat16).astype(jnp.float32)
    small_ref[32:, :] = jnp.zeros((16, width), jnp.float32)
    small_ref[taps + 1 : taps + 2, :] = two

    place = scalar_ref[:, 1:2] + lax.broadcasted_iota(jnp.int32, (frames, 128), 0)
    valid = place < scalar_ref[:, 0:1]

    def lanes(i):
        cols = slice(i * 128, (i + 1) * 128)
        high = slice(i * 128 + width, (i + 1) * 128 + width)
        block = grad_ref[:, cols]
        own = block[first : first + frames]
        total = jnp.zeros((frames, 128), jnp.float32)
        for shift in range(8):
            moved = block if shift == 0 else pltpu.roll(block, near - shift, 0)
            for j in range(taps):
                start = first + half - j
                if start % 8 == shift:
                    total = total + taps_ref[j : j + 1, cols] * moved[start - shift : start - shift + frames]
        block = glu_ref[:, cols]
        for shift in range(8):
            moved = block if shift == 0 else pltpu.roll(block, wide - shift, 0)
            for j in range(taps):
                start = MARGIN + j - half
                if start % 8 == shift:
                    small_ref[j : j + 1, cols] = jnp.sum(
                        own * moved[start - shift : start - shift + frames], axis=0, keepdims=True
                    )
        total = jnp.where(valid, total, 0.0)
        gate = gate_ref[:, cols]
        linear_grad = (total * gate).astype(jnp.bfloat16)
        gate_grad = (total * linear_ref[:, cols] * gate * (1.0 - gate)).astype(jnp.bfloat16)
        lifted_ref[:, cols] = linear_grad
        lifted_ref[:, high] = gate_grad
        message_ref[i, :frames, :128] = linear_grad
        message_ref[i, :frames, 128:256] = gate_grad

    for i in range(width // 128):
        lanes(i)
    for copy in copies:
        copy.wait()
    input_grad = lax.dot_general(
        lifted_ref[...], held_ref[...], (((1,), (1,)), ((), ())), preferred_element_type=jnp.float32
    )
    small_ref[taps : taps + 1, :] = jnp.sum(input_grad * one_ref[...], axis=0, keepdims=True)
    for i in range(width // 128):
        for part in range(2):
            rows = small_ref[part * 24 : (part + 1) * 24, :]
            message_ref[i, frames:, part * 128 : (part + 1) * 128] = jnp.concatenate(
                [rows[:, i * 64 : (i + 1) * 64], rows[:, (i + 8) * 64 : (i + 9) * 64]], axis=1
            ).astype(jnp.bfloat16)


def block_kernel(hidden_ref, activated_ref, down_ref, block_ref, held_ref, sems):
    width = hidden_ref.shape[1]
    copies = fetches(
        down_ref, held_ref, sems, [pl.ds(i * 256, 256) for i in range(width // 256)]
    )
    for copy in copies:
        copy.wait()
    block_ref[...] = (
        hidden_ref[...]
        + jnp.dot(
            activated_ref[:, :width], held_ref[...], preferred_element_type=jnp.float32
        )
    ).astype(jnp.bfloat16)


def block_part(hidden, activated, down):
    return pl.pallas_call(
        block_kernel,
        out_shape=struct(hidden.shape, jnp.bfloat16),
        in_specs=[VMEM, VMEM, HBM],
        out_specs=VMEM,
        scratch_shapes=[
            pltpu.VMEM(down.shape, down.dtype),
            pltpu.SemaphoreType.DMA((down.shape[0] // 256,)),
        ],
        compiler_params=params(12),
        name="block_out",
    )(hidden, activated, in_hbm(down))


def back_part(*operands):
    frames, width = operands[2].shape
    near = frames + MARGIN
    f32, bf = jnp.float32, jnp.bfloat16
    return pl.pallas_call(
        back_kernel,
        out_shape=struct((width // 128, frames + 24, 256), bf),
        in_specs=[VMEM] * 10 + [HBM],
        out_specs=VMEM,
        scratch_shapes=[
            pltpu.VMEM((near, width), f32),
            pltpu.VMEM((48, width), f32),
            pltpu.VMEM((frames, 2 * width), bf),
            pltpu.VMEM((width, 2 * width), bf),
            pltpu.SemaphoreType.DMA((width // 256,)),
        ],
        compiler_params=params(20),
        name="backward",
    )(*operands[:-1], in_hbm(operands[-1]))


TURNED = (((0,), (0,)), ((), ()))


def up_kernel(count, message_ref, *refs):
    parts_ref, cols_ref, one_ref = refs[2 * count :]
    frames, width = refs[0].shape
    core, line = lax.axis_index("dlo"), lax.axis_index("chi")
    small = jnp.zeros((24, 256), jnp.float32)
    for side in range(2):
        for k in range(count):
            at = (side * count + k) * frames
            source = (core ^ side) * count + (line ^ k)
            cols_ref[at : at + frames, :] = message_ref[source, :frames, :]
            one_ref[at : at + frames, :] = refs[side * count + k][...]
            small = small + message_ref[source, frames:, :].astype(jnp.float32)
    up = lax.dot_general(
        cols_ref[...], one_ref[...], TURNED, preferred_element_type=jnp.float32
    ).astype(jnp.bfloat16)
    small = small.astype(jnp.bfloat16)
    for s in range(4):
        parts_ref[s, :64, :] = up[s * 64 : (s + 1) * 64]
        for i in range(6):
            at = (i // 3) * 128 + s * 32
            parts_ref[s, 64:, i * 128 : (i + 1) * 128] = jnp.concatenate(
                [small[(i % 3) * 8 : (i % 3 + 1) * 8, at : at + 32]] * 4, axis=1
            )
        parts_ref[s, 64:, 768:] = jnp.zeros((8, width - 768), jnp.bfloat16)


def up_part(message, pieces):
    count = len(pieces) // 2
    frames, width = pieces[0].shape
    bf = jnp.bfloat16
    rows = 2 * count * frames
    return pl.pallas_call(
        functools.partial(up_kernel, count),
        out_shape=struct((4, 72, width), bf),
        in_specs=[VMEM] * (1 + len(pieces)),
        out_specs=VMEM,
        scratch_shapes=[pltpu.VMEM((rows, 256), bf), pltpu.VMEM((rows, width), bf)],
        compiler_params=params(12),
        name="up_products",
    )(message, *pieces)


def pack_kernel(act_ref, own_ref, y_ref, x_ref, xy_ref, packed_ref, to_y_ref, to_x_ref):
    width, span = act_ref.shape[1], own_ref.shape[1]
    for cols_ref, out_ref in ((own_ref, packed_ref), (y_ref, to_y_ref), (x_ref, to_x_ref)):
        out_ref[:, :width] = act_ref[...]
        out_ref[:, width : width + span] = cols_ref[...]
    to_x_ref[:, width + span :] = xy_ref[...]


def pack_part(act, cols):
    rows, width = act.shape
    span = cols[0].shape[1]
    return pl.pallas_call(
        pack_kernel,
        out_shape=(
            struct((rows, width + span), act.dtype),
            struct((rows, width + span), act.dtype),
            struct((rows, width + 2 * span), act.dtype),
        ),
        in_specs=[VMEM] * 5,
        out_specs=(VMEM,) * 3,
        compiler_params=params(),
        name="pack",
    )(act, *cols)


def down_kernel(*refs):
    pieces, (mine_ref, theirs_ref, rows_ref) = refs[:-3], refs[-3:]
    width = mine_ref.shape[1]
    frames = pieces[0].shape[0]
    for i, piece in enumerate(pieces):
        rows = slice(i * frames, (i + 1) * frames)
        span = rows_ref.shape[1] - width
        at = width + (span if i == 3 else 0)
        rows_ref[rows, :width] = piece[:, :width]
        rows_ref[rows, width:] = piece[:, at : at + span]
    total = lax.dot_general(
        rows_ref[:, width:], rows_ref[:, :width], TURNED, preferred_element_type=jnp.float32
    ).astype(jnp.bfloat16)
    half = total.shape[0] // 2
    mine_ref[...] = total[:half]
    theirs_ref[...] = total[half:]


def down_part(pieces, width):
    frames, wide = pieces[0].shape
    shape = struct(((wide - width) // 2, width), jnp.bfloat16)
    return pl.pallas_call(
        down_kernel,
        out_shape=(shape, shape),
        in_specs=[VMEM] * len(pieces),
        out_specs=(VMEM, VMEM),
        scratch_shapes=[pltpu.VMEM((len(pieces) * frames, wide), jnp.bfloat16)],
        compiler_params=params(12),
        name="down_products",
    )(*pieces)


def share_kernel(mine_ref, other_ref, *refs):
    outs, total_ref = refs[:-1], refs[-1]
    total_ref[...] = mine_ref[...].astype(jnp.float32) + other_ref[...].astype(jnp.float32)
    for k, out in enumerate(outs):
        at = pl.multiple_of((lax.axis_index("chi") ^ k) * 32, 32)
        out[...] = total_ref[pl.ds(at, 32), :].astype(jnp.bfloat16)


def share_part(mine, other):
    rows, width = mine.shape
    count = rows // 32
    return pl.pallas_call(
        share_kernel,
        out_shape=(struct((32, width), jnp.bfloat16),) * count,
        in_specs=[VMEM, VMEM],
        out_specs=(VMEM,) * count,
        scratch_shapes=[pltpu.VMEM((rows, width), jnp.float32)],
        compiler_params=params(),
        name="down_shares",
    )(mine, other)


def sum_kernel(taps, parts_ref, *refs):
    pieces, (up_ref, down_ref, kernel_ref, one_ref, two_ref) = refs[:4], refs[4:]
    total = parts_ref[0].astype(jnp.float32)
    for s in range(1, parts_ref.shape[0]):
        total = total + parts_ref[s].astype(jnp.float32)
    up_ref[...] = total[:64]
    down_ref[...] = (pieces[0][...].astype(jnp.float32) + pieces[1][...].astype(jnp.float32)) + (
        pieces[2][...].astype(jnp.float32) + pieces[3][...].astype(jnp.float32)
    )
    small = jnp.concatenate(
        [total[64:72, i * 128 : (i + 1) * 128] for i in range(6)], axis=0
    )
    kernel_ref[...] = jnp.transpose(small[:32])[:32, :taps]
    one_ref[...] = small[taps : taps + 1, :32]
    two_ref[...] = small[taps + 1 : taps + 2, :32]


def sum_part(parts, pieces, taps):
    width = parts.shape[2]
    f32 = jnp.float32
    return pl.pallas_call(
        functools.partial(sum_kernel, taps),
        out_shape=(
            struct((64, width), f32),
            struct((32, width), f32),
            struct((32, taps), f32),
            struct((1, 32), f32),
            struct((1, 32), f32),
        ),
        in_specs=[VMEM] * 5,
        out_specs=(VMEM,) * 5,
        compiler_params=params(),
        name="sums",
    )(parts, *pieces)


def flipped(rows, axis, bit):
    size = lax.axis_size(axis)
    return lax.ppermute(rows, axis, [(i, i ^ bit) for i in range(size)])


def with_swapped(pieces):
    return list(pieces) + [flipped(piece, "dlo", 1) for piece in pieces]


def small_device(
    residual, projections, out_weight, gain_one, up_weight, conv_kernel, gain_two, down_weight,
    lengths, out_grad,
):
    frames, _, width = residual.shape
    taps = conv_kernel.shape[0]
    chi, clo = lax.axis_size("chi"), lax.axis_size("clo")
    ctx = chi * clo
    head_size = width // HEADS
    me = lax.axis_index(CTX)
    scalars = jnp.stack([lengths[0], me * frames]).astype(jnp.int32).reshape(1, 2)
    res = residual.reshape(frames, width)
    grad = out_grad.reshape(frames, width)
    gain_one = gain_one.reshape(1, width)
    gain_two = gain_two.reshape(1, width)

    qkv = split_heads(projections.reshape(frames, 3 * width), ctx)
    qkv = lax.all_to_all(qkv, CTX, split_axis=0, concat_axis=0, tiled=True)
    low, high = edges(res, grad)
    up = [(i, i + 1) for i in range(ctx - 1)]
    down = [(j, i) for i, j in up]
    before = lax.ppermute(high, CTX, up)
    after = lax.ppermute(low, CTX, down)
    qkv, before, after = lax.optimization_barrier((qkv, before, after))
    windows = attend_windows(scalars, qkv.reshape(ctx * frames, -1), head_size, frames, ctx)
    windows, before, after = lax.optimization_barrier((windows, before, after))
    windows = lax.all_to_all(windows, CTX, split_axis=0, concat_axis=0, tiled=True)
    *cols, act_grad, ready = cot_part(scalars, grad, before, after, down_weight, out_weight)
    windows, act_grad, cols, ready = lax.optimization_barrier((windows, act_grad, cols, ready))

    (
        hidden, normed_one, scaled, activated, linear, gate, glu, normed_two, inverse_two
    ) = forward_part(
        scalars, windows, res, before, after, out_weight, ready, gain_one, up_weight, conv_kernel,
        gain_two,
    )
    packed, to_y, to_x = pack_part(activated, cols)
    received = [flipped(to_y, "clo", 1), flipped(to_x, "dhi", 1)]
    one_near, one_far = flipped(scaled, "chi", 1), flipped(scaled, "chi", 2)
    message = back_part(
        scalars, act_grad, normed_one, linear, gate,
        glu, normed_two, inverse_two, conv_kernel, gain_two, up_weight,
    )
    received, one_near, one_far, message = lax.optimization_barrier(
        (received, one_near, one_far, message)
    )
    message = lax.all_to_all(message, FIRST, split_axis=0, concat_axis=0, tiled=True)
    one_last = flipped(one_far, "chi", 1)
    diagonal = flipped(received[1], "clo", 1)
    early = with_swapped([scaled, one_near, one_far])
    early, diagonal, one_last = lax.optimization_barrier((early, diagonal, one_last))
    mine, theirs = down_part([packed, *received, diagonal], width)
    downs = share_part(mine, flipped(theirs, "dlo", 1))
    last = with_swapped([one_last])
    ones = early[:3] + last[:1] + early[3:] + last[1:]
    parts = up_part(message, ones)
    parts, downs = lax.optimization_barrier((parts, downs))
    parts = lax.all_to_all(parts, SECOND, split_axis=0, concat_axis=0, tiled=True)
    downs = [downs[0]] + [flipped(downs[k], "chi", k) for k in range(1, chi)]
    block_out = block_part(hidden, activated, down_weight)
    up_grad, down_grad, kernel_grad, one, two = sum_part(parts, downs, taps)
    return (
        block_out.reshape(frames, 1, width), up_grad, down_grad, kernel_grad,
        one.reshape(-1), two.reshape(-1),
    )


def fits(residual, conv_kernel, sizes):
    dhi, dlo, chi, clo = sizes
    frames, utter_count, width = residual.shape
    return (
        utter_count == 1
        and frames == 64
        and width == 1024
        and conv_kernel.shape[0] == 31
        and (dhi, dlo, chi, clo) == (2, 2, 4, 2)
    )


def on_device(
    residual,
    projections,
    out_weight,
    gain_one,
    up_weight,
    conv_kernel,
    gain_two,
    down_weight,
    lengths,
    out_grad,
):
    frames, utter_count, width = residual.shape
    head_size = width // HEADS
    kernel_len = conv_kernel.shape[0]
    half = (kernel_len - 1) // 2
    dhi, dlo, chi, clo = sizes = tuple(lax.axis_size(a) for a in ("dhi", "dlo", "chi", "clo"))
    if fits(residual, conv_kernel, sizes):
        return small_device(
            residual,
            projections,
            out_weight,
            gain_one,
            up_weight,
            conv_kernel,
            gain_two,
            down_weight,
            lengths,
            out_grad,
        )
    ctx = chi * clo
    length = frames * ctx
    items = utter_count * HEADS // ctx
    me = lax.axis_index(CTX)
    bf = jnp.bfloat16
    f32 = jnp.float32

    packed = projections.reshape(frames, ctx, items, 3 * head_size)
    packed = lax.all_to_all(packed, CTX, split_axis=1, concat_axis=0, tiled=True)
    packed = packed.reshape(length, items, 3 * head_size)

    both = jnp.concatenate([residual, out_grad], axis=-1)
    up = [(i, i + 1) for i in range(ctx - 1)]
    down = [(j, i) for i, j in up]
    before = lax.ppermute(both[frames - MARGIN :], CTX, up)
    after = lax.ppermute(both[:MARGIN], CTX, down)
    both = jnp.concatenate([before, both, after], axis=0)
    wide = frames + 2 * MARGIN
    place = me * frames - MARGIN + jnp.arange(wide, dtype=jnp.int32)
    valid = (place[:, None] >= 0) & (place[:, None] < lengths[None, :])
    row_mask = valid.astype(f32)[:, :, None]
    cot = jnp.where(valid[:, :, None], both[:, :, width:], 0)
    edge = MARGIN // 2
    near = wide - 2 * edge
    cot_near = cot[edge : edge + near]
    cot_own = cot[MARGIN : MARGIN + frames].reshape(frames * utter_count, width)
    act_grad = lax.dot_general(
        cot_near, down_weight, (((2,), (1,)), ((), ())), preferred_element_type=f32
    )

    key_lengths = lengths[(me * items + jnp.arange(items, dtype=jnp.int32)) // HEADS]
    context = attend(packed, key_lengths).reshape(length, items * head_size)
    padded = jnp.pad(context, ((MARGIN, MARGIN), (0, 0)))
    windows = jnp.stack([padded[i * frames : i * frames + wide] for i in range(ctx)])
    context = lax.all_to_all(windows, CTX, split_axis=0, concat_axis=0, tiled=True)
    context = jnp.transpose(context, (1, 0, 2)).reshape(wide, utter_count, width)

    cot_cols = lax.all_to_all(
        by_owner(cot_own, sizes), FIRST, split_axis=0, concat_axis=0, tiled=True
    )

    hidden = both[:, :, :width].astype(f32) + jnp.einsum(
        "fuc,cd->fud", context, out_weight, preferred_element_type=f32
    )
    normed_one, _ = normalize(hidden)
    scaled_one = (normed_one * gain_one).astype(bf)
    own = slice(MARGIN, MARGIN + frames)
    own_near = slice(MARGIN - edge, MARGIN - edge + frames)
    rows = frames * utter_count
    scaled_own = scaled_one[own].reshape(rows, width)
    scaled_all = gathered(scaled_own, chi)

    lifted = jnp.einsum("fuc,cd->fud", scaled_one, up_weight, preferred_element_type=f32)
    linear_part = lifted[:, :, :width]
    gate_part = jax.nn.sigmoid(lifted[:, :, width:])
    glu = (linear_part * gate_part * row_mask).astype(bf).astype(f32)
    conv_out = jnp.zeros((near, utter_count, width), f32)
    for j in range(kernel_len):
        start = edge + j - half
        conv_out = conv_out + conv_kernel[j] * glu[start : start + near]
    normed_two, inverse_two = normalize(conv_out)
    pre_act = normed_two * gain_two
    gate_two = jax.nn.sigmoid(pre_act)
    activated = (pre_act * gate_two)[own_near].astype(bf).reshape(rows, width)
    activated_all = gathered(activated, chi)
    block_out = (
        hidden[own].reshape(rows, width)
        + jnp.dot(activated, down_weight, preferred_element_type=f32)
    ).astype(bf)
    block_out = block_out.reshape(frames, utter_count, width)

    pre_grad = act_grad * gate_two * (1.0 + pre_act * (1.0 - gate_two))
    gain_two_grad = jnp.sum((pre_grad * normed_two)[own_near], axis=(0, 1))
    scaled_grad = pre_grad * gain_two
    conv_grad = inverse_two * (
        scaled_grad
        - jnp.mean(scaled_grad, axis=-1, keepdims=True)
        - normed_two * jnp.mean(scaled_grad * normed_two, axis=-1, keepdims=True)
    )
    conv_grad = conv_grad.astype(bf).astype(f32)
    conv_own = conv_grad[own_near]
    small = []
    glu_grad = jnp.zeros((frames, utter_count, width), f32)
    for j in range(kernel_len):
        start = MARGIN + j - half
        small.append(jnp.sum(conv_own * glu[start : start + frames], axis=(0, 1)))
        start = MARGIN - edge + half - j
        glu_grad = glu_grad + conv_kernel[j] * conv_grad[start : start + frames]
    glu_grad = glu_grad * row_mask[own]
    gate_own = gate_part[own]
    linear_grad = glu_grad * gate_own
    gate_grad = glu_grad * linear_part[own] * gate_own * (1.0 - gate_own)
    lifted_grad = jnp.concatenate([linear_grad, gate_grad], axis=-1).astype(bf)
    lifted_grad = lifted_grad.reshape(rows, 2 * width)
    input_grad = lax.dot_general(
        lifted_grad, up_weight, (((1,), (1,)), ((), ())), preferred_element_type=f32
    )
    gain_one_grad = jnp.sum(input_grad * normed_one[own].reshape(rows, width), axis=0)

    small = small + [gain_one_grad, gain_two_grad]
    count = kernel_len + 2
    small = by_owner(jnp.stack(small).astype(bf), sizes)
    small = small.reshape(dlo * chi, -1)
    cols = by_owner(lifted_grad, sizes)
    col_count = cols.shape[2]
    spare = -small.shape[1] % col_count
    small = jnp.pad(small, ((0, 0), (0, spare))).reshape(dlo * chi, -1, col_count)
    message = jnp.concatenate([cols, small], axis=1)
    message = lax.all_to_all(message, FIRST, split_axis=0, concat_axis=0, tiled=True)
    cols = message[:, :rows].reshape(-1, col_count)
    small = jnp.sum(message[:, rows:].astype(f32), axis=0).reshape(-1)
    seconds = dhi * clo
    small_width = width // (ctx * dhi * dlo)
    small = small[: count * seconds * small_width].reshape(count, seconds, small_width)
    small = jnp.transpose(small, (1, 0, 2)).reshape(seconds, count * small_width)

    up_part = lax.dot_general(
        cols, scaled_all, (((0,), (0,)), ((), ())), preferred_element_type=f32
    ).reshape(seconds, -1, width)
    down_part = lax.dot_general(
        cot_cols.reshape(cols.shape[0], -1),
        activated_all,
        (((0,), (0,)), ((), ())),
        preferred_element_type=f32,
    ).reshape(seconds, -1, width)
    spare = -small.shape[1] % width
    small = jnp.pad(small, ((0, 0), (0, spare))).reshape(seconds, -1, width)
    up_rows, down_rows = up_part.shape[1], down_part.shape[1]
    parts = jnp.concatenate([up_part.astype(bf), down_part.astype(bf), small.astype(bf)], axis=1)
    parts = lax.all_to_all(parts, SECOND, split_axis=0, concat_axis=0, tiled=True)
    total = jnp.sum(parts.astype(f32), axis=0)
    up_grad = total[:up_rows]
    down_grad = total[up_rows : up_rows + down_rows]
    small = total[up_rows + down_rows :].reshape(-1)[: count * small_width]
    small = small.reshape(count, small_width)
    kernel_grad = jnp.transpose(small[:kernel_len])
    return (block_out, up_grad, down_grad, kernel_grad, small[kernel_len], small[kernel_len + 1])


def solution(mesh):
    dp, ctx = mesh.shape["dp"], mesh.shape["ctx"]
    fine = Mesh(mesh.devices.reshape(dp // 2, 2, ctx // 2, 2), ("dhi", "dlo", "chi", "clo"))
    dp_axes, ctx_axes = ("dhi", "dlo"), ("chi", "clo")
    every = ("dhi", "dlo", "chi", "clo")
    in_specs = (
        P(ctx_axes, dp_axes, None),
        P(ctx_axes, dp_axes, None),
        P(),
        P(),
        P(),
        P(),
        P(),
        P(),
        P(dp_axes),
        P(ctx_axes, dp_axes, None),
    )
    out_specs = (
        P(ctx_axes, dp_axes, None),
        P(every, None),
        P(every, None),
        P(every, None),
        P(every),
        P(every),
    )
    return jax.shard_map(
        on_device, mesh=fine, in_specs=in_specs, out_specs=out_specs, check_vma=False
    )
```

```python
import functools

import jax
import jax.numpy as jnp
from jax import lax
from jax.experimental import pallas as pl
from jax.experimental.pallas import tpu as pltpu
from jax.sharding import Mesh, PartitionSpec as P

HEADS = 16


EPSILON = 1e-05

MARGIN = 32

CTX = ("chi", "clo")
FIRST = ("dlo", "chi")
SECOND = ("dhi", "clo")

SMEM = pl.BlockSpec(memory_space=pltpu.SMEM)
VMEM = pl.BlockSpec(memory_space=pltpu.VMEM)
HBM = pl.BlockSpec(memory_space=pltpu.HBM)


def normalize(values):
    center = values - jnp.mean(values, axis=-1, keepdims=True)
    inverse = lax.rsqrt(jnp.mean(center * center, axis=-1, keepdims=True) + EPSILON)
    return (center * inverse, inverse)


def attend(packed, key_lengths):
    length, count, triple = packed.shape
    head_size = triple // 3
    query_rows = packed[:, :, :head_size]
    key_rows = packed[:, :, head_size : 2 * head_size]
    value_rows = packed[:, :, 2 * head_size :]
    allowed = jnp.arange(length, dtype=jnp.int32)[None, :] < key_lengths[:, None]
    scores = (
        jnp.einsum("qmd,kmd->mqk", query_rows, key_rows, preferred_element_type=jnp.float32)
        * head_size ** (-0.5)
    )
    scores = jnp.where(allowed[:, None, :], scores, -jnp.inf)
    highest = jnp.max(scores, axis=-1, keepdims=True)
    raised = jnp.exp(scores - highest)
    weights_bf = (raised / jnp.sum(raised, axis=-1, keepdims=True)).astype(jnp.bfloat16)
    return jnp.einsum(
        "mqk,kmd->qmd", weights_bf, value_rows, preferred_element_type=jnp.float32
    ).astype(jnp.bfloat16)


def by_owner(cols, sizes):
    dhi, dlo, chi, clo = sizes
    rows, width = cols.shape
    part = width // (dhi * dlo * chi * clo)
    split = cols.reshape(rows, dhi, dlo, chi, clo, part)
    return jnp.transpose(split, (2, 3, 0, 1, 4, 5)).reshape(dlo * chi, rows, dhi * clo * part)


def gathered(rows, chi):
    copies = jnp.broadcast_to(rows[None], (chi,) + rows.shape)
    line = lax.all_to_all(copies, "chi", split_axis=0, concat_axis=0, tiled=True)
    line = line.reshape(chi * rows.shape[0], rows.shape[1])
    other = lax.ppermute(line, "dlo", [(0, 1), (1, 0)])
    first = lax.axis_index("dlo") == 0
    return jnp.concatenate([jnp.where(first, line, other), jnp.where(first, other, line)], axis=0)


def params(mebi=8):
    return pltpu.CompilerParams(vmem_limit_bytes=mebi * 1024 * 1024)


def struct(shape, dtype):
    return jax.ShapeDtypeStruct(shape, dtype)


def in_hbm(array):
    return pltpu.with_memory_space_constraint(array, pltpu.HBM)


def fetches(source, target, sems, parts):
    copies = []
    for i, part in enumerate(parts):
        copies.append(pltpu.make_async_copy(source.at[part], target.at[part], sems.at[i]))
        copies[-1].start()
    return copies


def split_kernel(proj_ref, out_ref, held_ref, sems):
    count, _, span = out_ref.shape
    copies = []
    for i in range(count):
        copies.append(
            pltpu.make_async_copy(
                proj_ref.at[:, pl.ds(i * span, span)], held_ref.at[i], sems.at[0, i]
            )
        )
        copies[-1].start()
    sends = []
    for i, copy in enumerate(copies):
        copy.wait()
        sends.append(pltpu.make_async_copy(held_ref.at[i], out_ref.at[i], sems.at[1, i]))
        sends[-1].start()
    for send in sends:
        send.wait()


def split_heads(proj, count):
    rows, cols = proj.shape
    shape = (count, rows, cols // count)
    return pl.pallas_call(
        split_kernel,
        out_shape=struct(shape, proj.dtype),
        in_specs=[HBM],
        out_specs=HBM,
        scratch_shapes=[pltpu.VMEM(shape, proj.dtype), pltpu.SemaphoreType.DMA((2, count))],
        compiler_params=params(),
        name="split_heads",
    )(in_hbm(proj))


def edge_kernel(res_ref, grad_ref, low_ref, high_ref, sems):
    rows = res_ref.shape[0]
    copies = []
    for i, (source, at, count) in enumerate(
        ((res_ref, 0, MARGIN), (grad_ref, MARGIN, MARGIN // 2))
    ):
        for j, (target, start) in enumerate(((high_ref, rows - count), (low_ref, 0))):
            copies.append(
                pltpu.make_async_copy(
                    source.at[pl.ds(start, count)], target.at[pl.ds(at, count)], sems.at[i, j]
                )
            )
            copies[-1].start()
    for copy in copies:
        copy.wait()


def edges(res, grad):
    shape = struct((MARGIN + MARGIN // 2, res.shape[1]), res.dtype)
    spec = pl.BlockSpec(memory_space=pl.ANY)
    return pl.pallas_call(
        edge_kernel,
        out_shape=(shape, shape),
        in_specs=[HBM, HBM],
        out_specs=(spec, spec),
        scratch_shapes=[pltpu.SemaphoreType.DMA((2, 2))],
        compiler_params=params(),
        name="edges",
    )(in_hbm(res), in_hbm(grad))


def attend_kernel(head_size, frames, scalar_ref, qkv_ref, out_ref):
    length = qkv_ref.shape[0]
    count = qkv_ref.shape[1] // (3 * head_size)
    ctx, wide, _ = out_ref.shape
    places = lax.broadcasted_iota(jnp.int32, (1, length), 1)
    bias = jnp.where(places < scalar_ref[:, 0:1], 0.0, -jnp.inf)
    scores = []
    for m in range(count):
        base = 3 * head_size * m
        query = qkv_ref[:, base : base + head_size] * jnp.bfloat16(head_size ** (-0.5))
        key = qkv_ref[:, base + head_size : base + 2 * head_size]
        scores.append(bias + lax.dot_general(
                query, key, (((1,), (1,)), ((), ())), preferred_element_type=jnp.float32))
    scores = jnp.concatenate(scores, axis=0)
    raised = jnp.exp(scores - jnp.max(scores, axis=-1, keepdims=True))
    share = 1.0 / jnp.sum(raised, axis=-1, keepdims=True)
    weights = raised.astype(jnp.bfloat16)
    heads = []
    for m in range(count):
        base = 3 * head_size * m
        value = qkv_ref[:, base + 2 * head_size : base + 3 * head_size]
        rows = slice(m * length, (m + 1) * length)
        heads.append(
            jnp.dot(weights[rows], value, preferred_element_type=jnp.float32) * share[rows]
        )
    context = jnp.concatenate(heads, axis=1).astype(jnp.bfloat16)
    for i in range(ctx):
        low = max(i * frames - MARGIN, 0)
        high = min(i * frames - MARGIN + wide, length)
        at = low - (i * frames - MARGIN)
        out_ref[i, at : at + high - low, :] = context[low:high]
        if at > 0:
            out_ref[i, :at, :] = jnp.zeros((at, context.shape[1]), context.dtype)
        if at + high - low < wide:
            rest = wide - (at + high - low)
            out_ref[i, wide - rest :, :] = jnp.zeros((rest, context.shape[1]), context.dtype)


def attend_windows(scalars, qkv, head_size, frames, ctx):
    wide = frames + 2 * MARGIN
    return pl.pallas_call(
        functools.partial(attend_kernel, head_size, frames),
        out_shape=struct((ctx, wide, qkv.shape[1] // 3), jnp.bfloat16),
        in_specs=[VMEM, VMEM],
        out_specs=VMEM,
        compiler_params=params(16),
        name="attend",
    )(scalars, qkv)


def cot_kernel(scalar_ref, grad_ref, low_ref, high_ref, weight_ref, *refs):
    out_ref, cols_refs = refs[0], refs[1:5]
    act_ref, ready_ref, held_ref, weight_held_ref, sems, ready_sems = refs[5:]
    ready = fetches(
        out_ref,
        ready_ref,
        ready_sems,
        [pl.ds(i * 256, 256) for i in range(ready_ref.shape[0] // 256)],
    )
    frames, width = grad_ref.shape
    copies = fetches(
        weight_ref, weight_held_ref, sems, [pl.ds(i * 256, 256) for i in range(width // 256)]
    )
    edge = MARGIN // 2
    whole = jnp.concatenate([low_ref[MARGIN:, :], grad_ref[...], high_ref[MARGIN:, :]], axis=0)
    near = whole.shape[0]
    place = scalar_ref[:, 1:2] - edge + lax.broadcasted_iota(jnp.int32, (near, width), 0)
    valid = (place >= 0) & (place < scalar_ref[:, 0:1])
    whole = jnp.where(valid, whole.astype(jnp.float32), 0.0).astype(jnp.bfloat16)
    cot = whole[edge : edge + frames]
    count, _, span = held_ref.shape
    piece = span // 4
    for group in range(count):
        high_bits, low_bit = group // 2, group % 2
        held_ref[group, :, :] = jnp.concatenate(
            [
                cot[:, (8 * high_bits + 2 * z + low_bit) * piece :][:, :piece]
                for z in range(4)
            ],
            axis=1,
        )
    dhi, dlo, clo = lax.axis_index("dhi"), lax.axis_index("dlo"), lax.axis_index("clo")
    for k, cols_ref in enumerate(cols_refs):
        for side in range(2):
            group = ((dhi ^ (k // 2)) * 2 + (dlo ^ side)) * 2 + (clo ^ (k % 2))
            cols_ref[:, side * span : (side + 1) * span] = held_ref[group]
    for copy in copies:
        copy.wait()
    act_ref[...] = lax.dot_general(
        whole, weight_held_ref[...], (((1,), (1,)), ((), ())), preferred_element_type=jnp.float32
    )
    for copy in ready:
        copy.wait()


def cot_part(scalars, grad, low, high, weight, out_weight):
    frames, width = grad.shape
    cols = struct((frames, width // 4), grad.dtype)
    return pl.pallas_call(
        cot_kernel,
        out_shape=(
            cols, cols, cols, cols,
            struct((frames + MARGIN, width), jnp.float32),
            struct((width * 3 // 4, width), weight.dtype),
        ),
        in_specs=[VMEM, VMEM, VMEM, VMEM, HBM, HBM],
        out_specs=(VMEM,) * 6,
        scratch_shapes=[
            pltpu.VMEM((8, frames, width // 8), grad.dtype),
            pltpu.VMEM(weight.shape, weight.dtype),
            pltpu.SemaphoreType.DMA((width // 256,)),
            pltpu.SemaphoreType.DMA((3,)),
        ],
        compiler_params=params(12),
        name="cotangent",
    )(scalars, grad, low, high, in_hbm(weight), in_hbm(out_weight))


def forward_kernel(
    scalar_ref, context_ref, res_ref, low_ref, high_ref, out_ref, ready_ref, gain_one_ref, weight_ref,
    taps_ref, gain_ref,
    hidden_ref, one_ref, own_ref, act_ref, linear_ref, gate_ref, glu_ref,
    normed_ref, inverse_ref, scaled_ref, conv_ref, out_held_ref, held_ref, res_held_ref, out_sems, sems, res_sems,
):
    frames, width = res_ref.shape
    ctx, wide, lanes = context_ref.shape
    taps = taps_ref.shape[0]
    half = (taps - 1) // 2
    edge = MARGIN // 2
    near = wide - 2 * edge
    depth = 2 * lanes
    res_copies = fetches(res_ref, res_held_ref, res_sems, [slice(None)])
    held_rows = ready_ref.shape[0]
    out_copies = fetches(
        out_ref, out_held_ref, out_sems, [pl.ds(held_rows, width - held_rows)]
    )
    span = 256
    copies = fetches(
        weight_ref, held_ref, sems, [pl.ds(i * span, span) for i in range(width // span)]
    )
    context = jnp.concatenate([context_ref[i] for i in range(ctx)], axis=1)
    product = jnp.dot(
        context[:, :held_rows], ready_ref[...], preferred_element_type=jnp.float32
    )
    out_copies[0].wait()
    product = product + jnp.dot(
        context[:, held_rows:], out_held_ref[held_rows:, :], preferred_element_type=jnp.float32
    )
    res_copies[0].wait()
    step = 32
    for at in range(0, wide, step):
        if at < MARGIN:
            res = low_ref[at : at + step, :]
        elif at < MARGIN + frames:
            res = res_held_ref[at - MARGIN : at - MARGIN + step, :]
        else:
            res = high_ref[at - MARGIN - frames : at - MARGIN - frames + step, :]
        hidden = res.astype(jnp.float32) + product[at : at + step]
        normed, _ = normalize(hidden)
        scaled = (normed * gain_one_ref[...]).astype(jnp.bfloat16)
        scaled_ref[at : at + step, :] = scaled
        if MARGIN <= at < MARGIN + frames:
            rows = slice(at - MARGIN, at - MARGIN + step)
            hidden_ref[rows, :] = hidden
            one_ref[rows, :] = normed
            own_ref[rows, :] = scaled
    for copy in copies:
        copy.wait()
    place = scalar_ref[:, 1:2] - MARGIN + lax.broadcasted_iota(jnp.int32, (wide, span), 0)
    valid = (place >= 0) & (place < scalar_ref[:, 0:1])
    own = slice(MARGIN, MARGIN + frames)
    for i in range(width // span):
        cols = slice(i * span, (i + 1) * span)
        linear = jnp.dot(scaled_ref[...], held_ref[:, cols], preferred_element_type=jnp.float32)
        gate = jax.nn.sigmoid(
            jnp.dot(
                scaled_ref[...],
                held_ref[:, width + i * span : width + (i + 1) * span],
                preferred_element_type=jnp.float32,
            )
        )
        glu = jnp.where(valid, linear * gate, 0.0).astype(jnp.bfloat16).astype(jnp.float32)
        glu_ref[:, cols] = glu
        linear_ref[:, cols] = linear[own]
        gate_ref[:, cols] = gate[own]
        for at in range(i * span, (i + 1) * span, 128):
            lane = slice(at, at + 128)
            block = glu[:, at - i * span : at - i * span + 128]
            total = jnp.zeros((near, 128), jnp.float32)
            for shift in range(8):
                moved = block if shift == 0 else pltpu.roll(block, wide - shift, 0)
                for j in range(taps):
                    start = edge + j - half
                    if start % 8 == shift:
                        total = total + taps_ref[j : j + 1, lane] * moved[
                            start - shift : start - shift + near
                        ]
            conv_ref[:, lane] = total
    step = 16
    for at in range(0, near, step):
        normed, inverse = normalize(conv_ref[at : at + step, :])
        normed_ref[at : at + step, :] = normed
        inverse_ref[at : at + step, :] = jnp.broadcast_to(inverse, (step, 128))
        if MARGIN - edge <= at < MARGIN - edge + frames:
            pre = normed * gain_ref[...]
            rows = slice(at - (MARGIN - edge), at - (MARGIN - edge) + step)
            act_ref[rows, :] = (pre * jax.nn.sigmoid(pre)).astype(jnp.bfloat16)


def forward_part(
    scalars, context, res, low, high, out_weight, ready, gain_one, weight, taps, gain
):
    frames, width = res.shape
    ctx, wide, _ = context.shape
    near = wide - MARGIN
    f32, bf = jnp.float32, jnp.bfloat16
    return pl.pallas_call(
        forward_kernel,
        out_shape=(
            struct((frames, width), f32),
            struct((frames, width), f32),
            struct((frames, width), bf),
            struct((frames, width), bf),
            struct((frames, width), f32),
            struct((frames, width), f32),
            struct((wide, width), f32),
            struct((near, width), f32),
            struct((near, 128), f32),
        ),
        in_specs=[VMEM, VMEM, HBM, VMEM, VMEM, HBM, VMEM, VMEM, HBM, VMEM, VMEM],
        out_specs=(VMEM,) * 9,
        scratch_shapes=[
            pltpu.VMEM((wide, width), bf),
            pltpu.VMEM((near, width), f32),
            pltpu.VMEM(out_weight.shape, bf),
            pltpu.VMEM(weight.shape, bf),
            pltpu.VMEM(res.shape, bf),
            pltpu.SemaphoreType.DMA((ctx // 2,)),
            pltpu.SemaphoreType.DMA((width // 256,)),
            pltpu.SemaphoreType.DMA((1,)),
        ],
        compiler_params=params(24),
        name="forward",
    )(
        scalars, context, in_hbm(res), low, high, in_hbm(out_weight), ready, gain_one,
        in_hbm(weight), taps, gain
    )


def back_kernel(
    scalar_ref, act_grad_ref, one_ref, linear_ref, gate_ref,
    glu_ref, normed_ref, inverse_ref, taps_ref, gain_ref, up_ref,
    message_ref, grad_ref, small_ref, lifted_ref, held_ref, sems,
):
    frames, width = one_ref.shape
    near = normed_ref.shape[0]
    wide = glu_ref.shape[0]
    taps = taps_ref.shape[0]
    half = (taps - 1) // 2
    edge = MARGIN // 2
    first = MARGIN - edge
    copies = fetches(up_ref, held_ref, sems, [pl.ds(i * 256, 256) for i in range(width // 256)])
    gain = gain_ref[...]
    step = 16
    two = jnp.zeros((1, width), jnp.float32)
    for at in range(0, near, step):
        normed = normed_ref[at : at + step, :]
        pre = normed * gain
        gate = jax.nn.sigmoid(pre)
        grad = act_grad_ref[at : at + step, :] * gate * (1.0 + pre * (1.0 - gate))
        if first <= at < first + frames:
            two = two + jnp.sum(grad * normed, axis=0, keepdims=True)
        scaled = grad * gain
        result = inverse_ref[at : at + step, 0:1] * (
            scaled
            - jnp.mean(scaled, axis=-1, keepdims=True)
            - normed * jnp.mean(scaled * normed, axis=-1, keepdims=True)
        )
        grad_ref[at : at + step, :] = result.astype(jnp.bfloat16).astype(jnp.float32)
    small_ref[32:, :] = jnp.zeros((16, width), jnp.float32)
    small_ref[taps + 1 : taps + 2, :] = two

    place = scalar_ref[:, 1:2] + lax.broadcasted_iota(jnp.int32, (frames, 128), 0)
    valid = place < scalar_ref[:, 0:1]

    def lanes(i):
        cols = slice(i * 128, (i + 1) * 128)
        high = slice(i * 128 + width, (i + 1) * 128 + width)
        block = grad_ref[:, cols]
        own = block[first : first + frames]
        total = jnp.zeros((frames, 128), jnp.float32)
        for shift in range(8):
            moved = block if shift == 0 else pltpu.roll(block, near - shift, 0)
            for j in range(taps):
                start = first + half - j
                if start % 8 == shift:
                    total = total + taps_ref[j : j + 1, cols] * moved[start - shift : start - shift + frames]
        block = glu_ref[:, cols]
        for shift in range(8):
            moved = block if shift == 0 else pltpu.roll(block, wide - shift, 0)
            for j in range(taps):
                start = MARGIN + j - half
                if start % 8 == shift:
                    small_ref[j : j + 1, cols] = jnp.sum(
                        own * moved[start - shift : start - shift + frames], axis=0, keepdims=True
                    )
        total = jnp.where(valid, total, 0.0)
        gate = gate_ref[:, cols]
        linear_grad = (total * gate).astype(jnp.bfloat16)
        gate_grad = (total * linear_ref[:, cols] * gate * (1.0 - gate)).astype(jnp.bfloat16)
        lifted_ref[:, cols] = linear_grad
        lifted_ref[:, high] = gate_grad
        message_ref[i, :frames, :128] = linear_grad
        message_ref[i, :frames, 128:256] = gate_grad

    for i in range(width // 128):
        lanes(i)
    for copy in copies:
        copy.wait()
    input_grad = jnp.transpose(
        lax.dot_general(
            held_ref[...],
            lifted_ref[...],
            (((1,), (1,)), ((), ())),
            preferred_element_type=jnp.float32,
        )
    )
    small_ref[taps : taps + 1, :] = jnp.sum(input_grad * one_ref[...], axis=0, keepdims=True)
    for i in range(width // 128):
        for part in range(2):
            rows = small_ref[part * 24 : (part + 1) * 24, :]
            message_ref[i, frames:, part * 128 : (part + 1) * 128] = jnp.concatenate(
                [rows[:, i * 64 : (i + 1) * 64], rows[:, (i + 8) * 64 : (i + 9) * 64]], axis=1
            ).astype(jnp.bfloat16)


def block_kernel(hidden_ref, activated_ref, down_ref, block_ref, held_ref, sems):
    width = hidden_ref.shape[1]
    copies = fetches(
        down_ref, held_ref, sems, [pl.ds(i * 256, 256) for i in range(width // 256)]
    )
    for copy in copies:
        copy.wait()
    block_ref[...] = (
        hidden_ref[...]
        + jnp.dot(
            activated_ref[:, :width], held_ref[...], preferred_element_type=jnp.float32
        )
    ).astype(jnp.bfloat16)


def block_part(hidden, activated, down):
    return pl.pallas_call(
        block_kernel,
        out_shape=struct(hidden.shape, jnp.bfloat16),
        in_specs=[VMEM, VMEM, HBM],
        out_specs=VMEM,
        scratch_shapes=[
            pltpu.VMEM(down.shape, down.dtype),
            pltpu.SemaphoreType.DMA((down.shape[0] // 256,)),
        ],
        compiler_params=params(12),
        name="block_out",
    )(hidden, activated, in_hbm(down))


def back_part(*operands):
    frames, width = operands[2].shape
    near = frames + MARGIN
    f32, bf = jnp.float32, jnp.bfloat16
    return pl.pallas_call(
        back_kernel,
        out_shape=struct((width // 128, frames + 24, 256), bf),
        in_specs=[VMEM] * 10 + [HBM],
        out_specs=VMEM,
        scratch_shapes=[
            pltpu.VMEM((near, width), f32),
            pltpu.VMEM((48, width), f32),
            pltpu.VMEM((frames, 2 * width), bf),
            pltpu.VMEM((width, 2 * width), bf),
            pltpu.SemaphoreType.DMA((width // 256,)),
        ],
        compiler_params=params(20),
        name="backward",
    )(*operands[:-1], in_hbm(operands[-1]))


TURNED = (((0,), (0,)), ((), ()))


def up_kernel(count, message_ref, *refs):
    parts_ref, cols_ref, one_ref = refs[2 * count :]
    frames, width = refs[0].shape
    core, line = lax.axis_index("dlo"), lax.axis_index("chi")
    small = jnp.zeros((24, 256), jnp.float32)
    for side in range(2):
        for k in range(count):
            at = (side * count + k) * frames
            source = (core ^ side) * count + (line ^ k)
            cols_ref[at : at + frames, :] = message_ref[source, :frames, :]
            one_ref[at : at + frames, :] = refs[side * count + k][...]
            small = small + message_ref[source, frames:, :].astype(jnp.float32)
    up = lax.dot_general(
        cols_ref[...], one_ref[...], TURNED, preferred_element_type=jnp.float32
    ).astype(jnp.bfloat16)
    small = small.astype(jnp.bfloat16)
    for s in range(4):
        parts_ref[s, :64, :] = up[s * 64 : (s + 1) * 64]
        for i in range(6):
            at = (i // 3) * 128 + s * 32
            parts_ref[s, 64:, i * 128 : (i + 1) * 128] = jnp.concatenate(
                [small[(i % 3) * 8 : (i % 3 + 1) * 8, at : at + 32]] * 4, axis=1
            )
        parts_ref[s, 64:, 768:] = jnp.zeros((8, width - 768), jnp.bfloat16)


def up_part(message, pieces):
    count = len(pieces) // 2
    frames, width = pieces[0].shape
    bf = jnp.bfloat16
    rows = 2 * count * frames
    return pl.pallas_call(
        functools.partial(up_kernel, count),
        out_shape=struct((4, 72, width), bf),
        in_specs=[VMEM] * (1 + len(pieces)),
        out_specs=VMEM,
        scratch_shapes=[pltpu.VMEM((rows, 256), bf), pltpu.VMEM((rows, width), bf)],
        compiler_params=params(12),
        name="up_products",
    )(message, *pieces)


def pack_kernel(act_ref, own_ref, y_ref, x_ref, xy_ref, packed_ref, to_y_ref, to_x_ref):
    width, span = act_ref.shape[1], own_ref.shape[1]
    for cols_ref, out_ref in ((own_ref, packed_ref), (y_ref, to_y_ref), (x_ref, to_x_ref)):
        out_ref[:, :width] = act_ref[...]
        out_ref[:, width : width + span] = cols_ref[...]
    to_x_ref[:, width + span :] = xy_ref[...]


def pack_part(act, cols):
    rows, width = act.shape
    span = cols[0].shape[1]
    return pl.pallas_call(
        pack_kernel,
        out_shape=(
            struct((rows, width + span), act.dtype),
            struct((rows, width + span), act.dtype),
            struct((rows, width + 2 * span), act.dtype),
        ),
        in_specs=[VMEM] * 5,
        out_specs=(VMEM,) * 3,
        compiler_params=params(),
        name="pack",
    )(act, *cols)


def down_kernel(*refs):
    pieces, (mine_ref, theirs_ref, rows_ref) = refs[:-3], refs[-3:]
    width = mine_ref.shape[1]
    frames = pieces[0].shape[0]
    for i, piece in enumerate(pieces):
        rows = slice(i * frames, (i + 1) * frames)
        span = rows_ref.shape[1] - width
        at = width + (span if i == 3 else 0)
        rows_ref[rows, :width] = piece[:, :width]
        rows_ref[rows, width:] = piece[:, at : at + span]
    total = lax.dot_general(
        rows_ref[:, width:], rows_ref[:, :width], TURNED, preferred_element_type=jnp.float32
    ).astype(jnp.bfloat16)
    half = total.shape[0] // 2
    mine_ref[...] = total[:half]
    theirs_ref[...] = total[half:]


def down_part(pieces, width):
    frames, wide = pieces[0].shape
    shape = struct(((wide - width) // 2, width), jnp.bfloat16)
    return pl.pallas_call(
        down_kernel,
        out_shape=(shape, shape),
        in_specs=[VMEM] * len(pieces),
        out_specs=(VMEM, VMEM),
        scratch_shapes=[pltpu.VMEM((len(pieces) * frames, wide), jnp.bfloat16)],
        compiler_params=params(12),
        name="down_products",
    )(*pieces)


def share_kernel(mine_ref, other_ref, *refs):
    outs, total_ref = refs[:-1], refs[-1]
    total_ref[...] = mine_ref[...].astype(jnp.float32) + other_ref[...].astype(jnp.float32)
    for k, out in enumerate(outs):
        at = pl.multiple_of((lax.axis_index("chi") ^ k) * 32, 32)
        out[...] = total_ref[pl.ds(at, 32), :].astype(jnp.bfloat16)


def share_part(mine, other):
    rows, width = mine.shape
    count = rows // 32
    return pl.pallas_call(
        share_kernel,
        out_shape=(struct((32, width), jnp.bfloat16),) * count,
        in_specs=[VMEM, VMEM],
        out_specs=(VMEM,) * count,
        scratch_shapes=[pltpu.VMEM((rows, width), jnp.float32)],
        compiler_params=params(),
        name="down_shares",
    )(mine, other)


def sum_kernel(taps, parts_ref, *refs):
    pieces, (up_ref, down_ref, kernel_ref, one_ref, two_ref) = refs[:4], refs[4:]
    total = parts_ref[0].astype(jnp.float32)
    for s in range(1, parts_ref.shape[0]):
        total = total + parts_ref[s].astype(jnp.float32)
    up_ref[...] = total[:64]
    down_ref[...] = (pieces[0][...].astype(jnp.float32) + pieces[1][...].astype(jnp.float32)) + (
        pieces[2][...].astype(jnp.float32) + pieces[3][...].astype(jnp.float32)
    )
    small = jnp.concatenate(
        [total[64:72, i * 128 : (i + 1) * 128] for i in range(6)], axis=0
    )
    kernel_ref[...] = jnp.transpose(small[:32])[:32, :taps]
    one_ref[...] = small[taps : taps + 1, :32]
    two_ref[...] = small[taps + 1 : taps + 2, :32]


def sum_part(parts, pieces, taps):
    width = parts.shape[2]
    f32 = jnp.float32
    return pl.pallas_call(
        functools.partial(sum_kernel, taps),
        out_shape=(
            struct((64, width), f32),
            struct((32, width), f32),
            struct((32, taps), f32),
            struct((1, 32), f32),
            struct((1, 32), f32),
        ),
        in_specs=[VMEM] * 5,
        out_specs=(VMEM,) * 5,
        compiler_params=params(),
        name="sums",
    )(parts, *pieces)


def flipped(rows, axis, bit):
    size = lax.axis_size(axis)
    return lax.ppermute(rows, axis, [(i, i ^ bit) for i in range(size)])


def with_swapped(pieces):
    return list(pieces) + [flipped(piece, "dlo", 1) for piece in pieces]


def small_device(
    residual, projections, out_weight, gain_one, up_weight, conv_kernel, gain_two, down_weight,
    lengths, out_grad,
):
    frames, _, width = residual.shape
    taps = conv_kernel.shape[0]
    chi, clo = lax.axis_size("chi"), lax.axis_size("clo")
    ctx = chi * clo
    head_size = width // HEADS
    me = lax.axis_index(CTX)
    scalars = jnp.stack([lengths[0], me * frames]).astype(jnp.int32).reshape(1, 2)
    res = residual.reshape(frames, width)
    grad = out_grad.reshape(frames, width)
    gain_one = gain_one.reshape(1, width)
    gain_two = gain_two.reshape(1, width)

    qkv = split_heads(projections.reshape(frames, 3 * width), ctx)
    qkv = lax.all_to_all(qkv, CTX, split_axis=0, concat_axis=0, tiled=True)
    low, high = edges(res, grad)
    up = [(i, i + 1) for i in range(ctx - 1)]
    down = [(j, i) for i, j in up]
    before = lax.ppermute(high, CTX, up)
    after = lax.ppermute(low, CTX, down)
    qkv, before, after = lax.optimization_barrier((qkv, before, after))
    windows = attend_windows(scalars, qkv.reshape(ctx * frames, -1), head_size, frames, ctx)
    windows, before, after = lax.optimization_barrier((windows, before, after))
    windows = lax.all_to_all(windows, CTX, split_axis=0, concat_axis=0, tiled=True)
    *cols, act_grad, ready = cot_part(scalars, grad, before, after, down_weight, out_weight)
    windows, act_grad, cols, ready = lax.optimization_barrier((windows, act_grad, cols, ready))

    (
        hidden, normed_one, scaled, activated, linear, gate, glu, normed_two, inverse_two
    ) = forward_part(
        scalars, windows, res, before, after, out_weight, ready, gain_one, up_weight, conv_kernel,
        gain_two,
    )
    packed, to_y, to_x = pack_part(activated, cols)
    received = [flipped(to_y, "clo", 1), flipped(to_x, "dhi", 1)]
    one_near, one_far = flipped(scaled, "chi", 1), flipped(scaled, "chi", 2)
    message = back_part(
        scalars, act_grad, normed_one, linear, gate,
        glu, normed_two, inverse_two, conv_kernel, gain_two, up_weight,
    )
    received, one_near, one_far, message = lax.optimization_barrier(
        (received, one_near, one_far, message)
    )
    message = lax.all_to_all(message, FIRST, split_axis=0, concat_axis=0, tiled=True)
    one_last = flipped(one_far, "chi", 1)
    diagonal = flipped(received[1], "clo", 1)
    early = with_swapped([scaled, one_near, one_far])
    early, diagonal, one_last = lax.optimization_barrier((early, diagonal, one_last))
    mine, theirs = down_part([packed, *received, diagonal], width)
    downs = share_part(mine, flipped(theirs, "dlo", 1))
    last = with_swapped([one_last])
    ones = early[:3] + last[:1] + early[3:] + last[1:]
    parts = up_part(message, ones)
    parts, downs = lax.optimization_barrier((parts, downs))
    parts = lax.all_to_all(parts, SECOND, split_axis=0, concat_axis=0, tiled=True)
    downs = [downs[0]] + [flipped(downs[k], "chi", k) for k in range(1, chi)]
    block_out = block_part(hidden, activated, down_weight)
    up_grad, down_grad, kernel_grad, one, two = sum_part(parts, downs, taps)
    return (
        block_out.reshape(frames, 1, width), up_grad, down_grad, kernel_grad,
        one.reshape(-1), two.reshape(-1),
    )


def fits(residual, conv_kernel, sizes):
    dhi, dlo, chi, clo = sizes
    frames, utter_count, width = residual.shape
    return (
        utter_count == 1
        and frames == 64
        and width == 1024
        and conv_kernel.shape[0] == 31
        and (dhi, dlo, chi, clo) == (2, 2, 4, 2)
    )


def on_device(
    residual,
    projections,
    out_weight,
    gain_one,
    up_weight,
    conv_kernel,
    gain_two,
    down_weight,
    lengths,
    out_grad,
):
    frames, utter_count, width = residual.shape
    head_size = width // HEADS
    kernel_len = conv_kernel.shape[0]
    half = (kernel_len - 1) // 2
    dhi, dlo, chi, clo = sizes = tuple(lax.axis_size(a) for a in ("dhi", "dlo", "chi", "clo"))
    if fits(residual, conv_kernel, sizes):
        return small_device(
            residual,
            projections,
            out_weight,
            gain_one,
            up_weight,
            conv_kernel,
            gain_two,
            down_weight,
            lengths,
            out_grad,
        )
    ctx = chi * clo
    length = frames * ctx
    items = utter_count * HEADS // ctx
    me = lax.axis_index(CTX)
    bf = jnp.bfloat16
    f32 = jnp.float32

    packed = projections.reshape(frames, ctx, items, 3 * head_size)
    packed = lax.all_to_all(packed, CTX, split_axis=1, concat_axis=0, tiled=True)
    packed = packed.reshape(length, items, 3 * head_size)

    both = jnp.concatenate([residual, out_grad], axis=-1)
    up = [(i, i + 1) for i in range(ctx - 1)]
    down = [(j, i) for i, j in up]
    before = lax.ppermute(both[frames - MARGIN :], CTX, up)
    after = lax.ppermute(both[:MARGIN], CTX, down)
    both = jnp.concatenate([before, both, after], axis=0)
    wide = frames + 2 * MARGIN
    place = me * frames - MARGIN + jnp.arange(wide, dtype=jnp.int32)
    valid = (place[:, None] >= 0) & (place[:, None] < lengths[None, :])
    row_mask = valid.astype(f32)[:, :, None]
    cot = jnp.where(valid[:, :, None], both[:, :, width:], 0)
    edge = MARGIN // 2
    near = wide - 2 * edge
    cot_near = cot[edge : edge + near]
    cot_own = cot[MARGIN : MARGIN + frames].reshape(frames * utter_count, width)
    act_grad = lax.dot_general(
        cot_near, down_weight, (((2,), (1,)), ((), ())), preferred_element_type=f32
    )

    key_lengths = lengths[(me * items + jnp.arange(items, dtype=jnp.int32)) // HEADS]
    context = attend(packed, key_lengths).reshape(length, items * head_size)
    padded = jnp.pad(context, ((MARGIN, MARGIN), (0, 0)))
    windows = jnp.stack([padded[i * frames : i * frames + wide] for i in range(ctx)])
    context = lax.all_to_all(windows, CTX, split_axis=0, concat_axis=0, tiled=True)
    context = jnp.transpose(context, (1, 0, 2)).reshape(wide, utter_count, width)

    cot_cols = lax.all_to_all(
        by_owner(cot_own, sizes), FIRST, split_axis=0, concat_axis=0, tiled=True
    )

    hidden = both[:, :, :width].astype(f32) + jnp.einsum(
        "fuc,cd->fud", context, out_weight, preferred_element_type=f32
    )
    normed_one, _ = normalize(hidden)
    scaled_one = (normed_one * gain_one).astype(bf)
    own = slice(MARGIN, MARGIN + frames)
    own_near = slice(MARGIN - edge, MARGIN - edge + frames)
    rows = frames * utter_count
    scaled_own = scaled_one[own].reshape(rows, width)
    scaled_all = gathered(scaled_own, chi)

    lifted = jnp.einsum("fuc,cd->fud", scaled_one, up_weight, preferred_element_type=f32)
    linear_part = lifted[:, :, :width]
    gate_part = jax.nn.sigmoid(lifted[:, :, width:])
    glu = (linear_part * gate_part * row_mask).astype(bf).astype(f32)
    conv_out = jnp.zeros((near, utter_count, width), f32)
    for j in range(kernel_len):
        start = edge + j - half
        conv_out = conv_out + conv_kernel[j] * glu[start : start + near]
    normed_two, inverse_two = normalize(conv_out)
    pre_act = normed_two * gain_two
    gate_two = jax.nn.sigmoid(pre_act)
    activated = (pre_act * gate_two)[own_near].astype(bf).reshape(rows, width)
    activated_all = gathered(activated, chi)
    block_out = (
        hidden[own].reshape(rows, width)
        + jnp.dot(activated, down_weight, preferred_element_type=f32)
    ).astype(bf)
    block_out = block_out.reshape(frames, utter_count, width)

    pre_grad = act_grad * gate_two * (1.0 + pre_act * (1.0 - gate_two))
    gain_two_grad = jnp.sum((pre_grad * normed_two)[own_near], axis=(0, 1))
    scaled_grad = pre_grad * gain_two
    conv_grad = inverse_two * (
        scaled_grad
        - jnp.mean(scaled_grad, axis=-1, keepdims=True)
        - normed_two * jnp.mean(scaled_grad * normed_two, axis=-1, keepdims=True)
    )
    conv_grad = conv_grad.astype(bf).astype(f32)
    conv_own = conv_grad[own_near]
    small = []
    glu_grad = jnp.zeros((frames, utter_count, width), f32)
    for j in range(kernel_len):
        start = MARGIN + j - half
        small.append(jnp.sum(conv_own * glu[start : start + frames], axis=(0, 1)))
        start = MARGIN - edge + half - j
        glu_grad = glu_grad + conv_kernel[j] * conv_grad[start : start + frames]
    glu_grad = glu_grad * row_mask[own]
    gate_own = gate_part[own]
    linear_grad = glu_grad * gate_own
    gate_grad = glu_grad * linear_part[own] * gate_own * (1.0 - gate_own)
    lifted_grad = jnp.concatenate([linear_grad, gate_grad], axis=-1).astype(bf)
    lifted_grad = lifted_grad.reshape(rows, 2 * width)
    input_grad = lax.dot_general(
        lifted_grad, up_weight, (((1,), (1,)), ((), ())), preferred_element_type=f32
    )
    gain_one_grad = jnp.sum(input_grad * normed_one[own].reshape(rows, width), axis=0)

    small = small + [gain_one_grad, gain_two_grad]
    count = kernel_len + 2
    small = by_owner(jnp.stack(small).astype(bf), sizes)
    small = small.reshape(dlo * chi, -1)
    cols = by_owner(lifted_grad, sizes)
    col_count = cols.shape[2]
    spare = -small.shape[1] % col_count
    small = jnp.pad(small, ((0, 0), (0, spare))).reshape(dlo * chi, -1, col_count)
    message = jnp.concatenate([cols, small], axis=1)
    message = lax.all_to_all(message, FIRST, split_axis=0, concat_axis=0, tiled=True)
    cols = message[:, :rows].reshape(-1, col_count)
    small = jnp.sum(message[:, rows:].astype(f32), axis=0).reshape(-1)
    seconds = dhi * clo
    small_width = width // (ctx * dhi * dlo)
    small = small[: count * seconds * small_width].reshape(count, seconds, small_width)
    small = jnp.transpose(small, (1, 0, 2)).reshape(seconds, count * small_width)

    up_part = lax.dot_general(
        cols, scaled_all, (((0,), (0,)), ((), ())), preferred_element_type=f32
    ).reshape(seconds, -1, width)
    down_part = lax.dot_general(
        cot_cols.reshape(cols.shape[0], -1),
        activated_all,
        (((0,), (0,)), ((), ())),
        preferred_element_type=f32,
    ).reshape(seconds, -1, width)
    spare = -small.shape[1] % width
    small = jnp.pad(small, ((0, 0), (0, spare))).reshape(seconds, -1, width)
    up_rows, down_rows = up_part.shape[1], down_part.shape[1]
    parts = jnp.concatenate([up_part.astype(bf), down_part.astype(bf), small.astype(bf)], axis=1)
    parts = lax.all_to_all(parts, SECOND, split_axis=0, concat_axis=0, tiled=True)
    total = jnp.sum(parts.astype(f32), axis=0)
    up_grad = total[:up_rows]
    down_grad = total[up_rows : up_rows + down_rows]
    small = total[up_rows + down_rows :].reshape(-1)[: count * small_width]
    small = small.reshape(count, small_width)
    kernel_grad = jnp.transpose(small[:kernel_len])
    return (block_out, up_grad, down_grad, kernel_grad, small[kernel_len], small[kernel_len + 1])


def solution(mesh):
    dp, ctx = mesh.shape["dp"], mesh.shape["ctx"]
    fine = Mesh(mesh.devices.reshape(dp // 2, 2, ctx // 2, 2), ("dhi", "dlo", "chi", "clo"))
    dp_axes, ctx_axes = ("dhi", "dlo"), ("chi", "clo")
    every = ("dhi", "dlo", "chi", "clo")
    in_specs = (
        P(ctx_axes, dp_axes, None),
        P(ctx_axes, dp_axes, None),
        P(),
        P(),
        P(),
        P(),
        P(),
        P(),
        P(dp_axes),
        P(ctx_axes, dp_axes, None),
    )
    out_specs = (
        P(ctx_axes, dp_axes, None),
        P(every, None),
        P(every, None),
        P(every, None),
        P(every),
        P(every),
    )
    return jax.shard_map(
        on_device, mesh=fine, in_specs=in_specs, out_specs=out_specs, check_vma=False
    )
```
